32 devices in a mesh: groups: 2 (over y), ctx: 4 (over z), heads: 2 (over x), dp: 2 (over core).
Axes of the slice: x: 2, y: 2, z: 4, core: 2. Of those that a mesh axis runs over, the one named last changes fastest.
Arguments:
- tokens: bfloat16 [4, 2048, 1024], P(('groups', 'dp'), 'ctx', 'heads'), parts along dimension 0, may hold values from -12 to 12
- w_qkv: bfloat16 [3, 1024, 1024], P(None, None, 'heads'), may hold values from -0.375 to 0.375
- w_out: bfloat16 [1024, 1024], P('heads'), may hold values from -0.1875 to 0.1875
- ln_gain: float32 [1024], P('heads'), may hold values from 0.5 to 1.5
- ln_bias: float32 [1024], P('heads'), may hold values from -3 to 3
- random_blocks: int32 [4, 16, 3], P(('groups', 'dp'), 'ctx'), parts along dimension 0, may hold values from 0 to 15, as said below
- summary_pos: int32 [4, 16], P(('groups', 'dp')), parts along dimension 0, may hold values from 0 to 2047, as said below
- summary_blocks: int32 [4, 16, 8], P(('groups', 'dp')), parts along dimension 0, may hold values from 0 to 15, as said below
- pair_lengths: int32 [4, 4], P(('groups', 'dp')), parts along dimension 0, may hold values from 1 to 1536, 2048 in all within a row
Outputs:
- normed: bfloat16 [4, 2048, 1024], P(('groups', 'dp'), 'ctx', 'heads'), parts along dimension 0
The draws below stay inside these ranges and needn't reach their ends.
There are 2 independent parts, one for each index of `groups`. The reference program is written for one: setup_inputs(seed, part) draws one part's arguments, and reference() takes and returns one part's arrays. A program takes and returns all parts, laid end to end along the dimension named above; an argument that names none is the same for every part. Nothing has to cross between parts.
Inputs may be any that keep to these rules, and one draw needn't show every extreme that they name: `random_blocks`: the 4 x 3 entries of one device's range name at most 3 blocks of any one device's range of 4 blocks, repeats counted; in every draw some range is named exactly 3 times from every device's range. `summary_pos`: each range of 512 positions of a sequence holds exactly 4 of them; they are distinct and increasing. `summary_blocks`: the first entry of each list is the block holding that row's summary position; entries may repeat.
All inputs are finite; a program needn't handle non-finite values.
Results may differ from the reference program's by a relative error of at most 0.012.
The reference program's roundings to bfloat16 on the way count: a program that leaves them out, or rounds other values in their place, can miss the bound.
Values may be sent and summed in bfloat16 or wider, within the bound.
No kernel may reach another device: no remote copies, remote signals or barrier semaphores. Data moves between devices by JAX's collectives and lax.ppermute only.
A program may use at most 64 MiB of HBM per device.

```python
import math
import jax
import jax.numpy as jnp
import numpy as np
from jax import lax

D = 1024
HEADS = 16
HEAD = 64
BLOCK = 128
RAND = 3
LISTED = 8
PAIRS = 4
TOK_DEV = 512
SUMM_DEV = 4
BLOCKS_DEV = 4
SEQ_LEN = 2048
NBLOCKS = 16
SEQS = 2
CAP = 3
SUMMARIES = 16
N_CTX = 4
N_HEADS = 2


def summary_positions(key):
    base = jax.random.fold_in(key, 7001)

    def pick_one(flat_index):
        chosen = jax.random.permutation(jax.random.fold_in(base, flat_index), TOK_DEV)[:SUMM_DEV]
        return jnp.sort(chosen.astype(jnp.int32))
    picked = jax.vmap(pick_one)(jnp.arange(SEQS * N_CTX)).reshape(SEQS, N_CTX, SUMM_DEV)
    offsets = (jnp.arange(N_CTX, dtype=jnp.int32) * TOK_DEV)[None, :, None]
    return (picked + offsets).reshape(SEQS, SUMMARIES).astype(jnp.int32)


def draw_summary_pos(key, part):
    return summary_positions(key)


def draw_summary_blocks(key, part):
    positions = summary_positions(key)
    own_block = positions // BLOCK
    others = jax.random.randint(jax.random.fold_in(key, 7002), (SEQS, SUMMARIES, LISTED - 1), 0, NBLOCKS)
    return jnp.concatenate([own_block[:, :, None], others.astype(jnp.int32)], axis=2).astype(jnp.int32)


def draw_random_blocks(key, part):
    pick_count = BLOCKS_DEV * RAND
    base = jax.random.fold_in(key, 7003)
    hottest = jax.random.randint(jax.random.fold_in(base, 1), (SEQS,), 0, N_CTX).astype(jnp.int32)

    def one_range(seq_index, ctx_index):
        range_key = jax.random.fold_in(jax.random.fold_in(base, seq_index + 2), ctx_index)
        others = jax.random.permutation(jax.random.fold_in(range_key, 1), CAP * (N_CTX - 1))[:pick_count - CAP] // CAP
        others = others.astype(jnp.int32)
        others = others + (others >= hottest[seq_index]).astype(jnp.int32)
        owners = jnp.concatenate([jnp.zeros((CAP,), jnp.int32) + hottest[seq_index], others])
        owners = jax.random.permutation(jax.random.fold_in(range_key, 2), owners)
        within = jax.random.randint(jax.random.fold_in(range_key, 3), (pick_count,), 0, BLOCKS_DEV).astype(jnp.int32)
        return (owners * BLOCKS_DEV + within).reshape(BLOCKS_DEV, RAND)
    grid = jax.vmap(lambda seq_index: jax.vmap(lambda ctx_index: one_range(seq_index, ctx_index))(jnp.arange(N_CTX)))(jnp.arange(SEQS))
    return grid.reshape(SEQS, NBLOCKS, RAND).astype(jnp.int32)


def draw_tokens(key, part):
    base = jax.random.fold_in(key, 7004)
    values = jnp.clip(jax.random.normal(jax.random.fold_in(base, 7), (SEQS, SEQ_LEN, D), jnp.float32), -6.0, 6.0)
    return values.astype(jnp.bfloat16)


def block_scale(stream_key, shape, shards, smallest, largest):
    loudness = 1.0
    for dim, shards_of in shards:
        draws = jax.random.uniform(jax.random.fold_in(jax.random.fold_in(stream_key, 6), dim), (shards_of,), jnp.float32, smallest / len(shards), largest / len(shards))
        loudness = loudness * jnp.repeat(jnp.exp(draws), shape[dim] // shards_of).reshape((-1,) + (1,) * (len(shape) - 1 - dim))
    return loudness


def split_up(amount, total, bound, slope):
    portions = [(1 << 20) // math.isqrt(standing ** slope) + 1 for standing in range(2, amount + 1)]
    rest, counts = total - bound - (amount - 1), [1] * (amount - 1)
    while rest > 0:
        free = [i for i in range(amount - 1) if counts[i] < bound]
        mass, budget = sum([portions[i] for i in free]), rest
        for i in free:
            addition = min(bound - counts[i], max(1, budget * portions[i] // mass), rest)
            counts[i] = counts[i] + addition
            rest = rest - addition
    return np.array([bound] + counts)


def ragged(own_key, count, total, limit, lean):
    if count == 2:
        one = jax.random.randint(own_key, (), max(1, total - limit), min(limit, total - 1) + 1)
        return jnp.stack([one, total - one])
    tallies = jnp.asarray(split_up(count, total, limit, lean), jnp.int32)
    couples = (count - 1) // 2
    donor, sink = tallies[1:1 + 2 * couples:2], tallies[2:2 + 2 * couples:2]
    margin = jnp.minimum(donor - 1, limit - sink)
    passed = jax.random.randint(jax.random.fold_in(own_key, 1), (couples,), 0, 1 << 20) % (margin + 1)
    tallies = tallies.at[1:1 + 2 * couples:2].set(donor - passed).at[2:2 + 2 * couples:2].set(sink + passed)
    return tallies[jax.random.permutation(jax.random.fold_in(own_key, 2), count)]


def normal_values(stream_key, dims, spread, limit, cuts=(), held_as=jnp.bfloat16):
    level = block_scale(stream_key, dims, cuts, -0.22, 0.18) if cuts else 1.0
    entries = jax.random.normal(stream_key, dims, jnp.float32) * spread * level
    return jnp.minimum(jnp.maximum(entries, -limit), limit).astype(held_as)


def setup_inputs(seed: int = 0, part: int = 0) -> dict:
    seeds = jax.random.split(jax.random.key(seed), 10)
    own_keys = jax.random.split(jax.random.fold_in(seeds[9], part), 10)
    tokens = draw_tokens(jax.random.fold_in(jax.random.fold_in(seeds[9], part), 71), part)
    w_qkv = normal_values(seeds[1], (3, D, D), (D // 4) ** -0.5, 0.375, ((2, 2),))
    w_out = normal_values(seeds[2], (D, D), D ** -0.5, 0.1875, ((0, 2),))
    ln_gain = jnp.clip(1.0 + 0.1 * jax.random.normal(seeds[3], (D,), jnp.float32), 0.5, 1.5)
    ln_bias = normal_values(seeds[4], (D,), 0.5, 3.0, ((0, 2),), jnp.float32)
    random_blocks = draw_random_blocks(jax.random.fold_in(jax.random.fold_in(seeds[9], part), 71), part)
    summary_pos = draw_summary_pos(jax.random.fold_in(jax.random.fold_in(seeds[9], part), 71), part)
    summary_blocks = draw_summary_blocks(jax.random.fold_in(jax.random.fold_in(seeds[9], part), 71), part)
    pair_lengths = jax.vmap(lambda own: ragged(own, PAIRS, SEQ_LEN, 3 * SEQ_LEN // 4, 0))(jax.random.split(own_keys[8], SEQS)).reshape((SEQS, PAIRS)).astype(jnp.int32)
    return {"tokens": tokens, "w_qkv": w_qkv, "w_out": w_out, "ln_gain": ln_gain, "ln_bias": ln_bias, "random_blocks": random_blocks, "summary_pos": summary_pos, "summary_blocks": summary_blocks, "pair_lengths": pair_lengths}


MASKED = -1e+30

def segment_ids(positions, bounds):
    return lax.optimization_barrier(jnp.sum((positions[..., None] >= bounds).astype(jnp.int32), axis=-1))

def attend(queries, keys, values, allowed, head_count):
    group_count, query_len, all_width = queries.shape
    key_len = keys.shape[1]
    query_heads = queries.astype(jnp.float32).reshape(group_count, query_len, head_count, HEAD)
    key_heads = keys.astype(jnp.float32).reshape(group_count, key_len, head_count, HEAD)
    value_heads = values.astype(jnp.float32).reshape(group_count, key_len, head_count, HEAD)
    scores = jnp.einsum('gqhe,gkhe->ghqk', query_heads, key_heads) * HEAD ** (-0.5)
    scores = jnp.where(allowed[:, None], scores, MASKED)
    maxima = lax.optimization_barrier(jnp.max(scores, axis=-1, keepdims=True))
    weights = jnp.where(allowed[:, None], jnp.exp(scores - maxima), 0.0)
    totals = lax.optimization_barrier(jnp.sum(weights, axis=-1))
    rounded = lax.optimization_barrier(weights.astype(jnp.bfloat16)).astype(jnp.float32)
    mixture = jnp.einsum('ghqk,gkhe->gqhe', rounded, value_heads)
    mixture = mixture / jnp.transpose(totals, (0, 2, 1))[..., None]
    return mixture.reshape(group_count, query_len, all_width).astype(jnp.bfloat16)

def one_sequence(seq_tokens, w_qkv, w_out, ln_gain, ln_bias, random_rows, summary_rows, summary_lists, pair_row):
    seq_len = seq_tokens.shape[0]
    block_count = seq_len // BLOCK
    queries = jnp.dot(seq_tokens, w_qkv[0], preferred_element_type=jnp.float32).astype(jnp.bfloat16)
    keys = jnp.dot(seq_tokens, w_qkv[1], preferred_element_type=jnp.float32).astype(jnp.bfloat16)
    values = jnp.dot(seq_tokens, w_qkv[2], preferred_element_type=jnp.float32).astype(jnp.bfloat16)
    bounds = jnp.cumsum(pair_row)
    positions = jnp.arange(seq_len, dtype=jnp.int32)
    segments = segment_ids(positions, bounds)
    padding = jnp.zeros((BLOCK, keys.shape[1]), jnp.bfloat16)
    keys_pad = jnp.concatenate([padding, keys, padding], axis=0)
    values_pad = jnp.concatenate([padding, values, padding], axis=0)
    rim_pos = jnp.arange(seq_len + 2 * BLOCK, dtype=jnp.int32) - BLOCK
    rim_ok = (rim_pos >= 0) & (rim_pos < seq_len)
    rim_seg = segment_ids(rim_pos, bounds)
    offsets = jnp.arange(BLOCK, dtype=jnp.int32)

    def per_block(block_index):
        first_row = (block_index * BLOCK).astype(jnp.int32)
        query_block = lax.dynamic_slice_in_dim(queries, first_row, BLOCK, 0)
        near_keys = lax.dynamic_slice_in_dim(keys_pad, first_row, 3 * BLOCK, 0)
        near_values = lax.dynamic_slice_in_dim(values_pad, first_row, 3 * BLOCK, 0)
        far_pos = (random_rows[block_index][:, None] * BLOCK + offsets[None, :]).reshape(-1).astype(jnp.int32)
        all_keys = jnp.concatenate([near_keys, jnp.take(keys, far_pos, axis=0)], axis=0)
        all_values = jnp.concatenate([near_values, jnp.take(values, far_pos, axis=0)], axis=0)
        key_seg = jnp.concatenate([lax.dynamic_slice_in_dim(rim_seg, first_row, 3 * BLOCK, 0), jnp.take(segments, far_pos)])
        key_ok = jnp.concatenate([lax.dynamic_slice_in_dim(rim_ok, first_row, 3 * BLOCK, 0), jnp.ones((far_pos.shape[0],), jnp.bool_)])
        query_seg = lax.dynamic_slice_in_dim(segments, first_row, BLOCK, 0)
        allowed = key_ok[None, :] & (key_seg[None, :] == query_seg[:, None])
        return attend(query_block[None], all_keys[None], all_values[None], allowed[None], HEADS)[0]
    blocks_out = lax.map(per_block, jnp.arange(block_count, dtype=jnp.int32)).reshape(seq_len, -1)
    list_len = summary_lists.shape[1]
    slot_order = jnp.arange(list_len, dtype=jnp.int32)

    def per_summary(summary_index):
        position = summary_rows[summary_index].astype(jnp.int32)
        listing = summary_lists[summary_index]
        repeated = jnp.any((listing[:, None] == listing[None, :]) & (slot_order[None, :] < slot_order[:, None]), axis=1)
        key_pos = (listing[:, None] * BLOCK + offsets[None, :]).reshape(-1).astype(jnp.int32)
        fresh = jnp.repeat(jnp.logical_not(repeated), BLOCK)
        allowed = fresh & (jnp.take(segments, key_pos) == segments[position])
        query_row = lax.dynamic_slice_in_dim(queries, position, 1, 0)
        listed_keys = jnp.take(keys, key_pos, axis=0)
        listed_values = jnp.take(values, key_pos, axis=0)
        return attend(query_row[None], listed_keys[None], listed_values[None], allowed[None, None], HEADS)[0, 0]
    summary_out = lax.map(per_summary, jnp.arange(summary_rows.shape[0], dtype=jnp.int32))
    attention = blocks_out.at[summary_rows].set(summary_out)
    part_cols = attention.shape[1] // N_HEADS
    summed = jnp.zeros((seq_len, w_out.shape[1]), jnp.float32)
    for group_index in range(N_HEADS):
        low_col = group_index * part_cols
        term = jnp.dot(attention[:, low_col:low_col + part_cols], w_out[low_col:low_col + part_cols], preferred_element_type=jnp.float32)
        summed = summed + lax.optimization_barrier(term.astype(jnp.bfloat16)).astype(jnp.float32)
    hidden = seq_tokens.astype(jnp.float32) + summed
    row_mean = lax.optimization_barrier(jnp.mean(hidden, axis=1, keepdims=True))
    row_var = lax.optimization_barrier(jnp.mean(hidden * hidden, axis=1, keepdims=True)) - row_mean * row_mean
    normed = (hidden - row_mean) * lax.rsqrt(row_var + 1e-05) * ln_gain + ln_bias
    return normed.astype(jnp.bfloat16)

def reference(tokens, w_qkv, w_out, ln_gain, ln_bias, random_blocks, summary_pos, summary_blocks, pair_lengths):
    results = []
    for seq_index in range(tokens.shape[0]):
        results.append(one_sequence(tokens[seq_index], w_qkv, w_out, ln_gain, ln_bias, random_blocks[seq_index], summary_pos[seq_index], summary_blocks[seq_index], pair_lengths[seq_index]))
    return jnp.stack(results)
```

```python
import functools
import jax
import jax.numpy as jnp
from jax import lax
from jax.experimental import pallas as pl
from jax.experimental.pallas import tpu as pltpu
from jax.sharding import PartitionSpec as P

HEAD = 64
BLOCK = 128


MASKED = -1e30


def extended(x, sides, width):
    for axis, dim in sides:
        size, length = (lax.axis_size(axis), x.shape[dim])
        up = [(i, (i + 1) % size) for i in range(size - 1)]
        down = [(j, i) for i, j in up]
        last = lax.slice_in_dim(x, length - width, length, axis=dim)
        first = lax.slice_in_dim(x, 0, width, axis=dim)
        before = lax.ppermute(last, axis, up)
        after = lax.ppermute(first, axis, down)
        x = jnp.concatenate([before, x, after], axis=dim)
    return x


def segment_ids(positions, bounds):
    return jnp.sum((positions[..., None] >= bounds).astype(jnp.int32), axis=-1)


def attend(queries, keys, values, allowed, head_count):
    group_count, query_len, all_width = queries.shape
    key_len = keys.shape[1]
    query_heads = queries.reshape(group_count, query_len, head_count, HEAD)
    key_heads = keys.reshape(group_count, key_len, head_count, HEAD)
    value_heads = values.reshape(group_count, key_len, head_count, HEAD)
    scores = jnp.einsum(
        "gqhe,gkhe->ghqk", query_heads, key_heads, preferred_element_type=jnp.float32
    ) * HEAD ** (-0.5)
    scores = jnp.where(allowed[:, None], scores, MASKED)
    maxima = jnp.max(scores, axis=-1, keepdims=True)
    weights = jnp.where(allowed[:, None], jnp.exp(scores - maxima), 0.0)
    totals = jnp.sum(weights, axis=-1)
    mixture = jnp.einsum(
        "ghqk,gkhe->gqhe",
        weights.astype(jnp.bfloat16),
        value_heads,
        preferred_element_type=jnp.float32,
    )
    mixture = mixture / jnp.transpose(totals, (0, 2, 1))[..., None]
    return mixture.reshape(group_count, query_len, all_width).astype(jnp.bfloat16)


def three_views(window_span, group_size, axis_pos):
    views = []
    for shift_index in range(3):
        piece = lax.slice_in_dim(
            window_span,
            shift_index * BLOCK,
            shift_index * BLOCK + group_size * BLOCK,
            axis=axis_pos,
        )
        new_shape = (
            window_span.shape[:axis_pos] + (group_size, BLOCK) + window_span.shape[axis_pos + 1 :]
        )
        views.append(piece.reshape(new_shape))
    return jnp.concatenate(views, axis=axis_pos + 1)


def requested(
    tokens, w_qkv, w_out, ln_gain, ln_bias, random_blocks, summary_pos, summary_blocks, pair_lengths
):
    tok_rows = tokens.shape[1]
    head_cols = tokens.shape[2]
    heads_here = head_cols // HEAD
    full_width = w_out.shape[1]
    ctx_count = lax.axis_size("ctx")
    ctx_index = lax.axis_index("ctx")
    block_count = tok_rows // BLOCK
    seq_total = tok_rows * ctx_count
    bounds = jnp.cumsum(pair_lengths[0])
    own_tokens = tokens[0]
    projected = jnp.einsum(
        "nc,kcd->knd",
        lax.all_gather(own_tokens, "heads", axis=1, tiled=True),
        w_qkv,
        preferred_element_type=jnp.float32,
    ).astype(jnp.bfloat16)
    queries = projected[0]
    own_kv = projected[1:3]
    rim_kv = extended(own_kv, (("ctx", 1),), BLOCK)
    query_pos = ctx_index * tok_rows + jnp.arange(tok_rows, dtype=jnp.int32)
    own_seg = segment_ids(query_pos, bounds)
    rim_pos = ctx_index * tok_rows - BLOCK + jnp.arange(tok_rows + 2 * BLOCK, dtype=jnp.int32)
    rim_ok = (rim_pos >= 0) & (rim_pos < seq_total)
    rim_seg = segment_ids(rim_pos, bounds)
    rand_count = random_blocks.shape[2]
    picked = random_blocks[0].reshape(-1)
    pick_count = picked.shape[0]
    capacity = max(2, -(-pick_count // ctx_count))
    owners = picked // block_count
    within = picked % block_count
    slot_order = jnp.arange(pick_count, dtype=jnp.int32)
    earlier = (owners[:, None] == owners[None, :]) & (slot_order[None, :] < slot_order[:, None])
    pick_rank = jnp.sum(earlier.astype(jnp.int32), axis=1)
    pick_slot = owners * capacity + pick_rank
    slot_table = (
        pick_slot[:, None] == jnp.arange(ctx_count * capacity, dtype=jnp.int32)[None, :]
    ).astype(jnp.int32)
    requests = jnp.sum(slot_table * within[:, None], axis=0).reshape(ctx_count, capacity)
    own_blocks = own_kv.reshape(2, block_count, BLOCK, head_cols).transpose(1, 0, 2, 3)
    reply = jnp.take(
        own_blocks, lax.all_to_all(requests, "ctx", split_axis=0, concat_axis=0, tiled=True), axis=0
    )
    fetched = lax.all_to_all(reply, "ctx", split_axis=0, concat_axis=0, tiled=True)
    flat_blocks = fetched.reshape(ctx_count * capacity, 2, BLOCK, head_cols)
    far_kv = jnp.take(flat_blocks, pick_slot, axis=0).reshape(
        block_count, rand_count, 2, BLOCK, head_cols
    )
    far_kv = far_kv.transpose(2, 0, 1, 3, 4).reshape(2, block_count, rand_count * BLOCK, head_cols)
    far_pos = (
        picked.reshape(block_count, rand_count)[:, :, None] * BLOCK
        + jnp.arange(BLOCK, dtype=jnp.int32)
    ).reshape(block_count, rand_count * BLOCK)
    far_seg = segment_ids(far_pos, bounds)
    group_size = min(4, block_count)
    group_steps = block_count // group_size

    def window_step(unused, step_index):
        near_kv = three_views(rim_kv, group_size, 1)
        near_ok = three_views(rim_ok, group_size, 0)
        near_seg = three_views(rim_seg, group_size, 0)
        key_set = jnp.concatenate([near_kv, far_kv], axis=2)
        key_seg = jnp.concatenate([near_seg, far_seg], axis=1)
        key_ok = jnp.concatenate([near_ok, jnp.ones(far_seg.shape, jnp.bool_)], axis=1)
        query_seg = own_seg.reshape(group_size, BLOCK)
        allowed = key_ok[:, None, :] & (key_seg[:, None, :] == query_seg[:, :, None])
        query_group = queries.reshape(group_size, BLOCK, head_cols)
        return (unused, attend(query_group, key_set[0], key_set[1], allowed, heads_here))

    _, window_out = lax.scan(window_step, 0, jnp.arange(group_steps, dtype=jnp.int32))
    attention = window_out.reshape(tok_rows, head_cols)
    summary_rows = summary_pos[0]
    summary_lists = summary_blocks[0]
    summaries = summary_rows.shape[0]
    per_device = summaries // ctx_count
    mine = (
        lax.dynamic_slice_in_dim(summary_rows, ctx_index * per_device, per_device, 0)
        - ctx_index * tok_rows
    )
    summary_query = jnp.take(queries, mine, axis=0)
    all_queries = lax.all_gather(summary_query, "ctx", axis=0, tiled=True)
    summary_seg = segment_ids(summary_rows, bounds)
    key_block = ctx_index * block_count + jnp.arange(block_count, dtype=jnp.int32)
    listed = jnp.any(summary_lists[:, :, None] == key_block[None, None, :], axis=1)
    key_heads = own_kv[0].reshape(tok_rows, heads_here, HEAD)
    value_heads = own_kv[1].reshape(tok_rows, heads_here, HEAD)
    summary_group = min(128, summaries)
    group_total = summaries // summary_group

    def group_scores():
        query_part = all_queries.reshape(summary_group, heads_here, HEAD)
        allowed = jnp.broadcast_to(listed[:, :, None], (summary_group, block_count, BLOCK)).reshape(
            summary_group, tok_rows
        )
        allowed = allowed & (own_seg[None, :] == summary_seg[:, None])
        scores = jnp.einsum(
            "qhe,khe->hqk", query_part, key_heads, preferred_element_type=jnp.float32
        ) * HEAD ** (-0.5)
        return (jnp.where(allowed[None], scores, MASKED), allowed)

    def weigh(scores, allowed, maxima):
        weights = jnp.where(allowed[None], jnp.exp(scores - maxima[:, :, None]), 0.0)
        totals = jnp.sum(weights, axis=-1)
        mixture = jnp.einsum(
            "hqk,khe->qhe",
            weights.astype(jnp.bfloat16),
            value_heads,
            preferred_element_type=jnp.float32,
        )
        return (totals.T, mixture.reshape(summary_group, head_cols))

    def max_step(unused, group_index):
        scores, allowed = group_scores()
        return (unused, jnp.max(scores, axis=-1).T)

    _, maxima_all = lax.scan(max_step, 0, jnp.arange(group_total, dtype=jnp.int32))
    maxima_all = lax.pmax(maxima_all.reshape(summaries, heads_here), "ctx")

    def sum_step(unused, group_index):
        scores, allowed = group_scores()
        maxima = maxima_all.T
        return (unused, weigh(scores, allowed, maxima))

    _, (totals_all, mixture_all) = lax.scan(sum_step, 0, jnp.arange(group_total, dtype=jnp.int32))
    totals_all = totals_all.reshape(summaries, heads_here)
    mixture_all = mixture_all.reshape(summaries, head_cols)
    totals_all, mixture_all = (
        lax.psum(totals_all.astype(jnp.bfloat16), "ctx").astype(jnp.float32),
        lax.psum(mixture_all.astype(jnp.bfloat16), "ctx").astype(jnp.float32),
    )
    own_totals = lax.dynamic_slice_in_dim(totals_all, ctx_index * per_device, per_device, 0)
    own_mixture = lax.dynamic_slice_in_dim(mixture_all, ctx_index * per_device, per_device, 0)
    summary_out = (own_mixture / jnp.repeat(own_totals, HEAD, axis=1)).astype(jnp.bfloat16)
    attention = attention.at[mine].set(summary_out)
    partial_value = jnp.dot(attention, w_out, preferred_element_type=jnp.float32)
    summed = lax.psum_scatter(
        partial_value.astype(jnp.bfloat16), "heads", scatter_dimension=1, tiled=True
    ).astype(jnp.float32)
    hidden = own_tokens.astype(jnp.float32) + summed
    row_sums = lax.psum((jnp.sum(hidden, axis=1), jnp.sum(hidden * hidden, axis=1)), "heads")
    row_mean = row_sums[0] / full_width
    row_var = row_sums[1] / full_width - row_mean * row_mean
    normed = (hidden - row_mean[:, None]) * lax.rsqrt(row_var + 1e-05)[:, None] * ln_gain + ln_bias
    return normed.astype(jnp.bfloat16)[None]


LANES = 128
PAIR = LANES // HEAD
VMEM_LIMIT = 48 * 1024 * 1024
F32 = jnp.float32
BF16 = jnp.bfloat16
NT = (((1,), (1,)), ((), ()))


def whole_block(shape):
    return pl.BlockSpec(shape, lambda *_: (0,) * len(shape))


def params(*semantics):
    return pltpu.CompilerParams(
        dimension_semantics=semantics or None, vmem_limit_bytes=VMEM_LIMIT
    )


def project_kernel(side_ref, here_ref, there_ref, w_ref, *refs):
    out_ref = refs[-1]
    half = here_ref.shape[1]
    low = pl.multiple_of(side_ref[0] * half, half)
    high = pl.multiple_of((1 - side_ref[0]) * half, half)
    product = jnp.dot(here_ref[...], w_ref[0, pl.ds(low, half), :], preferred_element_type=F32)
    product += jnp.dot(there_ref[...], w_ref[0, pl.ds(high, half), :], preferred_element_type=F32)
    out_ref[0] = product.astype(BF16)


def project(side, here, there, w_qkv, first, total_rows, row_block, held):
    rows, half = here.shape
    cols = w_qkv.shape[2]
    in_specs = [
        pl.BlockSpec(memory_space=pltpu.SMEM),
        whole_block((rows, half)),
        whole_block((rows, half)),
        pl.BlockSpec((1, 2 * half, cols), lambda j: (j + first, 0, 0)),
    ]
    args = [side, here, there, w_qkv]
    aliases = {}
    if held is not None:
        in_specs.append(pl.BlockSpec(memory_space=pl.ANY))
        args.append(held)
        aliases = {4: 0}
    count = 3 - first
    return pl.pallas_call(
        project_kernel,
        grid=(count,),
        in_specs=in_specs,
        out_specs=pl.BlockSpec((1, rows, cols), lambda j: (j + first, row_block, 0)),
        out_shape=jax.ShapeDtypeStruct((3, total_rows, cols), BF16),
        input_output_aliases=aliases,
        compiler_params=params("arbitrary"),
        cost_estimate=pl.CostEstimate(
            flops=4 * rows * half * cols * count,
            bytes_accessed=2 * count * (2 * half * cols + rows * cols) + 4 * rows * half,
            transcendentals=0,
        ),
        name="project",
    )(*args)


def segments_of(position, bounds_ref, pair_count):
    segment = jnp.zeros(position.shape, jnp.int32)
    for pair in range(pair_count):
        segment += (position >= bounds_ref[pair]).astype(jnp.int32)
    return segment


def item_bias(query_seg, key_pos, bounds_ref, pair_count):
    lane = lax.broadcasted_iota(jnp.int32, (1, BLOCK), 1)
    key_seg = segments_of(key_pos + lane, bounds_ref, pair_count)
    key_seg = jnp.where(key_pos >= 0, key_seg, -1)
    return jnp.where(query_seg == key_seg, 0.0, MASKED)


def split_heads(pair_queries):
    lane = lax.broadcasted_iota(jnp.int32, pair_queries.shape, 1)
    scaled = pair_queries.astype(F32) * HEAD ** (-0.5)
    low = jnp.where(lane < HEAD, scaled, 0.0)
    high = jnp.where(lane >= HEAD, scaled, 0.0)
    return jnp.concatenate([low, high], axis=0).astype(BF16)


def join_heads(stacked):
    rows = stacked.shape[0] // PAIR
    lane = lax.broadcasted_iota(jnp.int32, (rows, LANES), 1)
    return jnp.where(lane < HEAD, stacked[:rows], stacked[rows:])


def spread_pair(low, high):
    lane = lax.broadcasted_iota(jnp.int32, (low.shape[0], LANES), 1)
    return jnp.where(lane < HEAD, low, high)


def summary_queries(rows_ref, q_ref, head_count):
    tok_rows, cols = q_ref.shape
    row = lax.broadcasted_iota(jnp.int32, (8, tok_rows), 0)
    col = lax.broadcasted_iota(jnp.int32, (8, tok_rows), 1)
    chosen = jnp.zeros((8, tok_rows), F32)
    for u in range(rows_ref.shape[0]):
        chosen = jnp.where((row == u) & (col == rows_ref[u]), 1.0, chosen)
    picked = jnp.dot(chosen.astype(BF16), q_ref[...], preferred_element_type=F32)
    picked = picked * HEAD ** (-0.5)
    lane = lax.broadcasted_iota(jnp.int32, (8, cols), 1)
    parts = [
        jnp.where((lane >= h * HEAD) & (lane < (h + 1) * HEAD), picked, 0.0)
        for h in range(head_count)
    ]
    return jnp.concatenate(parts, axis=0).astype(BF16)


def early_kernel(
    off_ref, pos_ref, bounds_ref, mine_ref, base_ref,
    q_ref, q_all_ref, k_ref, v_ref, sbias_ref,
    acc_ref, ml_ref, sacc_ref, sml_ref,
    bias_ref, *, items, pair_count, head_count,
):
    step = pl.program_id(0)
    row = lax.broadcasted_iota(jnp.int32, (BLOCK, 1), 0)
    query_seg = segments_of(base_ref[0] + step * BLOCK + row, bounds_ref, pair_count)
    offsets = []
    for item in range(items):
        at = step * items + item
        offsets.append(pl.multiple_of(off_ref[at], BLOCK))
        bias = item_bias(query_seg, pos_ref[at], bounds_ref, pair_count)
        bias_ref[:BLOCK, item * BLOCK : (item + 1) * BLOCK] = bias
        bias_ref[BLOCK:, item * BLOCK : (item + 1) * BLOCK] = bias
    lane = lax.broadcasted_iota(jnp.int32, (BLOCK, LANES), 1)
    state = jnp.zeros((BLOCK, LANES), F32)
    for pair in range(head_count // PAIR):
        cols = slice(pair * LANES, (pair + 1) * LANES)
        stacked = split_heads(q_ref[0, :, cols])
        scores = [
            lax.dot_general(
                stacked, k_ref[0, pl.ds(offsets[i], BLOCK), cols], NT, preferred_element_type=F32
            )
            + bias_ref[:, i * BLOCK : (i + 1) * BLOCK]
            for i in range(items)
        ]
        top = functools.reduce(jnp.maximum, scores)
        top = jnp.max(top, axis=1, keepdims=True)
        weights = [jnp.exp(s - top) for s in scores]
        total = jnp.sum(functools.reduce(jnp.add, weights), axis=1, keepdims=True)
        mixture = functools.reduce(
            jnp.add,
            [
                jnp.dot(
                    weights[i].astype(BF16),
                    v_ref[0, pl.ds(offsets[i], BLOCK), cols],
                    preferred_element_type=F32,
                )
                for i in range(items)
            ],
        )
        acc_ref[:, cols] = join_heads(mixture)
        for j in range(PAIR):
            h = pair * PAIR + j
            rows = slice(j * BLOCK, (j + 1) * BLOCK)
            state = jnp.where(lane == h, top[rows], state)
            state = jnp.where(lane == head_count + h, total[rows], state)
    ml_ref[...] = state

    @pl.when(step == 0)
    def _():
        queries = summary_queries(mine_ref, q_all_ref.at[0], head_count)
        keys = k_ref.shape[1]
        scores = lax.dot_general(queries, k_ref[0], NT, preferred_element_type=F32)
        scores = scores + jnp.concatenate([sbias_ref[:, :keys]] * head_count, axis=0)
        top = jnp.max(scores, axis=1, keepdims=True)
        weights = jnp.exp(scores - top)
        total = jnp.sum(weights, axis=1, keepdims=True)
        sacc_ref[...] = jnp.dot(weights.astype(BF16), v_ref[0], preferred_element_type=F32)
        slane = lax.broadcasted_iota(jnp.int32, sml_ref.shape, 1)
        sml_ref[...] = jnp.where(slane == 0, top, total)


def late_kernel(
    valid_ref, block_ref, off_ref, pos_ref, bounds_ref, mine_ref, base_ref, side_ref,
    q_ref, q_all_ref, k_ref, v_ref, sbias_ref, acc_ref, ml_ref, sacc_ref, sml_ref, w_ref,
    own_ref, other_ref,
    mix_ref, state_ref, sum_ref, *, items, pair_count, head_count, early_keys,
):
    step = pl.program_id(0)
    cols_all = head_count * HEAD
    lane = lax.broadcasted_iota(jnp.int32, (BLOCK, LANES), 1)

    @pl.when(step == 0)
    def _():
        queries = summary_queries(mine_ref, q_all_ref.at[0], head_count)
        scores = lax.dot_general(queries, k_ref[0], NT, preferred_element_type=F32)
        scores = scores + jnp.concatenate([sbias_ref[:, early_keys:]] * head_count, axis=0)
        before = sml_ref[:, 0:1]
        top = jnp.maximum(before, jnp.max(scores, axis=1, keepdims=True))
        weights = jnp.exp(scores - top)
        fade = jnp.exp(before - top)
        total = sml_ref[:, 1:2] * fade + jnp.sum(weights, axis=1, keepdims=True)
        mixture = sacc_ref[...] * fade + jnp.dot(
            weights.astype(BF16), v_ref[0], preferred_element_type=F32
        )
        mixture = mixture / total
        slane = lax.broadcasted_iota(jnp.int32, (8, cols_all), 1)
        joined = jnp.zeros((8, cols_all), F32)
        for h in range(head_count):
            joined = jnp.where(
                (slane >= h * HEAD) & (slane < (h + 1) * HEAD), mixture[h * 8 : (h + 1) * 8], joined
            )
        sum_ref[...] = joined

    mix_ref[...] = acc_ref[...]
    state_ref[...] = ml_ref[...]
    row = lax.broadcasted_iota(jnp.int32, (BLOCK, 1), 0)
    query_seg = segments_of(base_ref[0] + step * BLOCK + row, bounds_ref, pair_count)
    for item in range(items):

        @pl.when((valid_ref[item] == 1) & (block_ref[item] == step))
        def _():
            offset = pl.multiple_of(off_ref[item], BLOCK)
            bias = item_bias(query_seg, pos_ref[item], bounds_ref, pair_count)
            bias = jnp.concatenate([bias] * PAIR, axis=0)
            state = state_ref[...]
            fresh = state
            for pair in range(head_count // PAIR):
                cols = slice(pair * LANES, (pair + 1) * LANES)
                heads = [pair * PAIR + j for j in range(PAIR)]
                scores = (
                    lax.dot_general(
                        split_heads(q_ref[0, :, cols]),
                        k_ref[0, pl.ds(offset, BLOCK), cols],
                        NT,
                        preferred_element_type=F32,
                    )
                    + bias
                )
                before = jnp.concatenate([state[:, h : h + 1] for h in heads], axis=0)
                count = jnp.concatenate(
                    [state[:, head_count + h : head_count + h + 1] for h in heads], axis=0
                )
                top = jnp.maximum(before, jnp.max(scores, axis=1, keepdims=True))
                weights = jnp.exp(scores - top)
                fade = jnp.exp(before - top)
                total = count * fade + jnp.sum(weights, axis=1, keepdims=True)
                mixture = jnp.dot(
                    weights.astype(BF16),
                    v_ref[0, pl.ds(offset, BLOCK), cols],
                    preferred_element_type=F32,
                )
                mix_ref[:, cols] = mix_ref[:, cols] * spread_pair(
                    fade[:BLOCK], fade[BLOCK:]
                ) + join_heads(mixture)
                for j, h in enumerate(heads):
                    rows = slice(j * BLOCK, (j + 1) * BLOCK)
                    fresh = jnp.where(lane == h, top[rows], fresh)
                    fresh = jnp.where(lane == head_count + h, total[rows], fresh)
            state_ref[...] = fresh

    state = state_ref[...]
    for pair in range(head_count // PAIR):
        cols = slice(pair * LANES, (pair + 1) * LANES)
        h = head_count + pair * PAIR
        totals = spread_pair(state[:, h : h + 1], state[:, h + 1 : h + 2])
        mix_ref[:, cols] = mix_ref[:, cols] / totals
    attention = mix_ref[...]
    here = step * BLOCK + row
    for u in range(mine_ref.shape[0]):
        attention = jnp.where(here == mine_ref[u], sum_ref[u : u + 1, :], attention)
    attention = attention.astype(BF16)
    half = w_ref.shape[1] // 2
    low = pl.multiple_of(side_ref[0] * half, half)
    high = pl.multiple_of((1 - side_ref[0]) * half, half)
    own_ref[...] = jnp.dot(
        attention, w_ref[:, pl.ds(low, half)], preferred_element_type=F32
    ).astype(BF16)
    other_ref[...] = jnp.dot(
        attention, w_ref[:, pl.ds(high, half)], preferred_element_type=F32
    ).astype(BF16)


def gathered(
    tokens, w_qkv, w_out, ln_gain, ln_bias, random_blocks, summary_pos, summary_blocks, pair_lengths
):
    tok_rows, half = tokens.shape[1:]
    cols = w_qkv.shape[2]
    head_count = cols // HEAD
    full_width = w_out.shape[1]
    ctx_count = lax.axis_size("ctx")
    ctx_index = lax.axis_index("ctx")
    side = lax.axis_index("heads").astype(jnp.int32).reshape(1)
    block_count = tok_rows // BLOCK
    total_blocks = block_count * ctx_count
    pair_count = pair_lengths.shape[1]
    own_tokens = tokens[0]
    swap = [(0, 1), (1, 0)]
    last = ctx_count - 1

    def other_half(x):
        return lax.ppermute(x, "heads", swap)

    def from_slot(x, slot):
        return lax.ppermute(x, "ctx", [(i, i ^ slot) for i in range(ctx_count)])

    bounds = jnp.cumsum(pair_lengths[0]).astype(jnp.int32)
    base = (ctx_index * tok_rows).astype(jnp.int32).reshape(1)
    picks = random_blocks[0]
    rand_count = picks.shape[1]
    block_ids = ctx_index * block_count + jnp.arange(block_count, dtype=jnp.int32)
    window = block_ids[:, None] + jnp.arange(-1, 2, dtype=jnp.int32)[None, :]
    listed = jnp.concatenate([window, picks], axis=1)
    inside = (listed >= 0) & (listed < total_blocks)
    slot_of = (listed // block_count) ^ ctx_index
    within = listed % block_count
    early = inside & (slot_of != last)
    items = listed.shape[1]
    early_off = jnp.where(early, (slot_of * block_count + within) * BLOCK, 0).reshape(-1)
    early_pos = jnp.where(early, listed * BLOCK, -(2**30)).reshape(-1)
    late = (inside & (slot_of == last)).reshape(-1)
    pick_count = block_count * rand_count
    late_items = min(max(2, -(-pick_count // ctx_count)) + 2, block_count * items)
    rank = jnp.cumsum(late.astype(jnp.int32)) - 1
    place = late[None, :] & (rank[None, :] == jnp.arange(late_items, dtype=jnp.int32)[:, None])

    def compact(x):
        return jnp.sum(jnp.where(place, x.reshape(-1)[None, :], 0), axis=1).astype(jnp.int32)

    late_valid = jnp.any(place, axis=1).astype(jnp.int32)
    late_block = compact(jnp.broadcast_to(jnp.arange(block_count)[:, None], listed.shape))
    late_off = compact(within * BLOCK)
    late_pos = compact(listed * BLOCK)
    summaries = summary_pos.shape[1]
    per_device = summaries // ctx_count
    mine_pos = lax.dynamic_slice_in_dim(summary_pos[0], ctx_index * per_device, per_device, 0)
    mine_lists = lax.dynamic_slice_in_dim(summary_blocks[0], ctx_index * per_device, per_device, 0)
    mine = (mine_pos - ctx_index * tok_rows).astype(jnp.int32)
    slot_blocks = (
        (jnp.arange(ctx_count, dtype=jnp.int32) ^ ctx_index)[:, None] * block_count
        + jnp.arange(block_count, dtype=jnp.int32)
    ).reshape(-1)
    in_list = jnp.any(mine_lists[:, :, None] == slot_blocks[None, None, :], axis=1)
    slot_pos = (slot_blocks[:, None] * BLOCK + jnp.arange(BLOCK, dtype=jnp.int32)).reshape(-1)
    seen = jnp.repeat(in_list, BLOCK, axis=1) & (
        segment_ids(slot_pos, bounds)[None, :] == segment_ids(mine_pos, bounds)[:, None]
    )
    sbias = jnp.pad(jnp.where(seen, 0.0, MASKED), ((0, 8 - per_device), (0, 0)))

    there = [other_half(own_tokens)]
    here = [own_tokens]
    for slot in range(1, last):
        here.append(from_slot(own_tokens, slot))
        there.append(other_half(here[-1]))
    split = 2
    piece = tok_rows // split
    late_here = [from_slot(own_tokens[i * piece : (i + 1) * piece], last) for i in range(split)]
    late_there = [other_half(x) for x in late_here]

    early_rows = last * tok_rows
    held = project(side, here[0], there[0], w_qkv, 0, early_rows, 0, None)
    for slot in range(1, last):
        held = project(side, here[slot], there[slot], w_qkv, 1, early_rows, slot, held)
    late_held = None
    for i in range(split):
        late_held = project(side, late_here[i], late_there[i], w_qkv, 1, tok_rows, i, late_held)

    smem = pl.BlockSpec(memory_space=pltpu.SMEM)
    rows_spec = pl.BlockSpec((BLOCK, cols), lambda i: (i, 0))
    ml_spec = pl.BlockSpec((BLOCK, LANES), lambda i: (i, 0))
    q_spec = pl.BlockSpec((1, BLOCK, cols), lambda i: (0, i, 0))
    q_all_spec = pl.BlockSpec((1, tok_rows, cols), lambda i: (0, 0, 0))

    def kv_spec(j, rows):
        return pl.BlockSpec((1, rows, cols), lambda i: (j, 0, 0))

    srows = 8 * head_count
    acc, ml, sacc, sml = pl.pallas_call(
        functools.partial(
            early_kernel, items=items, pair_count=pair_count, head_count=head_count
        ),
        grid=(block_count,),
        in_specs=[smem] * 5
        + [
            q_spec,
            q_all_spec,
            kv_spec(1, early_rows),
            kv_spec(2, early_rows),
            whole_block(sbias.shape),
        ],
        out_specs=[rows_spec, ml_spec, whole_block((srows, cols)), whole_block((srows, LANES))],
        out_shape=[
            jax.ShapeDtypeStruct((tok_rows, cols), F32),
            jax.ShapeDtypeStruct((tok_rows, LANES), F32),
            jax.ShapeDtypeStruct((srows, cols), F32),
            jax.ShapeDtypeStruct((srows, LANES), F32),
        ],
        scratch_shapes=[pltpu.VMEM((PAIR * BLOCK, items * BLOCK), F32)],
        compiler_params=params("arbitrary"),
        cost_estimate=pl.CostEstimate(
            flops=8 * tok_rows * items * BLOCK * cols,
            bytes_accessed=4 * early_rows * cols + 8 * tok_rows * cols,
            transcendentals=tok_rows * items * BLOCK * head_count,
        ),
        name="early_attention",
    )(early_off, early_pos, bounds, mine, base, held, held, held, held, sbias)

    own_term, other_term = pl.pallas_call(
        functools.partial(
            late_kernel,
            items=late_items,
            pair_count=pair_count,
            head_count=head_count,
            early_keys=early_rows,
        ),
        grid=(block_count,),
        in_specs=[smem] * 8
        + [
            q_spec,
            q_all_spec,
            kv_spec(1, tok_rows),
            kv_spec(2, tok_rows),
            whole_block(sbias.shape),
            rows_spec,
            ml_spec,
            whole_block((srows, cols)),
            whole_block((srows, LANES)),
            whole_block(w_out.shape),
        ],
        out_specs=[pl.BlockSpec((BLOCK, half), lambda i: (i, 0))] * 2,
        out_shape=[jax.ShapeDtypeStruct((tok_rows, half), BF16)] * 2,
        scratch_shapes=[
            pltpu.VMEM((BLOCK, cols), F32),
            pltpu.VMEM((BLOCK, LANES), F32),
            pltpu.VMEM((8, cols), F32),
        ],
        compiler_params=params("arbitrary"),
        cost_estimate=pl.CostEstimate(
            flops=4 * tok_rows * cols * full_width,
            bytes_accessed=12 * tok_rows * cols,
            transcendentals=late_items * BLOCK * BLOCK * head_count,
        ),
        name="late_attention",
    )(
        late_valid, late_block, late_off, late_pos, bounds, mine, base, side,
        held, held, late_held, late_held, sbias, acc, ml, sacc, sml, w_out,
    )

    received = other_half(other_term)
    hidden = own_tokens.astype(F32) + (own_term.astype(F32) + received.astype(F32))
    sums = jnp.stack([jnp.sum(hidden, axis=1), jnp.sum(hidden * hidden, axis=1)])
    sums = sums + other_half(sums)
    row_mean = sums[0] / full_width
    row_var = sums[1] / full_width - row_mean * row_mean
    normed = (hidden - row_mean[:, None]) * lax.rsqrt(row_var + 1e-05)[:, None] * ln_gain + ln_bias
    return normed.astype(BF16)[None]


def shards(*arrays):
    tokens, w_qkv, random_blocks = arrays[0], arrays[1], arrays[5]
    ctx_count = lax.axis_size("ctx")
    picked = random_blocks.shape[1] * random_blocks.shape[2]
    if (
        lax.axis_size("heads") == 2
        and 2 <= ctx_count <= picked
        and ctx_count & (ctx_count - 1) == 0
        and w_qkv.shape[2] % LANES == 0
        and arrays[6].shape[1] // ctx_count <= 8
    ):
        return gathered(*arrays)
    return requested(*arrays)


def solution(mesh):
    in_specs = (
        P(("groups", "dp"), "ctx", "heads"),
        P(None, None, "heads"),
        P("heads", None),
        P("heads"),
        P("heads"),
        P(("groups", "dp"), "ctx", None),
        P(("groups", "dp"), None),
        P(("groups", "dp"), None, None),
        P(("groups", "dp"), None),
    )
    out_specs = P(("groups", "dp"), "ctx", "heads")
    return jax.shard_map(shards, mesh=mesh, in_specs=in_specs, out_specs=out_specs, check_vma=False)
```

```python
import functools
import jax
import jax.numpy as jnp
from jax import lax
from jax.experimental import pallas as pl
from jax.experimental.pallas import tpu as pltpu
from jax.sharding import PartitionSpec as P

HEAD = 64
BLOCK = 128


MASKED = -1e30


def extended(x, sides, width):
    for axis, dim in sides:
        size, length = (lax.axis_size(axis), x.shape[dim])
        up = [(i, (i + 1) % size) for i in range(size - 1)]
        down = [(j, i) for i, j in up]
        last = lax.slice_in_dim(x, length - width, length, axis=dim)
        first = lax.slice_in_dim(x, 0, width, axis=dim)
        before = lax.ppermute(last, axis, up)
        after = lax.ppermute(first, axis, down)
        x = jnp.concatenate([before, x, after], axis=dim)
    return x


def segment_ids(positions, bounds):
    return jnp.sum((positions[..., None] >= bounds).astype(jnp.int32), axis=-1)


def attend(queries, keys, values, allowed, head_count):
    group_count, query_len, all_width = queries.shape
    key_len = keys.shape[1]
    query_heads = queries.reshape(group_count, query_len, head_count, HEAD)
    key_heads = keys.reshape(group_count, key_len, head_count, HEAD)
    value_heads = values.reshape(group_count, key_len, head_count, HEAD)
    scores = jnp.einsum(
        "gqhe,gkhe->ghqk", query_heads, key_heads, preferred_element_type=jnp.float32
    ) * HEAD ** (-0.5)
    scores = jnp.where(allowed[:, None], scores, MASKED)
    maxima = jnp.max(scores, axis=-1, keepdims=True)
    weights = jnp.where(allowed[:, None], jnp.exp(scores - maxima), 0.0)
    totals = jnp.sum(weights, axis=-1)
    mixture = jnp.einsum(
        "ghqk,gkhe->gqhe",
        weights.astype(jnp.bfloat16),
        value_heads,
        preferred_element_type=jnp.float32,
    )
    mixture = mixture / jnp.transpose(totals, (0, 2, 1))[..., None]
    return mixture.reshape(group_count, query_len, all_width).astype(jnp.bfloat16)


def three_views(window_span, group_size, axis_pos):
    views = []
    for shift_index in range(3):
        piece = lax.slice_in_dim(
            window_span,
            shift_index * BLOCK,
            shift_index * BLOCK + group_size * BLOCK,
            axis=axis_pos,
        )
        new_shape = (
            window_span.shape[:axis_pos] + (group_size, BLOCK) + window_span.shape[axis_pos + 1 :]
        )
        views.append(piece.reshape(new_shape))
    return jnp.concatenate(views, axis=axis_pos + 1)


def requested(
    tokens, w_qkv, w_out, ln_gain, ln_bias, random_blocks, summary_pos, summary_blocks, pair_lengths
):
    tok_rows = tokens.shape[1]
    head_cols = tokens.shape[2]
    heads_here = head_cols // HEAD
    full_width = w_out.shape[1]
    ctx_count = lax.axis_size("ctx")
    ctx_index = lax.axis_index("ctx")
    block_count = tok_rows // BLOCK
    seq_total = tok_rows * ctx_count
    bounds = jnp.cumsum(pair_lengths[0])
    own_tokens = tokens[0]
    projected = jnp.einsum(
        "nc,kcd->knd",
        lax.all_gather(own_tokens, "heads", axis=1, tiled=True),
        w_qkv,
        preferred_element_type=jnp.float32,
    ).astype(jnp.bfloat16)
    queries = projected[0]
    own_kv = projected[1:3]
    rim_kv = extended(own_kv, (("ctx", 1),), BLOCK)
    query_pos = ctx_index * tok_rows + jnp.arange(tok_rows, dtype=jnp.int32)
    own_seg = segment_ids(query_pos, bounds)
    rim_pos = ctx_index * tok_rows - BLOCK + jnp.arange(tok_rows + 2 * BLOCK, dtype=jnp.int32)
    rim_ok = (rim_pos >= 0) & (rim_pos < seq_total)
    rim_seg = segment_ids(rim_pos, bounds)
    rand_count = random_blocks.shape[2]
    picked = random_blocks[0].reshape(-1)
    pick_count = picked.shape[0]
    capacity = max(2, -(-pick_count // ctx_count))
    owners = picked // block_count
    within = picked % block_count
    slot_order = jnp.arange(pick_count, dtype=jnp.int32)
    earlier = (owners[:, None] == owners[None, :]) & (slot_order[None, :] < slot_order[:, None])
    pick_rank = jnp.sum(earlier.astype(jnp.int32), axis=1)
    pick_slot = owners * capacity + pick_rank
    slot_table = (
        pick_slot[:, None] == jnp.arange(ctx_count * capacity, dtype=jnp.int32)[None, :]
    ).astype(jnp.int32)
    requests = jnp.sum(slot_table * within[:, None], axis=0).reshape(ctx_count, capacity)
    own_blocks = own_kv.reshape(2, block_count, BLOCK, head_cols).transpose(1, 0, 2, 3)
    reply = jnp.take(
        own_blocks, lax.all_to_all(requests, "ctx", split_axis=0, concat_axis=0, tiled=True), axis=0
    )
    fetched = lax.all_to_all(reply, "ctx", split_axis=0, concat_axis=0, tiled=True)
    flat_blocks = fetched.reshape(ctx_count * capacity, 2, BLOCK, head_cols)
    far_kv = jnp.take(flat_blocks, pick_slot, axis=0).reshape(
        block_count, rand_count, 2, BLOCK, head_cols
    )
    far_kv = far_kv.transpose(2, 0, 1, 3, 4).reshape(2, block_count, rand_count * BLOCK, head_cols)
    far_pos = (
        picked.reshape(block_count, rand_count)[:, :, None] * BLOCK
        + jnp.arange(BLOCK, dtype=jnp.int32)
    ).reshape(block_count, rand_count * BLOCK)
    far_seg = segment_ids(far_pos, bounds)
    group_size = min(4, block_count)
    group_steps = block_count // group_size

    def window_step(unused, step_index):
        near_kv = three_views(rim_kv, group_size, 1)
        near_ok = three_views(rim_ok, group_size, 0)
        near_seg = three_views(rim_seg, group_size, 0)
        key_set = jnp.concatenate([near_kv, far_kv], axis=2)
        key_seg = jnp.concatenate([near_seg, far_seg], axis=1)
        key_ok = jnp.concatenate([near_ok, jnp.ones(far_seg.shape, jnp.bool_)], axis=1)
        query_seg = own_seg.reshape(group_size, BLOCK)
        allowed = key_ok[:, None, :] & (key_seg[:, None, :] == query_seg[:, :, None])
        query_group = queries.reshape(group_size, BLOCK, head_cols)
        return (unused, attend(query_group, key_set[0], key_set[1], allowed, heads_here))

    _, window_out = lax.scan(window_step, 0, jnp.arange(group_steps, dtype=jnp.int32))
    attention = window_out.reshape(tok_rows, head_cols)
    summary_rows = summary_pos[0]
    summary_lists = summary_blocks[0]
    summaries = summary_rows.shape[0]
    per_device = summaries // ctx_count
    mine = (
        lax.dynamic_slice_in_dim(summary_rows, ctx_index * per_device, per_device, 0)
        - ctx_index * tok_rows
    )
    summary_query = jnp.take(queries, mine, axis=0)
    all_queries = lax.all_gather(summary_query, "ctx", axis=0, tiled=True)
    summary_seg = segment_ids(summary_rows, bounds)
    key_block = ctx_index * block_count + jnp.arange(block_count, dtype=jnp.int32)
    listed = jnp.any(summary_lists[:, :, None] == key_block[None, None, :], axis=1)
    key_heads = own_kv[0].reshape(tok_rows, heads_here, HEAD)
    value_heads = own_kv[1].reshape(tok_rows, heads_here, HEAD)
    summary_group = min(128, summaries)
    group_total = summaries // summary_group

    def group_scores():
        query_part = all_queries.reshape(summary_group, heads_here, HEAD)
        allowed = jnp.broadcast_to(listed[:, :, None], (summary_group, block_count, BLOCK)).reshape(
            summary_group, tok_rows
        )
        allowed = allowed & (own_seg[None, :] == summary_seg[:, None])
        scores = jnp.einsum(
            "qhe,khe->hqk", query_part, key_heads, preferred_element_type=jnp.float32
        ) * HEAD ** (-0.5)
        return (jnp.where(allowed[None], scores, MASKED), allowed)

    def weigh(scores, allowed, maxima):
        weights = jnp.where(allowed[None], jnp.exp(scores - maxima[:, :, None]), 0.0)
        totals = jnp.sum(weights, axis=-1)
        mixture = jnp.einsum(
            "hqk,khe->qhe",
            weights.astype(jnp.bfloat16),
            value_heads,
            preferred_element_type=jnp.float32,
        )
        return (totals.T, mixture.reshape(summary_group, head_cols))

    def max_step(unused, group_index):
        scores, allowed = group_scores()
        return (unused, jnp.max(scores, axis=-1).T)

    _, maxima_all = lax.scan(max_step, 0, jnp.arange(group_total, dtype=jnp.int32))
    maxima_all = lax.pmax(maxima_all.reshape(summaries, heads_here), "ctx")

    def sum_step(unused, group_index):
        scores, allowed = group_scores()
        maxima = maxima_all.T
        return (unused, weigh(scores, allowed, maxima))

    _, (totals_all, mixture_all) = lax.scan(sum_step, 0, jnp.arange(group_total, dtype=jnp.int32))
    totals_all = totals_all.reshape(summaries, heads_here)
    mixture_all = mixture_all.reshape(summaries, head_cols)
    totals_all, mixture_all = (
        lax.psum(totals_all.astype(jnp.bfloat16), "ctx").astype(jnp.float32),
        lax.psum(mixture_all.astype(jnp.bfloat16), "ctx").astype(jnp.float32),
    )
    own_totals = lax.dynamic_slice_in_dim(totals_all, ctx_index * per_device, per_device, 0)
    own_mixture = lax.dynamic_slice_in_dim(mixture_all, ctx_index * per_device, per_device, 0)
    summary_out = (own_mixture / jnp.repeat(own_totals, HEAD, axis=1)).astype(jnp.bfloat16)
    attention = attention.at[mine].set(summary_out)
    partial_value = jnp.dot(attention, w_out, preferred_element_type=jnp.float32)
    summed = lax.psum_scatter(
        partial_value.astype(jnp.bfloat16), "heads", scatter_dimension=1, tiled=True
    ).astype(jnp.float32)
    hidden = own_tokens.astype(jnp.float32) + summed
    row_sums = lax.psum((jnp.sum(hidden, axis=1), jnp.sum(hidden * hidden, axis=1)), "heads")
    row_mean = row_sums[0] / full_width
    row_var = row_sums[1] / full_width - row_mean * row_mean
    normed = (hidden - row_mean[:, None]) * lax.rsqrt(row_var + 1e-05)[:, None] * ln_gain + ln_bias
    return normed.astype(jnp.bfloat16)[None]


LANES = 128
PAIR = LANES // HEAD
VMEM_LIMIT = 48 * 1024 * 1024
F32 = jnp.float32
BF16 = jnp.bfloat16
NT = (((1,), (1,)), ((), ()))


def whole_block(shape):
    return pl.BlockSpec(shape, lambda *_: (0,) * len(shape))


def params(*semantics):
    return pltpu.CompilerParams(
        dimension_semantics=semantics or None, vmem_limit_bytes=VMEM_LIMIT
    )


def project_kernel(side_ref, here_ref, there_ref, w_ref, *refs):
    out_ref = refs[-1]
    half = here_ref.shape[1]
    low = pl.multiple_of(side_ref[0] * half, half)
    high = pl.multiple_of((1 - side_ref[0]) * half, half)
    product = jnp.dot(here_ref[...], w_ref[0, pl.ds(low, half), :], preferred_element_type=F32)
    product += jnp.dot(there_ref[...], w_ref[0, pl.ds(high, half), :], preferred_element_type=F32)
    out_ref[0] = product.astype(BF16)


def project(side, here, there, w_qkv, first, total_rows, row_block, held):
    rows, half = here.shape
    cols = w_qkv.shape[2]
    in_specs = [
        pl.BlockSpec(memory_space=pltpu.SMEM),
        whole_block((rows, half)),
        whole_block((rows, half)),
        pl.BlockSpec((1, 2 * half, cols), lambda j: (j + first, 0, 0)),
    ]
    args = [side, here, there, w_qkv]
    aliases = {}
    if held is not None:
        in_specs.append(pl.BlockSpec(memory_space=pl.ANY))
        args.append(held)
        aliases = {4: 0}
    count = 3 - first
    return pl.pallas_call(
        project_kernel,
        grid=(count,),
        in_specs=in_specs,
        out_specs=pl.BlockSpec((1, rows, cols), lambda j: (j + first, row_block, 0)),
        out_shape=jax.ShapeDtypeStruct((3, total_rows, cols), BF16),
        input_output_aliases=aliases,
        compiler_params=params("arbitrary"),
        cost_estimate=pl.CostEstimate(
            flops=4 * rows * half * cols * count,
            bytes_accessed=2 * count * (2 * half * cols + rows * cols) + 4 * rows * half,
            transcendentals=0,
        ),
        name="project",
    )(*args)


def segments_of(position, bounds_ref, pair_count):
    segment = jnp.zeros(position.shape, jnp.int32)
    for pair in range(pair_count):
        segment += (position >= bounds_ref[pair]).astype(jnp.int32)
    return segment


def item_bias(query_seg, key_pos, bounds_ref, pair_count):
    lane = lax.broadcasted_iota(jnp.int32, (1, BLOCK), 1)
    key_seg = segments_of(key_pos + lane, bounds_ref, pair_count)
    key_seg = jnp.where(key_pos >= 0, key_seg, -1)
    return jnp.where(query_seg == key_seg, 0.0, MASKED)


def split_heads(pair_queries):
    lane = lax.broadcasted_iota(jnp.int32, pair_queries.shape, 1)
    scaled = pair_queries.astype(F32) * HEAD ** (-0.5)
    low = jnp.where(lane < HEAD, scaled, 0.0)
    high = jnp.where(lane >= HEAD, scaled, 0.0)
    return jnp.concatenate([low, high], axis=0).astype(BF16)


def join_heads(stacked):
    rows = stacked.shape[0] // PAIR
    lane = lax.broadcasted_iota(jnp.int32, (rows, LANES), 1)
    return jnp.where(lane < HEAD, stacked[:rows], stacked[rows:])


def spread_pair(low, high):
    lane = lax.broadcasted_iota(jnp.int32, (low.shape[0], LANES), 1)
    return jnp.where(lane < HEAD, low, high)


def summary_queries(rows_ref, q_ref, head_count):
    tok_rows, cols = q_ref.shape
    row = lax.broadcasted_iota(jnp.int32, (8, tok_rows), 0)
    col = lax.broadcasted_iota(jnp.int32, (8, tok_rows), 1)
    chosen = jnp.zeros((8, tok_rows), F32)
    for u in range(rows_ref.shape[0]):
        chosen = jnp.where((row == u) & (col == rows_ref[u]), 1.0, chosen)
    picked = jnp.dot(chosen.astype(BF16), q_ref[...], preferred_element_type=F32)
    picked = picked * HEAD ** (-0.5)
    lane = lax.broadcasted_iota(jnp.int32, (8, cols), 1)
    parts = [
        jnp.where((lane >= h * HEAD) & (lane < (h + 1) * HEAD), picked, 0.0)
        for h in range(head_count)
    ]
    return jnp.concatenate(parts, axis=0).astype(BF16)


def early_kernel(
    off_ref, pos_ref, bounds_ref, mine_ref, base_ref,
    q_ref, q_all_ref, k_ref, v_ref, sbias_ref,
    acc_ref, ml_ref, sacc_ref, sml_ref, squery_ref,
    bias_ref, *, items, pair_count, head_count,
):
    step = pl.program_id(0)
    row = lax.broadcasted_iota(jnp.int32, (BLOCK, 1), 0)
    query_seg = segments_of(base_ref[0] + step * BLOCK + row, bounds_ref, pair_count)
    offsets = []
    for item in range(items):
        at = step * items + item
        offsets.append(pl.multiple_of(off_ref[at], BLOCK))
        bias = item_bias(query_seg, pos_ref[at], bounds_ref, pair_count)
        bias_ref[:BLOCK, item * BLOCK : (item + 1) * BLOCK] = bias
        bias_ref[BLOCK:, item * BLOCK : (item + 1) * BLOCK] = bias
    lane = lax.broadcasted_iota(jnp.int32, (BLOCK, LANES), 1)
    state = jnp.zeros((BLOCK, LANES), F32)
    for pair in range(head_count // PAIR):
        cols = slice(pair * LANES, (pair + 1) * LANES)
        stacked = split_heads(q_ref[0, :, cols])
        keys = jnp.concatenate([k_ref[0, pl.ds(o, BLOCK), cols] for o in offsets], axis=0)
        values = jnp.concatenate([v_ref[0, pl.ds(o, BLOCK), cols] for o in offsets], axis=0)
        scores = lax.dot_general(stacked, keys, NT, preferred_element_type=F32) + bias_ref[...]
        top = jnp.max(scores, axis=1, keepdims=True)
        weights = jnp.exp(scores - top)
        total = jnp.sum(weights, axis=1, keepdims=True)
        mixture = jnp.dot(weights.astype(BF16), values, preferred_element_type=F32)
        acc_ref[:, cols] = join_heads(mixture)
        for j in range(PAIR):
            h = pair * PAIR + j
            rows = slice(j * BLOCK, (j + 1) * BLOCK)
            state = jnp.where(lane == h, top[rows], state)
            state = jnp.where(lane == head_count + h, total[rows], state)
    ml_ref[...] = state

    @pl.when(step == 0)
    def _():
        queries = summary_queries(mine_ref, q_all_ref.at[0], head_count)
        squery_ref[...] = queries
        keys = k_ref.shape[1]
        scores = lax.dot_general(queries, k_ref[0], NT, preferred_element_type=F32)
        scores = scores + jnp.concatenate([sbias_ref[:, :keys]] * head_count, axis=0)
        top = jnp.max(scores, axis=1, keepdims=True)
        weights = jnp.exp(scores - top)
        total = jnp.sum(weights, axis=1, keepdims=True)
        sacc_ref[...] = jnp.dot(weights.astype(BF16), v_ref[0], preferred_element_type=F32)
        slane = lax.broadcasted_iota(jnp.int32, sml_ref.shape, 1)
        sml_ref[...] = jnp.where(slane == 0, top, total)


def late_kernel(
    valid_ref, block_ref, off_ref, pos_ref, bounds_ref, mine_ref, base_ref, side_ref,
    q_ref, k_ref, v_ref, sbias_ref, acc_ref, ml_ref, sacc_ref, sml_ref, squery_ref, w_ref,
    own_ref, other_ref,
    mix_ref, state_ref, *, items, pair_count, head_count, early_keys,
):
    tok_rows, cols_all = mix_ref.shape
    lane = lax.broadcasted_iota(jnp.int32, (BLOCK, LANES), 1)
    mix_ref[...] = acc_ref[...]
    state_ref[...] = ml_ref[...]
    row = lax.broadcasted_iota(jnp.int32, (BLOCK, 1), 0)
    for item in range(items):

        @pl.when(valid_ref[item] == 1)
        def _():
            offset = pl.multiple_of(off_ref[item], BLOCK)
            first = pl.multiple_of(block_ref[item] * BLOCK, BLOCK)
            queries = pl.ds(first, BLOCK)
            query_seg = segments_of(base_ref[0] + first + row, bounds_ref, pair_count)
            bias = item_bias(query_seg, pos_ref[item], bounds_ref, pair_count)
            bias = jnp.concatenate([bias] * PAIR, axis=0)
            state = state_ref[queries, :]
            fresh = state
            for pair in range(head_count // PAIR):
                cols = slice(pair * LANES, (pair + 1) * LANES)
                heads = [pair * PAIR + j for j in range(PAIR)]
                scores = (
                    lax.dot_general(
                        split_heads(q_ref[0, queries, cols]),
                        k_ref[0, pl.ds(offset, BLOCK), cols],
                        NT,
                        preferred_element_type=F32,
                    )
                    + bias
                )
                before = jnp.concatenate([state[:, h : h + 1] for h in heads], axis=0)
                count = jnp.concatenate(
                    [state[:, head_count + h : head_count + h + 1] for h in heads], axis=0
                )
                top = jnp.maximum(before, jnp.max(scores, axis=1, keepdims=True))
                weights = jnp.exp(scores - top)
                fade = jnp.exp(before - top)
                total = count * fade + jnp.sum(weights, axis=1, keepdims=True)
                mixture = jnp.dot(
                    weights.astype(BF16),
                    v_ref[0, pl.ds(offset, BLOCK), cols],
                    preferred_element_type=F32,
                )
                mix_ref[queries, cols] = mix_ref[queries, cols] * spread_pair(
                    fade[:BLOCK], fade[BLOCK:]
                ) + join_heads(mixture)
                for j, h in enumerate(heads):
                    rows = slice(j * BLOCK, (j + 1) * BLOCK)
                    fresh = jnp.where(lane == h, top[rows], fresh)
                    fresh = jnp.where(lane == head_count + h, total[rows], fresh)
            state_ref[queries, :] = fresh

    scores = lax.dot_general(squery_ref[...], k_ref[0], NT, preferred_element_type=F32)
    scores = scores + jnp.concatenate([sbias_ref[:, early_keys:]] * head_count, axis=0)
    before = sml_ref[:, 0:1]
    top = jnp.maximum(before, jnp.max(scores, axis=1, keepdims=True))
    weights = jnp.exp(scores - top)
    fade = jnp.exp(before - top)
    total = sml_ref[:, 1:2] * fade + jnp.sum(weights, axis=1, keepdims=True)
    mixture = sacc_ref[...] * fade + jnp.dot(
        weights.astype(BF16), v_ref[0], preferred_element_type=F32
    )
    mixture = mixture / total
    slane = lax.broadcasted_iota(jnp.int32, (8, cols_all), 1)
    summary = jnp.zeros((8, cols_all), F32)
    for h in range(head_count):
        summary = jnp.where(
            (slane >= h * HEAD) & (slane < (h + 1) * HEAD), mixture[h * 8 : (h + 1) * 8], summary
        )

    all_rows = lax.broadcasted_iota(jnp.int32, (tok_rows, 1), 0)
    columns = []
    for pair in range(head_count // PAIR):
        cols = slice(pair * LANES, (pair + 1) * LANES)
        h = head_count + pair * PAIR
        part = mix_ref[:, cols] / spread_pair(state_ref[:, h : h + 1], state_ref[:, h + 1 : h + 2])
        for u in range(mine_ref.shape[0]):
            part = jnp.where(all_rows == mine_ref[u], summary[u : u + 1, cols], part)
        columns.append(part.astype(BF16))
    attention = jnp.concatenate(columns, axis=1)
    half = w_ref.shape[1] // 2
    low = pl.multiple_of(side_ref[0] * half, half)
    high = pl.multiple_of((1 - side_ref[0]) * half, half)
    other_ref[...] = jnp.dot(
        attention, w_ref[:, pl.ds(high, half)], preferred_element_type=F32
    ).astype(BF16)
    own_ref[...] = jnp.dot(
        attention, w_ref[:, pl.ds(low, half)], preferred_element_type=F32
    ).astype(BF16)


def gathered(
    tokens, w_qkv, w_out, ln_gain, ln_bias, random_blocks, summary_pos, summary_blocks, pair_lengths
):
    tok_rows, half = tokens.shape[1:]
    cols = w_qkv.shape[2]
    head_count = cols // HEAD
    full_width = w_out.shape[1]
    ctx_count = lax.axis_size("ctx")
    ctx_index = lax.axis_index("ctx")
    side = lax.axis_index("heads").astype(jnp.int32).reshape(1)
    block_count = tok_rows // BLOCK
    total_blocks = block_count * ctx_count
    pair_count = pair_lengths.shape[1]
    own_tokens = tokens[0]
    swap = [(0, 1), (1, 0)]
    last = ctx_count - 1

    def other_half(x):
        return lax.ppermute(x, "heads", swap)

    def from_slot(x, slot):
        return lax.ppermute(x, "ctx", [(i, i ^ slot) for i in range(ctx_count)])

    bounds = jnp.cumsum(pair_lengths[0]).astype(jnp.int32)
    base = (ctx_index * tok_rows).astype(jnp.int32).reshape(1)
    picks = random_blocks[0]
    rand_count = picks.shape[1]
    block_ids = ctx_index * block_count + jnp.arange(block_count, dtype=jnp.int32)
    window = block_ids[:, None] + jnp.arange(-1, 2, dtype=jnp.int32)[None, :]
    listed = jnp.concatenate([window, picks], axis=1)
    inside = (listed >= 0) & (listed < total_blocks)
    slot_of = (listed // block_count) ^ ctx_index
    within = listed % block_count
    early = inside & (slot_of != last)
    items = listed.shape[1]
    early_off = jnp.where(early, (slot_of * block_count + within) * BLOCK, 0).reshape(-1)
    early_pos = jnp.where(early, listed * BLOCK, -(2**30)).reshape(-1)
    late = (inside & (slot_of == last)).reshape(-1)
    pick_count = block_count * rand_count
    late_items = min(max(2, -(-pick_count // ctx_count)) + 2, block_count * items)
    rank = jnp.cumsum(late.astype(jnp.int32)) - 1
    place = late[None, :] & (rank[None, :] == jnp.arange(late_items, dtype=jnp.int32)[:, None])

    def compact(x):
        return jnp.sum(jnp.where(place, x.reshape(-1)[None, :], 0), axis=1).astype(jnp.int32)

    late_valid = jnp.any(place, axis=1).astype(jnp.int32)
    late_block = compact(jnp.broadcast_to(jnp.arange(block_count)[:, None], listed.shape))
    late_off = compact(within * BLOCK)
    late_pos = compact(listed * BLOCK)
    summaries = summary_pos.shape[1]
    per_device = summaries // ctx_count
    mine_pos = lax.dynamic_slice_in_dim(summary_pos[0], ctx_index * per_device, per_device, 0)
    mine_lists = lax.dynamic_slice_in_dim(summary_blocks[0], ctx_index * per_device, per_device, 0)
    mine = (mine_pos - ctx_index * tok_rows).astype(jnp.int32)
    slot_blocks = (
        (jnp.arange(ctx_count, dtype=jnp.int32) ^ ctx_index)[:, None] * block_count
        + jnp.arange(block_count, dtype=jnp.int32)
    ).reshape(-1)
    in_list = jnp.any(mine_lists[:, :, None] == slot_blocks[None, None, :], axis=1)
    slot_pos = (slot_blocks[:, None] * BLOCK + jnp.arange(BLOCK, dtype=jnp.int32)).reshape(-1)
    seen = jnp.repeat(in_list, BLOCK, axis=1) & (
        segment_ids(slot_pos, bounds)[None, :] == segment_ids(mine_pos, bounds)[:, None]
    )
    sbias = jnp.pad(jnp.where(seen, 0.0, MASKED), ((0, 8 - per_device), (0, 0)))

    split = 2
    piece = tok_rows // split
    pieces = [[own_tokens[i * piece : (i + 1) * piece] for i in range(split)]]
    here = {0: [own_tokens]}
    for slot in range(1, ctx_count):
        low = slot & -slot
        source = here[0] if slot == 1 else (pieces[0] if slot == low else here[slot - low])
        here[slot] = [from_slot(x, low) for x in source]
    there = {}
    for slot in range(ctx_count):
        ready = here[slot]
        if slot >= 2:
            ready = lax.optimization_barrier((ready, there[slot - 2]))[0]
        there[slot] = [other_half(x) for x in ready]

    early_rows = last * tok_rows
    held, late_held = None, None
    for slot in range(ctx_count):
        for i, (a, b) in enumerate(zip(here[slot], there[slot])):
            if slot == last:
                late_held = project(side, a, b, w_qkv, 1, tok_rows, i, late_held)
            else:
                row_block = slot * len(here[slot]) + i
                held = project(
                    side, a, b, w_qkv, 0 if slot == 0 else 1, early_rows, row_block, held
                )

    smem = pl.BlockSpec(memory_space=pltpu.SMEM)
    rows_spec = pl.BlockSpec((BLOCK, cols), lambda i: (i, 0))
    ml_spec = pl.BlockSpec((BLOCK, LANES), lambda i: (i, 0))
    q_spec = pl.BlockSpec((1, BLOCK, cols), lambda i: (0, i, 0))
    q_all_spec = pl.BlockSpec((1, tok_rows, cols), lambda i: (0, 0, 0))

    def kv_spec(j, rows):
        return pl.BlockSpec((1, rows, cols), lambda i: (j, 0, 0))

    srows = 8 * head_count
    acc, ml, sacc, sml, squery = pl.pallas_call(
        functools.partial(
            early_kernel, items=items, pair_count=pair_count, head_count=head_count
        ),
        grid=(block_count,),
        in_specs=[smem] * 5
        + [
            q_spec,
            q_all_spec,
            kv_spec(1, early_rows),
            kv_spec(2, early_rows),
            whole_block(sbias.shape),
        ],
        out_specs=[
            rows_spec,
            ml_spec,
            whole_block((srows, cols)),
            whole_block((srows, LANES)),
            whole_block((srows, cols)),
        ],
        out_shape=[
            jax.ShapeDtypeStruct((tok_rows, cols), F32),
            jax.ShapeDtypeStruct((tok_rows, LANES), F32),
            jax.ShapeDtypeStruct((srows, cols), F32),
            jax.ShapeDtypeStruct((srows, LANES), F32),
            jax.ShapeDtypeStruct((srows, cols), BF16),
        ],
        scratch_shapes=[pltpu.VMEM((PAIR * BLOCK, items * BLOCK), F32)],
        compiler_params=params("arbitrary"),
        cost_estimate=pl.CostEstimate(
            flops=8 * tok_rows * items * BLOCK * cols,
            bytes_accessed=4 * early_rows * cols + 8 * tok_rows * cols,
            transcendentals=tok_rows * items * BLOCK * head_count,
        ),
        name="early_attention",
    )(early_off, early_pos, bounds, mine, base, held, held, held, held, sbias)

    own_term, other_term = pl.pallas_call(
        functools.partial(
            late_kernel,
            items=late_items,
            pair_count=pair_count,
            head_count=head_count,
            early_keys=early_rows,
        ),
        grid=(1,),
        in_specs=[smem] * 8
        + [
            q_all_spec,
            kv_spec(1, tok_rows),
            kv_spec(2, tok_rows),
            whole_block(sbias.shape),
            whole_block((tok_rows, cols)),
            whole_block((tok_rows, LANES)),
            whole_block((srows, cols)),
            whole_block((srows, LANES)),
            whole_block((srows, cols)),
            whole_block(w_out.shape),
        ],
        out_specs=[whole_block((tok_rows, half))] * 2,
        out_shape=[jax.ShapeDtypeStruct((tok_rows, half), BF16)] * 2,
        scratch_shapes=[pltpu.VMEM((tok_rows, cols), F32), pltpu.VMEM((tok_rows, LANES), F32)],
        compiler_params=params("arbitrary"),
        cost_estimate=pl.CostEstimate(
            flops=4 * tok_rows * cols * full_width,
            bytes_accessed=12 * tok_rows * cols,
            transcendentals=late_items * BLOCK * BLOCK * head_count,
        ),
        name="late_attention",
    )(
        late_valid, late_block, late_off, late_pos, bounds, mine, base, side,
        held, late_held, late_held, sbias, acc, ml, sacc, sml, squery, w_out,
    )

    received = other_half(other_term)
    hidden = own_tokens.astype(F32) + (own_term.astype(F32) + received.astype(F32))
    sums = jnp.stack([jnp.sum(hidden, axis=1), jnp.sum(hidden * hidden, axis=1)])
    sums = sums + other_half(sums)
    row_mean = sums[0] / full_width
    row_var = sums[1] / full_width - row_mean * row_mean
    normed = (hidden - row_mean[:, None]) * lax.rsqrt(row_var + 1e-05)[:, None] * ln_gain + ln_bias
    return normed.astype(BF16)[None]


def shards(*arrays):
    tokens, w_qkv, random_blocks = arrays[0], arrays[1], arrays[5]
    ctx_count = lax.axis_size("ctx")
    picked = random_blocks.shape[1] * random_blocks.shape[2]
    if (
        lax.axis_size("heads") == 2
        and 2 <= ctx_count <= picked
        and ctx_count & (ctx_count - 1) == 0
        and w_qkv.shape[2] % LANES == 0
        and arrays[6].shape[1] // ctx_count <= 8
    ):
        return gathered(*arrays)
    return requested(*arrays)


def solution(mesh):
    in_specs = (
        P(("groups", "dp"), "ctx", "heads"),
        P(None, None, "heads"),
        P("heads", None),
        P("heads"),
        P("heads"),
        P(("groups", "dp"), "ctx", None),
        P(("groups", "dp"), None),
        P(("groups", "dp"), None, None),
        P(("groups", "dp"), None),
    )
    out_specs = P(("groups", "dp"), "ctx", "heads")
    return jax.shard_map(shards, mesh=mesh, in_specs=in_specs, out_specs=out_specs, check_vma=False)
```

```python
import functools
import jax
import jax.numpy as jnp
from jax import lax
from jax.experimental import pallas as pl
from jax.experimental.pallas import tpu as pltpu
from jax.sharding import PartitionSpec as P

HEAD = 64
BLOCK = 128


MASKED = -1e30


def extended(x, sides, width):
    for axis, dim in sides:
        size, length = (lax.axis_size(axis), x.shape[dim])
        up = [(i, (i + 1) % size) for i in range(size - 1)]
        down = [(j, i) for i, j in up]
        last = lax.slice_in_dim(x, length - width, length, axis=dim)
        first = lax.slice_in_dim(x, 0, width, axis=dim)
        before = lax.ppermute(last, axis, up)
        after = lax.ppermute(first, axis, down)
        x = jnp.concatenate([before, x, after], axis=dim)
    return x


def segment_ids(positions, bounds):
    return jnp.sum((positions[..., None] >= bounds).astype(jnp.int32), axis=-1)


def attend(queries, keys, values, allowed, head_count):
    group_count, query_len, all_width = queries.shape
    key_len = keys.shape[1]
    query_heads = queries.reshape(group_count, query_len, head_count, HEAD)
    key_heads = keys.reshape(group_count, key_len, head_count, HEAD)
    value_heads = values.reshape(group_count, key_len, head_count, HEAD)
    scores = jnp.einsum(
        "gqhe,gkhe->ghqk", query_heads, key_heads, preferred_element_type=jnp.float32
    ) * HEAD ** (-0.5)
    scores = jnp.where(allowed[:, None], scores, MASKED)
    maxima = jnp.max(scores, axis=-1, keepdims=True)
    weights = jnp.where(allowed[:, None], jnp.exp(scores - maxima), 0.0)
    totals = jnp.sum(weights, axis=-1)
    mixture = jnp.einsum(
        "ghqk,gkhe->gqhe",
        weights.astype(jnp.bfloat16),
        value_heads,
        preferred_element_type=jnp.float32,
    )
    mixture = mixture / jnp.transpose(totals, (0, 2, 1))[..., None]
    return mixture.reshape(group_count, query_len, all_width).astype(jnp.bfloat16)


def three_views(window_span, group_size, axis_pos):
    views = []
    for shift_index in range(3):
        piece = lax.slice_in_dim(
            window_span,
            shift_index * BLOCK,
            shift_index * BLOCK + group_size * BLOCK,
            axis=axis_pos,
        )
        new_shape = (
            window_span.shape[:axis_pos] + (group_size, BLOCK) + window_span.shape[axis_pos + 1 :]
        )
        views.append(piece.reshape(new_shape))
    return jnp.concatenate(views, axis=axis_pos + 1)


def requested(
    tokens, w_qkv, w_out, ln_gain, ln_bias, random_blocks, summary_pos, summary_blocks, pair_lengths
):
    tok_rows = tokens.shape[1]
    head_cols = tokens.shape[2]
    heads_here = head_cols // HEAD
    full_width = w_out.shape[1]
    ctx_count = lax.axis_size("ctx")
    ctx_index = lax.axis_index("ctx")
    block_count = tok_rows // BLOCK
    seq_total = tok_rows * ctx_count
    bounds = jnp.cumsum(pair_lengths[0])
    own_tokens = tokens[0]
    projected = jnp.einsum(
        "nc,kcd->knd",
        lax.all_gather(own_tokens, "heads", axis=1, tiled=True),
        w_qkv,
        preferred_element_type=jnp.float32,
    ).astype(jnp.bfloat16)
    queries = projected[0]
    own_kv = projected[1:3]
    rim_kv = extended(own_kv, (("ctx", 1),), BLOCK)
    query_pos = ctx_index * tok_rows + jnp.arange(tok_rows, dtype=jnp.int32)
    own_seg = segment_ids(query_pos, bounds)
    rim_pos = ctx_index * tok_rows - BLOCK + jnp.arange(tok_rows + 2 * BLOCK, dtype=jnp.int32)
    rim_ok = (rim_pos >= 0) & (rim_pos < seq_total)
    rim_seg = segment_ids(rim_pos, bounds)
    rand_count = random_blocks.shape[2]
    picked = random_blocks[0].reshape(-1)
    pick_count = picked.shape[0]
    capacity = max(2, -(-pick_count // ctx_count))
    owners = picked // block_count
    within = picked % block_count
    slot_order = jnp.arange(pick_count, dtype=jnp.int32)
    earlier = (owners[:, None] == owners[None, :]) & (slot_order[None, :] < slot_order[:, None])
    pick_rank = jnp.sum(earlier.astype(jnp.int32), axis=1)
    pick_slot = owners * capacity + pick_rank
    slot_table = (
        pick_slot[:, None] == jnp.arange(ctx_count * capacity, dtype=jnp.int32)[None, :]
    ).astype(jnp.int32)
    requests = jnp.sum(slot_table * within[:, None], axis=0).reshape(ctx_count, capacity)
    own_blocks = own_kv.reshape(2, block_count, BLOCK, head_cols).transpose(1, 0, 2, 3)
    reply = jnp.take(
        own_blocks, lax.all_to_all(requests, "ctx", split_axis=0, concat_axis=0, tiled=True), axis=0
    )
    fetched = lax.all_to_all(reply, "ctx", split_axis=0, concat_axis=0, tiled=True)
    flat_blocks = fetched.reshape(ctx_count * capacity, 2, BLOCK, head_cols)
    far_kv = jnp.take(flat_blocks, pick_slot, axis=0).reshape(
        block_count, rand_count, 2, BLOCK, head_cols
    )
    far_kv = far_kv.transpose(2, 0, 1, 3, 4).reshape(2, block_count, rand_count * BLOCK, head_cols)
    far_pos = (
        picked.reshape(block_count, rand_count)[:, :, None] * BLOCK
        + jnp.arange(BLOCK, dtype=jnp.int32)
    ).reshape(block_count, rand_count * BLOCK)
    far_seg = segment_ids(far_pos, bounds)
    group_size = min(4, block_count)
    group_steps = block_count // group_size

    def window_step(unused, step_index):
        near_kv = three_views(rim_kv, group_size, 1)
        near_ok = three_views(rim_ok, group_size, 0)
        near_seg = three_views(rim_seg, group_size, 0)
        key_set = jnp.concatenate([near_kv, far_kv], axis=2)
        key_seg = jnp.concatenate([near_seg, far_seg], axis=1)
        key_ok = jnp.concatenate([near_ok, jnp.ones(far_seg.shape, jnp.bool_)], axis=1)
        query_seg = own_seg.reshape(group_size, BLOCK)
        allowed = key_ok[:, None, :] & (key_seg[:, None, :] == query_seg[:, :, None])
        query_group = queries.reshape(group_size, BLOCK, head_cols)
        return (unused, attend(query_group, key_set[0], key_set[1], allowed, heads_here))

    _, window_out = lax.scan(window_step, 0, jnp.arange(group_steps, dtype=jnp.int32))
    attention = window_out.reshape(tok_rows, head_cols)
    summary_rows = summary_pos[0]
    summary_lists = summary_blocks[0]
    summaries = summary_rows.shape[0]
    per_device = summaries // ctx_count
    mine = (
        lax.dynamic_slice_in_dim(summary_rows, ctx_index * per_device, per_device, 0)
        - ctx_index * tok_rows
    )
    summary_query = jnp.take(queries, mine, axis=0)
    all_queries = lax.all_gather(summary_query, "ctx", axis=0, tiled=True)
    summary_seg = segment_ids(summary_rows, bounds)
    key_block = ctx_index * block_count + jnp.arange(block_count, dtype=jnp.int32)
    listed = jnp.any(summary_lists[:, :, None] == key_block[None, None, :], axis=1)
    key_heads = own_kv[0].reshape(tok_rows, heads_here, HEAD)
    value_heads = own_kv[1].reshape(tok_rows, heads_here, HEAD)
    summary_group = min(128, summaries)
    group_total = summaries // summary_group

    def group_scores():
        query_part = all_queries.reshape(summary_group, heads_here, HEAD)
        allowed = jnp.broadcast_to(listed[:, :, None], (summary_group, block_count, BLOCK)).reshape(
            summary_group, tok_rows
        )
        allowed = allowed & (own_seg[None, :] == summary_seg[:, None])
        scores = jnp.einsum(
            "qhe,khe->hqk", query_part, key_heads, preferred_element_type=jnp.float32
        ) * HEAD ** (-0.5)
        return (jnp.where(allowed[None], scores, MASKED), allowed)

    def weigh(scores, allowed, maxima):
        weights = jnp.where(allowed[None], jnp.exp(scores - maxima[:, :, None]), 0.0)
        totals = jnp.sum(weights, axis=-1)
        mixture = jnp.einsum(
            "hqk,khe->qhe",
            weights.astype(jnp.bfloat16),
            value_heads,
            preferred_element_type=jnp.float32,
        )
        return (totals.T, mixture.reshape(summary_group, head_cols))

    def max_step(unused, group_index):
        scores, allowed = group_scores()
        return (unused, jnp.max(scores, axis=-1).T)

    _, maxima_all = lax.scan(max_step, 0, jnp.arange(group_total, dtype=jnp.int32))
    maxima_all = lax.pmax(maxima_all.reshape(summaries, heads_here), "ctx")

    def sum_step(unused, group_index):
        scores, allowed = group_scores()
        maxima = maxima_all.T
        return (unused, weigh(scores, allowed, maxima))

    _, (totals_all, mixture_all) = lax.scan(sum_step, 0, jnp.arange(group_total, dtype=jnp.int32))
    totals_all = totals_all.reshape(summaries, heads_here)
    mixture_all = mixture_all.reshape(summaries, head_cols)
    totals_all, mixture_all = (
        lax.psum(totals_all.astype(jnp.bfloat16), "ctx").astype(jnp.float32),
        lax.psum(mixture_all.astype(jnp.bfloat16), "ctx").astype(jnp.float32),
    )
    own_totals = lax.dynamic_slice_in_dim(totals_all, ctx_index * per_device, per_device, 0)
    own_mixture = lax.dynamic_slice_in_dim(mixture_all, ctx_index * per_device, per_device, 0)
    summary_out = (own_mixture / jnp.repeat(own_totals, HEAD, axis=1)).astype(jnp.bfloat16)
    attention = attention.at[mine].set(summary_out)
    partial_value = jnp.dot(attention, w_out, preferred_element_type=jnp.float32)
    summed = lax.psum_scatter(
        partial_value.astype(jnp.bfloat16), "heads", scatter_dimension=1, tiled=True
    ).astype(jnp.float32)
    hidden = own_tokens.astype(jnp.float32) + summed
    row_sums = lax.psum((jnp.sum(hidden, axis=1), jnp.sum(hidden * hidden, axis=1)), "heads")
    row_mean = row_sums[0] / full_width
    row_var = row_sums[1] / full_width - row_mean * row_mean
    normed = (hidden - row_mean[:, None]) * lax.rsqrt(row_var + 1e-05)[:, None] * ln_gain + ln_bias
    return normed.astype(jnp.bfloat16)[None]


LANES = 128
PAIR = LANES // HEAD
VMEM_LIMIT = 14 * 1024 * 1024
F32 = jnp.float32
BF16 = jnp.bfloat16
NT = (((1,), (1,)), ((), ()))


def whole_block(shape):
    return pl.BlockSpec(shape, lambda *_: (0,) * len(shape))


def params(*semantics):
    return pltpu.CompilerParams(
        dimension_semantics=semantics or None, vmem_limit_bytes=VMEM_LIMIT
    )


def project_rows(side_ref, here_ref, there_ref, w_ref):
    half = here_ref.shape[1]
    low = pl.multiple_of(side_ref[0] * half, half)
    high = pl.multiple_of((1 - side_ref[0]) * half, half)
    product = jnp.dot(here_ref[...], w_ref[pl.ds(low, half), :], preferred_element_type=F32)
    product += jnp.dot(there_ref[...], w_ref[pl.ds(high, half), :], preferred_element_type=F32)
    return product.astype(BF16)


def pair_up(refs):
    return list(zip(refs[0::2], refs[1::2]))


def first_kernel(side_ref, here_ref, there_ref, w_hbm, q_ref, kv_ref, w_kv_ref, w_q_ref, sem):
    copies = [pltpu.make_async_copy(w_hbm.at[0], w_q_ref, sem.at[0])]
    copies += [
        pltpu.make_async_copy(w_hbm.at[j + 1], w_kv_ref.at[j], sem.at[j + 1]) for j in range(2)
    ]
    for copy in copies:
        copy.start()
    copies[0].wait()
    q_ref[...] = project_rows(side_ref, here_ref, there_ref, w_q_ref)
    for j in range(2):
        copies[j + 1].wait()
        kv_ref[j] = project_rows(side_ref, here_ref, there_ref, w_kv_ref.at[j])


def pieces_kernel(side_ref, w_kv_ref, *refs):
    count = len(refs) // 3
    for piece, kv_ref in zip(pair_up(refs[: 2 * count]), refs[2 * count :]):
        project_pieces(side_ref, [piece], w_kv_ref, kv_ref, 0)


def segments_of(position, bounds_ref, pair_count):
    segment = jnp.zeros(position.shape, jnp.int32)
    for pair in range(pair_count):
        segment += (position >= bounds_ref[pair]).astype(jnp.int32)
    return segment


def item_bias(query_seg, key_pos, bounds_ref, pair_count):
    lane = lax.broadcasted_iota(jnp.int32, (1, BLOCK), 1)
    key_seg = segments_of(key_pos + lane, bounds_ref, pair_count)
    key_seg = jnp.where(key_pos >= 0, key_seg, -1)
    return jnp.where(query_seg == key_seg, 0.0, MASKED)


def split_heads(pair_queries):
    lane = lax.broadcasted_iota(jnp.int32, pair_queries.shape, 1)
    scaled = pair_queries.astype(F32) * HEAD ** (-0.5)
    low = jnp.where(lane < HEAD, scaled, 0.0)
    high = jnp.where(lane >= HEAD, scaled, 0.0)
    return jnp.concatenate([low, high], axis=0).astype(BF16)


def join_heads(stacked):
    rows = stacked.shape[0] // PAIR
    lane = lax.broadcasted_iota(jnp.int32, (rows, LANES), 1)
    return jnp.where(lane < HEAD, stacked[:rows], stacked[rows:])


def spread_pair(low, high):
    lane = lax.broadcasted_iota(jnp.int32, (low.shape[0], LANES), 1)
    return jnp.where(lane < HEAD, low, high)


def summary_queries(rows_ref, q_ref, head_count):
    tok_rows, cols = q_ref.shape
    row = lax.broadcasted_iota(jnp.int32, (8, tok_rows), 0)
    col = lax.broadcasted_iota(jnp.int32, (8, tok_rows), 1)
    chosen = jnp.zeros((8, tok_rows), F32)
    for u in range(rows_ref.shape[0]):
        chosen = jnp.where((row == u) & (col == rows_ref[u]), 1.0, chosen)
    picked = jnp.dot(chosen.astype(BF16), q_ref[...], preferred_element_type=F32)
    picked = picked * HEAD ** (-0.5)
    lane = lax.broadcasted_iota(jnp.int32, (8, cols), 1)
    parts = [
        jnp.where((lane >= h * HEAD) & (lane < (h + 1) * HEAD), picked, 0.0)
        for h in range(head_count)
    ]
    return jnp.concatenate(parts, axis=0).astype(BF16)


def attend_blocks(
    first_block, block_total, off_ref, pos_ref, bounds_ref, base_ref, q_ref, kv_ref,
    acc_ref, top_ref, sum_ref, bias_ref, score_ref, items, pair_count, head_count,
):
    row = lax.broadcasted_iota(jnp.int32, (BLOCK, 1), 0)

    def block_step(step, carry):
        place = pl.ds(pl.multiple_of(step * BLOCK, BLOCK), BLOCK)
        first = pl.multiple_of((first_block + step) * BLOCK, BLOCK)
        query_seg = segments_of(base_ref[0] + first + row, bounds_ref, pair_count)
        offsets = []
        for item in range(items):
            at = (first_block + step) * items + item
            offsets.append(pl.multiple_of(off_ref[at], BLOCK))
            bias_ref[:, item * BLOCK : (item + 1) * BLOCK] = item_bias(
                query_seg, pos_ref[at], bounds_ref, pair_count
            )
        tops = []
        for pair in range(head_count // PAIR):
            cols = slice(pair * LANES, (pair + 1) * LANES)
            keys = jnp.concatenate([kv_ref[0, pl.ds(o, BLOCK), cols] for o in offsets], axis=0)
            scores = lax.dot_general(
                split_heads(q_ref[pl.ds(first, BLOCK), cols]), keys, NT, preferred_element_type=F32
            )
            for j in range(PAIR):
                rows = slice(j * BLOCK, (j + 1) * BLOCK)
                part = scores[rows] + bias_ref[...]
                score_ref[pair, rows] = part
                tops.append(jnp.max(part, axis=1, keepdims=True))
        for pair in range(head_count // PAIR):
            cols = slice(pair * LANES, (pair + 1) * LANES)
            values = jnp.concatenate([kv_ref[1, pl.ds(o, BLOCK), cols] for o in offsets], axis=0)
            values = jnp.concatenate([values, jnp.ones_like(values)], axis=1)
            peaks = tops[pair * PAIR : (pair + 1) * PAIR]
            weights = jnp.exp(score_ref[pair] - jnp.concatenate(peaks, axis=0)).astype(BF16)
            product = jnp.dot(weights, values, preferred_element_type=F32)
            acc_ref[place, cols] = join_heads(product[:, :LANES])
            sum_ref[place, cols] = join_heads(product[:, LANES:])
            top_ref[place, cols] = spread_pair(*peaks)
        return carry

    lax.fori_loop(0, block_total, block_step, 0)


def project_pieces(side_ref, pieces, w_ref, kv_ref, row):
    for here_ref, there_ref in pieces:
        rows = here_ref.shape[0]
        for j in range(2):
            kv_ref[j, row : row + rows] = project_rows(side_ref, here_ref, there_ref, w_ref.at[j])
        row += rows


def early_kernel(
    off_ref, pos_ref, bounds_ref, base_ref, q_ref, own_ref, *refs, items, pair_count, head_count
):
    *held, acc_ref, top_ref, sum_ref, kv_ref, bias_ref, score_ref, sem = refs
    copies = []
    row = 0
    for i, part in enumerate([own_ref] + held):
        rows = part.shape[1]
        copies.append(pltpu.make_async_copy(part, kv_ref.at[:, pl.ds(row, rows)], sem.at[i]))
        copies[-1].start()
        row += rows
    for copy in copies:
        copy.wait()
    attend_blocks(
        0, acc_ref.shape[0] // BLOCK, off_ref, pos_ref, bounds_ref, base_ref, q_ref, kv_ref,
        acc_ref, top_ref, sum_ref, bias_ref, score_ref, items, pair_count, head_count,
    )


def item_part(q_ref, kv_ref, first, offset, bias, head_count):
    pairs = head_count // PAIR
    scores, tops = [], []
    for pair in range(pairs):
        cols = slice(pair * LANES, (pair + 1) * LANES)
        product = lax.dot_general(
            split_heads(q_ref[pl.ds(first, BLOCK), cols]),
            kv_ref[0, pl.ds(offset, BLOCK), cols],
            NT,
            preferred_element_type=F32,
        )
        product = product + jnp.concatenate([bias] * PAIR, axis=0)
        scores.append(product)
        tops.append(jnp.max(product, axis=1, keepdims=True))
    peaks, totals, mixtures = [], [], []
    for pair in range(pairs):
        cols = slice(pair * LANES, (pair + 1) * LANES)
        weights = jnp.exp(scores[pair] - tops[pair]).astype(BF16)
        values = kv_ref[1, pl.ds(offset, BLOCK), cols]
        values = jnp.concatenate([values, jnp.ones_like(values)], axis=1)
        product = jnp.dot(weights, values, preferred_element_type=F32)
        peaks.append(spread_pair(tops[pair][:BLOCK], tops[pair][BLOCK:]))
        mixtures.append(join_heads(product[:, :LANES]))
        totals.append(join_heads(product[:, LANES:]))
    return peaks, totals, mixtures


def add_items(
    tables, bounds_ref, base_ref, q_ref, kv_ref, state, items, group, pair_count, head_count
):
    valid_ref, block_ref, off_ref, pos_ref = tables
    peak_ref, total_ref, mix_ref = state
    row = lax.broadcasted_iota(jnp.int32, (BLOCK, 1), 0)

    def add_group(start):
        parts = []
        for item in range(start, min(start + group, items)):
            offset = pl.multiple_of(off_ref[item], BLOCK)
            first = pl.multiple_of(block_ref[item] * BLOCK, BLOCK)
            query_seg = segments_of(base_ref[0] + first + row, bounds_ref, pair_count)
            key_pos = jnp.where(valid_ref[item] == 1, pos_ref[item], -(2**30))
            bias = item_bias(query_seg, key_pos, bounds_ref, pair_count)
            parts.append((first, item_part(q_ref, kv_ref, first, offset, bias, head_count)))
        for first, (peaks, totals, mixtures) in parts:
            rows = pl.ds(first, BLOCK)
            for pair in range(head_count // PAIR):
                cols = slice(pair * LANES, (pair + 1) * LANES)
                before = peak_ref[rows, cols]
                top = jnp.maximum(before, peaks[pair])
                fade = jnp.exp(before - top)
                share = jnp.exp(peaks[pair] - top)
                peak_ref[rows, cols] = top
                total_ref[rows, cols] = total_ref[rows, cols] * fade + totals[pair] * share
                mix_ref[rows, cols] = mix_ref[rows, cols] * fade + mixtures[pair] * share

    for start in range(0, items, group):
        pl.when(valid_ref[start] == 1)(functools.partial(add_group, start))


def middle_kernel(
    valid_ref, block_ref, off_ref, pos_ref, bounds_ref, base_ref, mine_ref, side_ref,
    q_ref, w_kv_ref, kv_early_ref, sbias_ref, acc_in, top_in, sum_in,
    here0_ref, there0_ref, here1_ref, there1_ref, w_out_hbm,
    acc_ref, top_ref, sum_ref, sacc_ref, sml_ref, squery_ref, w_out_ref,
    kv_ref, sem, *, items, group, pair_count, head_count,
):
    copy = pltpu.make_async_copy(w_out_hbm, w_out_ref, sem)
    copy.start()
    acc_ref[...] = acc_in[...]
    top_ref[...] = top_in[...]
    sum_ref[...] = sum_in[...]
    pieces = [(here0_ref, there0_ref), (here1_ref, there1_ref)]
    project_pieces(side_ref, pieces, w_kv_ref, kv_ref, 0)
    add_items(
        (valid_ref, block_ref, off_ref, pos_ref), bounds_ref, base_ref, q_ref, kv_ref,
        (top_ref, sum_ref, acc_ref), items, group, pair_count, head_count,
    )
    queries = summary_queries(mine_ref, q_ref, head_count)
    squery_ref[...] = queries
    keys = kv_early_ref.shape[1]
    scores = jnp.concatenate(
        [
            lax.dot_general(queries, part[0], NT, preferred_element_type=F32)
            for part in (kv_early_ref, kv_ref)
        ],
        axis=1,
    )
    scores = scores + jnp.concatenate([sbias_ref[:, : scores.shape[1]]] * head_count, axis=0)
    top = jnp.max(scores, axis=1, keepdims=True)
    weights = jnp.exp(scores - top)
    total = jnp.sum(weights, axis=1, keepdims=True)
    weights = weights.astype(BF16)
    sacc_ref[...] = jnp.dot(weights[:, :keys], kv_early_ref[1], preferred_element_type=F32) + jnp.dot(
        weights[:, keys:], kv_ref[1], preferred_element_type=F32
    )
    slane = lax.broadcasted_iota(jnp.int32, sml_ref.shape, 1)
    sml_ref[...] = jnp.where(slane == 0, top, total)
    copy.wait()


def late_kernel(
    valid_ref, block_ref, off_ref, pos_ref, bounds_ref, base_ref, mine_ref, side_ref,
    q_ref, w_kv_ref, w_ref, sbias_ref, acc_ref, top_ref, sum_ref,
    sacc_ref, sml_ref, squery_ref, fresh_ref, here_ref, there_ref,
    own_ref, other_ref, kv_ref, mix_ref, peak_ref, total_ref,
    *, items, group, pair_count, head_count,
):
    tok_rows, cols_all = mix_ref.shape
    fresh_rows = fresh_ref.shape[1]
    mix_ref[...] = acc_ref[...]
    peak_ref[...] = top_ref[...]
    total_ref[...] = sum_ref[...]
    kv_ref[:, :fresh_rows] = fresh_ref[...]
    project_pieces(side_ref, [(here_ref, there_ref)], w_kv_ref, kv_ref, fresh_rows)
    add_items(
        (valid_ref, block_ref, off_ref, pos_ref), bounds_ref, base_ref, q_ref, kv_ref,
        (peak_ref, total_ref, mix_ref), items, group, pair_count, head_count,
    )

    scores = lax.dot_general(squery_ref[...], kv_ref[0], NT, preferred_element_type=F32)
    keys = scores.shape[1]
    scores = scores + jnp.concatenate([sbias_ref[:, -keys:]] * head_count, axis=0)
    before = sml_ref[:, 0:1]
    top = jnp.maximum(before, jnp.max(scores, axis=1, keepdims=True))
    weights = jnp.exp(scores - top)
    fade = jnp.exp(before - top)
    total = sml_ref[:, 1:2] * fade + jnp.sum(weights, axis=1, keepdims=True)
    mixture = sacc_ref[...] * fade + jnp.dot(
        weights.astype(BF16), kv_ref[1], preferred_element_type=F32
    )
    mixture = mixture / total
    slane = lax.broadcasted_iota(jnp.int32, (8, cols_all), 1)
    summary = jnp.zeros((8, cols_all), F32)
    for h in range(head_count):
        summary = jnp.where(
            (slane >= h * HEAD) & (slane < (h + 1) * HEAD), mixture[h * 8 : (h + 1) * 8], summary
        )

    all_rows = lax.broadcasted_iota(jnp.int32, (tok_rows, 1), 0)
    columns = []
    for pair in range(head_count // PAIR):
        cols = slice(pair * LANES, (pair + 1) * LANES)
        part = mix_ref[:, cols] / total_ref[:, cols]
        for u in range(mine_ref.shape[0]):
            part = jnp.where(all_rows == mine_ref[u], summary[u : u + 1, cols], part)
        columns.append(part.astype(BF16))
    attention = jnp.concatenate(columns, axis=1)
    half = w_ref.shape[1] // 2
    low = pl.multiple_of(side_ref[0] * half, half)
    high = pl.multiple_of((1 - side_ref[0]) * half, half)
    other_ref[...] = jnp.dot(
        attention, w_ref[:, pl.ds(high, half)], preferred_element_type=F32
    ).astype(BF16)
    own_ref[...] = jnp.dot(
        attention, w_ref[:, pl.ds(low, half)], preferred_element_type=F32
    ).astype(BF16)


def gathered(
    tokens, w_qkv, w_out, ln_gain, ln_bias, random_blocks, summary_pos, summary_blocks, pair_lengths
):
    tok_rows, half = tokens.shape[1:]
    cols = w_qkv.shape[2]
    head_count = cols // HEAD
    full_width = w_out.shape[1]
    ctx_count = lax.axis_size("ctx")
    ctx_index = lax.axis_index("ctx")
    side = lax.axis_index("heads").astype(jnp.int32).reshape(1)
    block_count = tok_rows // BLOCK
    total_blocks = block_count * ctx_count
    pair_count = pair_lengths.shape[1]
    own_tokens = tokens[0]
    piece = tok_rows // 2
    piece_blocks = block_count // 2
    arrival = jnp.array([0, 1, 2, 4, 3, 5, 6, 7], jnp.int32)
    place_of = jnp.array([0, 1, 2, 4, 3, 5, 6, 7], jnp.int32)
    early_count, late_count, piece_count = 4, 6, 2 * ctx_count
    early_rows, late_rows = early_count * piece, (piece_count - late_count) * piece

    bounds = jnp.cumsum(pair_lengths[0]).astype(jnp.int32)
    base = (ctx_index * tok_rows).astype(jnp.int32).reshape(1)
    picks = random_blocks[0]
    rand_count = picks.shape[1]
    block_ids = ctx_index * block_count + jnp.arange(block_count, dtype=jnp.int32)
    window = block_ids[:, None] + jnp.arange(-1, 2, dtype=jnp.int32)[None, :]
    listed = jnp.concatenate([window, picks], axis=1)
    items = listed.shape[1]
    inside = (listed >= 0) & (listed < total_blocks)
    slot_of = (listed // block_count) ^ ctx_index
    within = listed % block_count
    number = slot_of * 2 + within // piece_blocks
    place = jnp.sum(
        jnp.where(number[..., None] == jnp.arange(piece_count), place_of, 0), axis=-1
    )
    row = place * piece + (within % piece_blocks) * BLOCK
    early = inside & (place < early_count)
    early_off = jnp.where(early, row, 0).reshape(-1)
    early_pos = jnp.where(early, listed * BLOCK, -(2**30)).reshape(-1)
    capacity = max(2, -(-block_count * rand_count // ctx_count))

    def item_list(first, last, count):
        held = (inside & (place >= first) & (place < last)).reshape(-1)
        rank = jnp.cumsum(held.astype(jnp.int32)) - 1
        chosen = held[None, :] & (rank[None, :] == jnp.arange(count, dtype=jnp.int32)[:, None])

        def compact(x):
            return jnp.sum(jnp.where(chosen, x.reshape(-1)[None, :], 0), axis=1).astype(jnp.int32)

        blocks = jnp.broadcast_to(jnp.arange(block_count, dtype=jnp.int32)[:, None], listed.shape)
        valid = jnp.any(chosen, axis=1).astype(jnp.int32)
        return valid, compact(blocks), compact(row - first * piece), compact(listed * BLOCK)

    middle_items, late_items = 2 * capacity + 1, capacity + 1
    middle_list = item_list(early_count, late_count, middle_items)
    late_list = item_list(late_count, piece_count, late_items)
    summaries = summary_pos.shape[1]
    per_device = summaries // ctx_count
    mine_pos = lax.dynamic_slice_in_dim(summary_pos[0], ctx_index * per_device, per_device, 0)
    mine_lists = lax.dynamic_slice_in_dim(summary_blocks[0], ctx_index * per_device, per_device, 0)
    mine = (mine_pos - ctx_index * tok_rows).astype(jnp.int32)
    piece_first = ((arrival // 2) ^ ctx_index) * block_count + (arrival % 2) * piece_blocks
    key_blocks = (piece_first[:, None] + jnp.arange(piece_blocks, dtype=jnp.int32)).reshape(-1)
    in_list = jnp.any(mine_lists[:, :, None] == key_blocks[None, None, :], axis=1)
    key_pos = (key_blocks[:, None] * BLOCK + jnp.arange(BLOCK, dtype=jnp.int32)).reshape(-1)
    seen = jnp.repeat(in_list, BLOCK, axis=1) & (
        segment_ids(key_pos, bounds)[None, :] == segment_ids(mine_pos, bounds)[:, None]
    )
    sbias = jnp.pad(jnp.where(seen, 0.0, MASKED), ((0, 8 - per_device), (0, 0)))
    tables = (early_off, early_pos, middle_list, late_list, bounds, mine, base, sbias)

    swap = [(0, 1), (1, 0)]

    def other_half(x):
        return lax.ppermute(x, "heads", swap)

    def from_slot(x, slot):
        return lax.ppermute(x, "ctx", [(i, i ^ slot) for i in range(ctx_count)])

    def array(*shape, dtype=F32):
        return jax.ShapeDtypeStruct(shape, dtype)

    def like(arrays):
        return [pltpu.VMEM(x.shape, x.dtype) for x in arrays]

    def whole_call(kernel, scalars, args, far_args, outs, far_outs, scratch, work, name, **sizes):
        far = pl.BlockSpec(memory_space=pltpu.HBM)
        near = pl.BlockSpec(memory_space=pltpu.VMEM)
        return pl.pallas_call(
            functools.partial(kernel, **sizes),
            in_specs=[pl.BlockSpec(memory_space=pltpu.SMEM)] * len(scalars)
            + [near] * len(args)
            + [far] * len(far_args),
            out_specs=[far] * len(far_outs) + [near] * len(outs),
            out_shape=far_outs + outs,
            scratch_shapes=scratch,
            compiler_params=params(),
            cost_estimate=pl.CostEstimate(
                flops=int(work * 1e9), bytes_accessed=int(work * 3.5e6), transcendentals=0
            ),
            name=name,
        )(*scalars, *args, *far_args)

    low, high = own_tokens[:piece], own_tokens[piece:]
    own_there = other_half(own_tokens)
    here2a = from_slot(low, 2)
    here1a = from_slot(low, 1)
    here2a, here1a, high, tables = lax.optimization_barrier((here2a, here1a, high, tables))
    early_off, early_pos, middle_list, late_list, bounds, mine, base, sbias = tables
    here2b = from_slot(high, 2)
    here1b = from_slot(high, 1)
    there1a, there2a = other_half(here1a), other_half(here2a)
    queries, own_kv, w_kv = whole_call(
        first_kernel,
        [side],
        [own_tokens, own_there],
        [w_qkv],
        [array(tok_rows, cols, dtype=BF16), array(2, tok_rows, cols, dtype=BF16)]
        + [array(2, 2 * half, cols, dtype=BF16)],
        [],
        [pltpu.VMEM((2 * half, cols), BF16), pltpu.SemaphoreType.DMA((3,))],
        2,
        "own_projections",
    )
    here2b, here1b, w_kv = lax.optimization_barrier((here2b, here1b, w_kv))
    here3b = from_slot(here2b, 1)
    there1b, there2b = other_half(here1b), other_half(here2b)
    piece_kv = array(2, piece, cols, dtype=BF16)
    kv1a, kv2a = whole_call(
        pieces_kernel,
        [side],
        [w_kv, here1a, there1a, here2a, there2a],
        [],
        [piece_kv, piece_kv],
        [],
        [],
        1,
        "piece_projections",
    )
    kv3a = from_slot(kv2a, 1)
    there3b = other_half(here3b)

    sizes = dict(pair_count=pair_count, head_count=head_count)
    state = [array(tok_rows, cols)] * 3
    *state, kv = whole_call(
        early_kernel,
        [early_off, early_pos, bounds, base],
        [queries, own_kv, kv1a, kv2a],
        [],
        state + [array(2, early_rows, cols, dtype=BF16)],
        [],
        [
            pltpu.VMEM((BLOCK, items * BLOCK), F32),
            pltpu.VMEM((head_count // PAIR, PAIR * BLOCK, items * BLOCK), F32),
            pltpu.SemaphoreType.DMA((3,)),
        ],
        7,
        "early_attention",
        items=items,
        **sizes,
    )
    srows = 8 * head_count
    *state, sacc, sml, squery, w_out_near = whole_call(
        middle_kernel,
        [*middle_list, bounds, base, mine, side],
        [queries, w_kv, kv, sbias, *state, here1b, there1b, here2b, there2b],
        [w_out],
        [array(tok_rows, cols)] * 3
        + [array(srows, cols), array(srows, LANES), array(srows, cols, dtype=BF16)]
        + [array(*w_out.shape, dtype=BF16)],
        [],
        [pltpu.VMEM((2, 2 * piece, cols), BF16), pltpu.SemaphoreType.DMA],
        5,
        "middle_attention",
        items=middle_items,
        group=4,
        **sizes,
    )
    own_term, other_term = whole_call(
        late_kernel,
        [*late_list, bounds, base, mine, side],
        [queries, w_kv, w_out_near, sbias, *state, sacc, sml, squery, kv3a, here3b, there3b],
        [],
        [array(tok_rows, half, dtype=BF16)] * 2,
        [],
        [pltpu.VMEM((2, late_rows, cols), BF16)] + [pltpu.VMEM((tok_rows, cols), F32)] * 3,
        4,
        "late_attention",
        items=late_items,
        group=4,
        **sizes,
    )

    received = other_half(other_term)
    hidden = own_tokens.astype(F32) + (own_term.astype(F32) + received.astype(F32))
    sums = jnp.stack([jnp.sum(hidden, axis=1), jnp.sum(hidden * hidden, axis=1)])
    sums = sums + other_half(sums)
    row_mean = sums[0] / full_width
    row_var = sums[1] / full_width - row_mean * row_mean
    normed = (hidden - row_mean[:, None]) * lax.rsqrt(row_var + 1e-05)[:, None] * ln_gain + ln_bias
    return normed.astype(BF16)[None]


def shards(*arrays):
    tokens, w_qkv, random_blocks = arrays[0], arrays[1], arrays[5]
    ctx_count = lax.axis_size("ctx")
    picked = random_blocks.shape[1] * random_blocks.shape[2]
    if (
        lax.axis_size("heads") == 2
        and ctx_count == 4
        and picked >= ctx_count
        and tokens.shape[1] % (2 * BLOCK) == 0
        and w_qkv.shape[2] % LANES == 0
        and arrays[6].shape[1] // ctx_count <= 8
    ):
        return gathered(*arrays)
    return requested(*arrays)


def solution(mesh):
    in_specs = (
        P(("groups", "dp"), "ctx", "heads"),
        P(None, None, "heads"),
        P("heads", None),
        P("heads"),
        P("heads"),
        P(("groups", "dp"), "ctx", None),
        P(("groups", "dp"), None),
        P(("groups", "dp"), None, None),
        P(("groups", "dp"), None),
    )
    out_specs = P(("groups", "dp"), "ctx", "heads")
    return jax.shard_map(shards, mesh=mesh, in_specs=in_specs, out_specs=out_specs, check_vma=False)
```

```python
import functools
import jax
import jax.numpy as jnp
from jax import lax
from jax.experimental import pallas as pl
from jax.experimental.pallas import tpu as pltpu
from jax.sharding import PartitionSpec as P

HEAD = 64
BLOCK = 128


MASKED = -1e30


def extended(x, sides, width):
    for axis, dim in sides:
        size, length = (lax.axis_size(axis), x.shape[dim])
        up = [(i, (i + 1) % size) for i in range(size - 1)]
        down = [(j, i) for i, j in up]
        last = lax.slice_in_dim(x, length - width, length, axis=dim)
        first = lax.slice_in_dim(x, 0, width, axis=dim)
        before = lax.ppermute(last, axis, up)
        after = lax.ppermute(first, axis, down)
        x = jnp.concatenate([before, x, after], axis=dim)
    return x


def segment_ids(positions, bounds):
    return jnp.sum((positions[..., None] >= bounds).astype(jnp.int32), axis=-1)


def attend(queries, keys, values, allowed, head_count):
    group_count, query_len, all_width = queries.shape
    key_len = keys.shape[1]
    query_heads = queries.reshape(group_count, query_len, head_count, HEAD)
    key_heads = keys.reshape(group_count, key_len, head_count, HEAD)
    value_heads = values.reshape(group_count, key_len, head_count, HEAD)
    scores = jnp.einsum(
        "gqhe,gkhe->ghqk", query_heads, key_heads, preferred_element_type=jnp.float32
    ) * HEAD ** (-0.5)
    scores = jnp.where(allowed[:, None], scores, MASKED)
    maxima = jnp.max(scores, axis=-1, keepdims=True)
    weights = jnp.where(allowed[:, None], jnp.exp(scores - maxima), 0.0)
    totals = jnp.sum(weights, axis=-1)
    mixture = jnp.einsum(
        "ghqk,gkhe->gqhe",
        weights.astype(jnp.bfloat16),
        value_heads,
        preferred_element_type=jnp.float32,
    )
    mixture = mixture / jnp.transpose(totals, (0, 2, 1))[..., None]
    return mixture.reshape(group_count, query_len, all_width).astype(jnp.bfloat16)


def three_views(window_span, group_size, axis_pos):
    views = []
    for shift_index in range(3):
        piece = lax.slice_in_dim(
            window_span,
            shift_index * BLOCK,
            shift_index * BLOCK + group_size * BLOCK,
            axis=axis_pos,
        )
        new_shape = (
            window_span.shape[:axis_pos] + (group_size, BLOCK) + window_span.shape[axis_pos + 1 :]
        )
        views.append(piece.reshape(new_shape))
    return jnp.concatenate(views, axis=axis_pos + 1)


def requested(
    tokens, w_qkv, w_out, ln_gain, ln_bias, random_blocks, summary_pos, summary_blocks, pair_lengths
):
    tok_rows = tokens.shape[1]
    head_cols = tokens.shape[2]
    heads_here = head_cols // HEAD
    full_width = w_out.shape[1]
    ctx_count = lax.axis_size("ctx")
    ctx_index = lax.axis_index("ctx")
    block_count = tok_rows // BLOCK
    seq_total = tok_rows * ctx_count
    bounds = jnp.cumsum(pair_lengths[0])
    own_tokens = tokens[0]
    projected = jnp.einsum(
        "nc,kcd->knd",
        lax.all_gather(own_tokens, "heads", axis=1, tiled=True),
        w_qkv,
        preferred_element_type=jnp.float32,
    ).astype(jnp.bfloat16)
    queries = projected[0]
    own_kv = projected[1:3]
    rim_kv = extended(own_kv, (("ctx", 1),), BLOCK)
    query_pos = ctx_index * tok_rows + jnp.arange(tok_rows, dtype=jnp.int32)
    own_seg = segment_ids(query_pos, bounds)
    rim_pos = ctx_index * tok_rows - BLOCK + jnp.arange(tok_rows + 2 * BLOCK, dtype=jnp.int32)
    rim_ok = (rim_pos >= 0) & (rim_pos < seq_total)
    rim_seg = segment_ids(rim_pos, bounds)
    rand_count = random_blocks.shape[2]
    picked = random_blocks[0].reshape(-1)
    pick_count = picked.shape[0]
    capacity = max(2, -(-pick_count // ctx_count))
    owners = picked // block_count
    within = picked % block_count
    slot_order = jnp.arange(pick_count, dtype=jnp.int32)
    earlier = (owners[:, None] == owners[None, :]) & (slot_order[None, :] < slot_order[:, None])
    pick_rank = jnp.sum(earlier.astype(jnp.int32), axis=1)
    pick_slot = owners * capacity + pick_rank
    slot_table = (
        pick_slot[:, None] == jnp.arange(ctx_count * capacity, dtype=jnp.int32)[None, :]
    ).astype(jnp.int32)
    requests = jnp.sum(slot_table * within[:, None], axis=0).reshape(ctx_count, capacity)
    own_blocks = own_kv.reshape(2, block_count, BLOCK, head_cols).transpose(1, 0, 2, 3)
    reply = jnp.take(
        own_blocks, lax.all_to_all(requests, "ctx", split_axis=0, concat_axis=0, tiled=True), axis=0
    )
    fetched = lax.all_to_all(reply, "ctx", split_axis=0, concat_axis=0, tiled=True)
    flat_blocks = fetched.reshape(ctx_count * capacity, 2, BLOCK, head_cols)
    far_kv = jnp.take(flat_blocks, pick_slot, axis=0).reshape(
        block_count, rand_count, 2, BLOCK, head_cols
    )
    far_kv = far_kv.transpose(2, 0, 1, 3, 4).reshape(2, block_count, rand_count * BLOCK, head_cols)
    far_pos = (
        picked.reshape(block_count, rand_count)[:, :, None] * BLOCK
        + jnp.arange(BLOCK, dtype=jnp.int32)
    ).reshape(block_count, rand_count * BLOCK)
    far_seg = segment_ids(far_pos, bounds)
    group_size = min(4, block_count)
    group_steps = block_count // group_size

    def window_step(unused, step_index):
        near_kv = three_views(rim_kv, group_size, 1)
        near_ok = three_views(rim_ok, group_size, 0)
        near_seg = three_views(rim_seg, group_size, 0)
        key_set = jnp.concatenate([near_kv, far_kv], axis=2)
        key_seg = jnp.concatenate([near_seg, far_seg], axis=1)
        key_ok = jnp.concatenate([near_ok, jnp.ones(far_seg.shape, jnp.bool_)], axis=1)
        query_seg = own_seg.reshape(group_size, BLOCK)
        allowed = key_ok[:, None, :] & (key_seg[:, None, :] == query_seg[:, :, None])
        query_group = queries.reshape(group_size, BLOCK, head_cols)
        return (unused, attend(query_group, key_set[0], key_set[1], allowed, heads_here))

    _, window_out = lax.scan(window_step, 0, jnp.arange(group_steps, dtype=jnp.int32))
    attention = window_out.reshape(tok_rows, head_cols)
    summary_rows = summary_pos[0]
    summary_lists = summary_blocks[0]
    summaries = summary_rows.shape[0]
    per_device = summaries // ctx_count
    mine = (
        lax.dynamic_slice_in_dim(summary_rows, ctx_index * per_device, per_device, 0)
        - ctx_index * tok_rows
    )
    summary_query = jnp.take(queries, mine, axis=0)
    all_queries = lax.all_gather(summary_query, "ctx", axis=0, tiled=True)
    summary_seg = segment_ids(summary_rows, bounds)
    key_block = ctx_index * block_count + jnp.arange(block_count, dtype=jnp.int32)
    listed = jnp.any(summary_lists[:, :, None] == key_block[None, None, :], axis=1)
    key_heads = own_kv[0].reshape(tok_rows, heads_here, HEAD)
    value_heads = own_kv[1].reshape(tok_rows, heads_here, HEAD)
    summary_group = min(128, summaries)
    group_total = summaries // summary_group

    def group_scores():
        query_part = all_queries.reshape(summary_group, heads_here, HEAD)
        allowed = jnp.broadcast_to(listed[:, :, None], (summary_group, block_count, BLOCK)).reshape(
            summary_group, tok_rows
        )
        allowed = allowed & (own_seg[None, :] == summary_seg[:, None])
        scores = jnp.einsum(
            "qhe,khe->hqk", query_part, key_heads, preferred_element_type=jnp.float32
        ) * HEAD ** (-0.5)
        return (jnp.where(allowed[None], scores, MASKED), allowed)

    def weigh(scores, allowed, maxima):
        weights = jnp.where(allowed[None], jnp.exp(scores - maxima[:, :, None]), 0.0)
        totals = jnp.sum(weights, axis=-1)
        mixture = jnp.einsum(
            "hqk,khe->qhe",
            weights.astype(jnp.bfloat16),
            value_heads,
            preferred_element_type=jnp.float32,
        )
        return (totals.T, mixture.reshape(summary_group, head_cols))

    def max_step(unused, group_index):
        scores, allowed = group_scores()
        return (unused, jnp.max(scores, axis=-1).T)

    _, maxima_all = lax.scan(max_step, 0, jnp.arange(group_total, dtype=jnp.int32))
    maxima_all = lax.pmax(maxima_all.reshape(summaries, heads_here), "ctx")

    def sum_step(unused, group_index):
        scores, allowed = group_scores()
        maxima = maxima_all.T
        return (unused, weigh(scores, allowed, maxima))

    _, (totals_all, mixture_all) = lax.scan(sum_step, 0, jnp.arange(group_total, dtype=jnp.int32))
    totals_all = totals_all.reshape(summaries, heads_here)
    mixture_all = mixture_all.reshape(summaries, head_cols)
    totals_all, mixture_all = (
        lax.psum(totals_all.astype(jnp.bfloat16), "ctx").astype(jnp.float32),
        lax.psum(mixture_all.astype(jnp.bfloat16), "ctx").astype(jnp.float32),
    )
    own_totals = lax.dynamic_slice_in_dim(totals_all, ctx_index * per_device, per_device, 0)
    own_mixture = lax.dynamic_slice_in_dim(mixture_all, ctx_index * per_device, per_device, 0)
    summary_out = (own_mixture / jnp.repeat(own_totals, HEAD, axis=1)).astype(jnp.bfloat16)
    attention = attention.at[mine].set(summary_out)
    partial_value = jnp.dot(attention, w_out, preferred_element_type=jnp.float32)
    summed = lax.psum_scatter(
        partial_value.astype(jnp.bfloat16), "heads", scatter_dimension=1, tiled=True
    ).astype(jnp.float32)
    hidden = own_tokens.astype(jnp.float32) + summed
    row_sums = lax.psum((jnp.sum(hidden, axis=1), jnp.sum(hidden * hidden, axis=1)), "heads")
    row_mean = row_sums[0] / full_width
    row_var = row_sums[1] / full_width - row_mean * row_mean
    normed = (hidden - row_mean[:, None]) * lax.rsqrt(row_var + 1e-05)[:, None] * ln_gain + ln_bias
    return normed.astype(jnp.bfloat16)[None]


LANES = 128
PAIR = LANES // HEAD
VMEM_LIMIT = 14 * 1024 * 1024
F32 = jnp.float32
BF16 = jnp.bfloat16
NT = (((1,), (1,)), ((), ()))


def whole_block(shape):
    return pl.BlockSpec(shape, lambda *_: (0,) * len(shape))


def params(*semantics):
    return pltpu.CompilerParams(
        dimension_semantics=semantics or None, vmem_limit_bytes=VMEM_LIMIT
    )


def project_rows(side_ref, here_ref, there_ref, w_ref):
    half = here_ref.shape[1]
    low = pl.multiple_of(side_ref[0] * half, half)
    high = pl.multiple_of((1 - side_ref[0]) * half, half)
    product = jnp.dot(here_ref[...], w_ref[pl.ds(low, half), :], preferred_element_type=F32)
    product += jnp.dot(there_ref[...], w_ref[pl.ds(high, half), :], preferred_element_type=F32)
    return product.astype(BF16)


def pair_up(refs):
    return list(zip(refs[0::2], refs[1::2]))


def weights_kernel(w_hbm, w_q_ref, w_kv_ref, mark_ref, sem):
    mark_ref[...] = jnp.zeros(mark_ref.shape, F32)
    copies = [
        pltpu.make_async_copy(w_hbm.at[0], w_q_ref, sem.at[0]),
        pltpu.make_async_copy(w_hbm.at[pl.ds(1, 2)], w_kv_ref, sem.at[1]),
    ]
    for copy in copies:
        copy.start()
    for copy in copies:
        copy.wait()


def first_kernel(side_ref, here_ref, there_ref, w_q_ref, w_kv_ref, mark_ref, q_ref, kv_ref):
    q_ref[...] = project_rows(side_ref, here_ref, there_ref, w_q_ref)
    for j in range(2):
        kv_ref[j] = project_rows(side_ref, here_ref, there_ref, w_kv_ref.at[j])


def pieces_kernel(side_ref, w_kv_ref, *refs):
    count = len(refs) // 3
    for piece, kv_ref in zip(pair_up(refs[: 2 * count]), refs[2 * count :]):
        project_pieces(side_ref, [piece], w_kv_ref, kv_ref, 0)


def segments_of(position, bounds_ref, pair_count):
    segment = jnp.zeros(position.shape, jnp.int32)
    for pair in range(pair_count):
        segment += (position >= bounds_ref[pair]).astype(jnp.int32)
    return segment


def item_bias(query_seg, key_pos, bounds_ref, pair_count):
    lane = lax.broadcasted_iota(jnp.int32, (1, BLOCK), 1)
    key_seg = segments_of(key_pos + lane, bounds_ref, pair_count)
    key_seg = jnp.where(key_pos >= 0, key_seg, -1)
    return jnp.where(query_seg == key_seg, 0.0, MASKED)


def split_heads(pair_queries):
    lane = lax.broadcasted_iota(jnp.int32, pair_queries.shape, 1)
    scaled = pair_queries.astype(F32) * HEAD ** (-0.5)
    low = jnp.where(lane < HEAD, scaled, 0.0)
    high = jnp.where(lane >= HEAD, scaled, 0.0)
    return jnp.concatenate([low, high], axis=0).astype(BF16)


def join_heads(stacked):
    rows = stacked.shape[0] // PAIR
    lane = lax.broadcasted_iota(jnp.int32, (rows, LANES), 1)
    return jnp.where(lane < HEAD, stacked[:rows], stacked[rows:])


def spread_pair(low, high):
    lane = lax.broadcasted_iota(jnp.int32, (low.shape[0], LANES), 1)
    return jnp.where(lane < HEAD, low, high)


def summary_queries(rows_ref, q_ref, head_count):
    tok_rows, cols = q_ref.shape
    row = lax.broadcasted_iota(jnp.int32, (8, tok_rows), 0)
    col = lax.broadcasted_iota(jnp.int32, (8, tok_rows), 1)
    chosen = jnp.zeros((8, tok_rows), F32)
    for u in range(rows_ref.shape[0]):
        chosen = jnp.where((row == u) & (col == rows_ref[u]), 1.0, chosen)
    picked = jnp.dot(chosen.astype(BF16), q_ref[...], preferred_element_type=F32)
    picked = picked * HEAD ** (-0.5)
    lane = lax.broadcasted_iota(jnp.int32, (8, cols), 1)
    parts = [
        jnp.where((lane >= h * HEAD) & (lane < (h + 1) * HEAD), picked, 0.0)
        for h in range(head_count)
    ]
    return jnp.concatenate(parts, axis=0).astype(BF16)


def attend_blocks(
    first_block, block_total, off_ref, pos_ref, bounds_ref, base_ref, q_ref, kv_ref,
    acc_ref, top_ref, sum_ref, bias_ref, score_ref, items, pair_count, head_count,
):
    row = lax.broadcasted_iota(jnp.int32, (BLOCK, 1), 0)

    def block_step(step, carry):
        place = pl.ds(pl.multiple_of(step * BLOCK, BLOCK), BLOCK)
        first = pl.multiple_of((first_block + step) * BLOCK, BLOCK)
        query_seg = segments_of(base_ref[0] + first + row, bounds_ref, pair_count)
        offsets = []
        for item in range(items):
            at = (first_block + step) * items + item
            offsets.append(pl.multiple_of(off_ref[at], BLOCK))
            bias_ref[:, item * BLOCK : (item + 1) * BLOCK] = item_bias(
                query_seg, pos_ref[at], bounds_ref, pair_count
            )
        tops = []
        for pair in range(head_count // PAIR):
            cols = slice(pair * LANES, (pair + 1) * LANES)
            keys = jnp.concatenate([kv_ref[0, pl.ds(o, BLOCK), cols] for o in offsets], axis=0)
            scores = lax.dot_general(
                split_heads(q_ref[pl.ds(first, BLOCK), cols]), keys, NT, preferred_element_type=F32
            )
            for j in range(PAIR):
                rows = slice(j * BLOCK, (j + 1) * BLOCK)
                part = scores[rows] + bias_ref[...]
                score_ref[pair, rows] = part
                tops.append(jnp.max(part, axis=1, keepdims=True))
        for pair in range(head_count // PAIR):
            cols = slice(pair * LANES, (pair + 1) * LANES)
            values = jnp.concatenate([kv_ref[1, pl.ds(o, BLOCK), cols] for o in offsets], axis=0)
            values = jnp.concatenate([values, jnp.ones_like(values)], axis=1)
            peaks = tops[pair * PAIR : (pair + 1) * PAIR]
            weights = jnp.exp(score_ref[pair] - jnp.concatenate(peaks, axis=0)).astype(BF16)
            product = jnp.dot(weights, values, preferred_element_type=F32)
            acc_ref[place, cols] = join_heads(product[:, :LANES])
            sum_ref[place, cols] = join_heads(product[:, LANES:])
            top_ref[place, cols] = spread_pair(*peaks)
        return carry

    lax.fori_loop(0, block_total, block_step, 0)


def project_pieces(side_ref, pieces, w_ref, kv_ref, row):
    for here_ref, there_ref in pieces:
        rows = here_ref.shape[0]
        for j in range(2):
            kv_ref[j, row : row + rows] = project_rows(side_ref, here_ref, there_ref, w_ref.at[j])
        row += rows


def add_summary(queries, keys, values, bias, before, head_count):
    scores = lax.dot_general(queries, keys, NT, preferred_element_type=F32)
    scores = scores + jnp.concatenate([bias] * head_count, axis=0)
    top = jnp.max(scores, axis=1, keepdims=True)
    if before is not None:
        top = jnp.maximum(top, before[1])
    weights = jnp.exp(scores - top)
    total = jnp.sum(weights, axis=1, keepdims=True)
    mixture = jnp.dot(weights.astype(BF16), values, preferred_element_type=F32)
    if before is not None:
        fade = jnp.exp(before[1] - top)
        mixture = mixture + before[0] * fade
        total = total + before[2] * fade
    return mixture, top, total


def store_summary(state, sacc_ref, sml_ref):
    mixture, top, total = state
    sacc_ref[...] = mixture
    lane = lax.broadcasted_iota(jnp.int32, sml_ref.shape, 1)
    sml_ref[...] = jnp.where(lane == 0, top, total)


def load_summary(sacc_ref, sml_ref):
    return sacc_ref[...], sml_ref[:, 0:1], sml_ref[:, 1:2]


def early_kernel(
    off_ref, pos_ref, bounds_ref, base_ref, mine_ref, q_ref, sbias_ref, own_ref, *refs,
    items, pair_count, head_count,
):
    *held, acc_ref, top_ref, sum_ref, kv_ref, sacc_ref, sml_ref, squery_ref = refs[:-3]
    bias_ref, score_ref, sem = refs[-3:]
    copies = []
    row = 0
    for i, part in enumerate([own_ref] + held):
        rows = part.shape[1]
        copies.append(pltpu.make_async_copy(part, kv_ref.at[:, pl.ds(row, rows)], sem.at[i]))
        copies[-1].start()
        row += rows
    for copy in copies:
        copy.wait()
    attend_blocks(
        0, acc_ref.shape[0] // BLOCK, off_ref, pos_ref, bounds_ref, base_ref, q_ref, kv_ref,
        acc_ref, top_ref, sum_ref, bias_ref, score_ref, items, pair_count, head_count,
    )
    squery_ref[...] = summary_queries(mine_ref, q_ref, head_count)
    bias = sbias_ref[:, : kv_ref.shape[1]]
    state = add_summary(squery_ref[...], kv_ref[0], kv_ref[1], bias, None, head_count)
    store_summary(state, sacc_ref, sml_ref)


def item_part(q_ref, kv_ref, first, offset, bias, head_count):
    pairs = head_count // PAIR
    scores, tops = [], []
    for pair in range(pairs):
        cols = slice(pair * LANES, (pair + 1) * LANES)
        product = lax.dot_general(
            split_heads(q_ref[pl.ds(first, BLOCK), cols]),
            kv_ref[0, pl.ds(offset, BLOCK), cols],
            NT,
            preferred_element_type=F32,
        )
        product = product + jnp.concatenate([bias] * PAIR, axis=0)
        scores.append(product)
        tops.append(jnp.max(product, axis=1, keepdims=True))
    peaks, totals, mixtures = [], [], []
    for pair in range(pairs):
        cols = slice(pair * LANES, (pair + 1) * LANES)
        weights = jnp.exp(scores[pair] - tops[pair]).astype(BF16)
        values = kv_ref[1, pl.ds(offset, BLOCK), cols]
        values = jnp.concatenate([values, jnp.ones_like(values)], axis=1)
        product = jnp.dot(weights, values, preferred_element_type=F32)
        peaks.append(spread_pair(tops[pair][:BLOCK], tops[pair][BLOCK:]))
        mixtures.append(join_heads(product[:, :LANES]))
        totals.append(join_heads(product[:, LANES:]))
    return peaks, totals, mixtures


def add_items(
    tables, bounds_ref, base_ref, q_ref, kv_ref, state, items, group, pair_count, head_count
):
    valid_ref, block_ref, off_ref, pos_ref = tables
    peak_ref, total_ref, mix_ref = state
    row = lax.broadcasted_iota(jnp.int32, (BLOCK, 1), 0)

    def add_group(start):
        parts = []
        for item in range(start, min(start + group, items)):
            offset = pl.multiple_of(off_ref[item], BLOCK)
            first = pl.multiple_of(block_ref[item] * BLOCK, BLOCK)
            query_seg = segments_of(base_ref[0] + first + row, bounds_ref, pair_count)
            key_pos = jnp.where(valid_ref[item] == 1, pos_ref[item], -(2**30))
            bias = item_bias(query_seg, key_pos, bounds_ref, pair_count)
            parts.append((first, item_part(q_ref, kv_ref, first, offset, bias, head_count)))
        for first, (peaks, totals, mixtures) in parts:
            rows = pl.ds(first, BLOCK)
            for pair in range(head_count // PAIR):
                cols = slice(pair * LANES, (pair + 1) * LANES)
                before = peak_ref[rows, cols]
                top = jnp.maximum(before, peaks[pair])
                fade = jnp.exp(before - top)
                share = jnp.exp(peaks[pair] - top)
                peak_ref[rows, cols] = top
                total_ref[rows, cols] = total_ref[rows, cols] * fade + totals[pair] * share
                mix_ref[rows, cols] = mix_ref[rows, cols] * fade + mixtures[pair] * share

    for start in range(0, items, group):
        pl.when(valid_ref[start] == 1)(functools.partial(add_group, start))


def middle_kernel(
    valid_ref, block_ref, off_ref, pos_ref, bounds_ref, base_ref, side_ref,
    q_ref, w_kv_ref, sbias_ref, acc_in, top_in, sum_in, sacc_in, sml_in, squery_ref,
    here0_ref, there0_ref, here1_ref, there1_ref, w_out_hbm,
    acc_ref, top_ref, sum_ref, sacc_ref, sml_ref, w_out_ref,
    kv_ref, sem, *, items, group, pair_count, head_count, first_key,
):
    copy = pltpu.make_async_copy(w_out_hbm, w_out_ref, sem)
    copy.start()
    acc_ref[...] = acc_in[...]
    top_ref[...] = top_in[...]
    sum_ref[...] = sum_in[...]
    pieces = [(here0_ref, there0_ref), (here1_ref, there1_ref)]
    project_pieces(side_ref, pieces, w_kv_ref, kv_ref, 0)
    add_items(
        (valid_ref, block_ref, off_ref, pos_ref), bounds_ref, base_ref, q_ref, kv_ref,
        (top_ref, sum_ref, acc_ref), items, group, pair_count, head_count,
    )
    bias = sbias_ref[:, first_key : first_key + kv_ref.shape[1]]
    state = load_summary(sacc_in, sml_in)
    state = add_summary(squery_ref[...], kv_ref[0], kv_ref[1], bias, state, head_count)
    store_summary(state, sacc_ref, sml_ref)
    copy.wait()


def late_kernel(
    valid_ref, block_ref, off_ref, pos_ref, bounds_ref, base_ref, mine_ref, side_ref,
    q_ref, w_kv_ref, w_ref, sbias_ref, acc_ref, top_ref, sum_ref,
    sacc_ref, sml_ref, squery_ref, fresh_ref, here_ref, there_ref,
    own_ref, other_ref, kv_ref, mix_ref, peak_ref, total_ref,
    *, items, group, pair_count, head_count,
):
    tok_rows, cols_all = mix_ref.shape
    fresh_rows = fresh_ref.shape[1]
    mix_ref[...] = acc_ref[...]
    peak_ref[...] = top_ref[...]
    total_ref[...] = sum_ref[...]
    kv_ref[:, :fresh_rows] = fresh_ref[...]
    project_pieces(side_ref, [(here_ref, there_ref)], w_kv_ref, kv_ref, fresh_rows)
    add_items(
        (valid_ref, block_ref, off_ref, pos_ref), bounds_ref, base_ref, q_ref, kv_ref,
        (peak_ref, total_ref, mix_ref), items, group, pair_count, head_count,
    )

    bias = sbias_ref[:, -kv_ref.shape[1] :]
    state = load_summary(sacc_ref, sml_ref)
    state = add_summary(squery_ref[...], kv_ref[0], kv_ref[1], bias, state, head_count)
    mixture = state[0] / state[2]
    slane = lax.broadcasted_iota(jnp.int32, (8, cols_all), 1)
    summary = jnp.zeros((8, cols_all), F32)
    for h in range(head_count):
        summary = jnp.where(
            (slane >= h * HEAD) & (slane < (h + 1) * HEAD), mixture[h * 8 : (h + 1) * 8], summary
        )

    all_rows = lax.broadcasted_iota(jnp.int32, (tok_rows, 1), 0)
    columns = []
    for pair in range(head_count // PAIR):
        cols = slice(pair * LANES, (pair + 1) * LANES)
        part = mix_ref[:, cols] / total_ref[:, cols]
        for u in range(mine_ref.shape[0]):
            part = jnp.where(all_rows == mine_ref[u], summary[u : u + 1, cols], part)
        columns.append(part.astype(BF16))
    attention = jnp.concatenate(columns, axis=1)
    half = w_ref.shape[1] // 2
    low = pl.multiple_of(side_ref[0] * half, half)
    high = pl.multiple_of((1 - side_ref[0]) * half, half)
    other_ref[...] = jnp.dot(
        attention, w_ref[:, pl.ds(high, half)], preferred_element_type=F32
    ).astype(BF16)
    own_ref[...] = jnp.dot(
        attention, w_ref[:, pl.ds(low, half)], preferred_element_type=F32
    ).astype(BF16)


def gathered(
    tokens, w_qkv, w_out, ln_gain, ln_bias, random_blocks, summary_pos, summary_blocks, pair_lengths
):
    tok_rows, half = tokens.shape[1:]
    cols = w_qkv.shape[2]
    head_count = cols // HEAD
    full_width = w_out.shape[1]
    ctx_count = lax.axis_size("ctx")
    ctx_index = lax.axis_index("ctx")
    side = lax.axis_index("heads").astype(jnp.int32).reshape(1)
    block_count = tok_rows // BLOCK
    total_blocks = block_count * ctx_count
    pair_count = pair_lengths.shape[1]
    own_tokens = tokens[0]
    piece = tok_rows // 2
    piece_blocks = block_count // 2
    arrival = jnp.array([0, 1, 2, 4, 3, 5, 6, 7], jnp.int32)
    place_of = jnp.array([0, 1, 2, 4, 3, 5, 6, 7], jnp.int32)
    early_count, late_count, piece_count = 4, 6, 2 * ctx_count
    early_rows, late_rows = early_count * piece, (piece_count - late_count) * piece

    bounds = jnp.cumsum(pair_lengths[0]).astype(jnp.int32)
    base = (ctx_index * tok_rows).astype(jnp.int32).reshape(1)
    picks = random_blocks[0]
    rand_count = picks.shape[1]
    block_ids = ctx_index * block_count + jnp.arange(block_count, dtype=jnp.int32)
    window = block_ids[:, None] + jnp.arange(-1, 2, dtype=jnp.int32)[None, :]
    listed = jnp.concatenate([window, picks], axis=1)
    items = listed.shape[1]
    inside = (listed >= 0) & (listed < total_blocks)
    slot_of = (listed // block_count) ^ ctx_index
    within = listed % block_count
    number = slot_of * 2 + within // piece_blocks
    place = jnp.sum(
        jnp.where(number[..., None] == jnp.arange(piece_count), place_of, 0), axis=-1
    )
    row = place * piece + (within % piece_blocks) * BLOCK
    early = inside & (place < early_count)
    early_off = jnp.where(early, row, 0).reshape(-1)
    early_pos = jnp.where(early, listed * BLOCK, -(2**30)).reshape(-1)
    capacity = max(2, -(-block_count * rand_count // ctx_count))

    def item_list(first, last, count):
        held = (inside & (place >= first) & (place < last)).reshape(-1)
        rank = jnp.cumsum(held.astype(jnp.int32)) - 1
        chosen = held[None, :] & (rank[None, :] == jnp.arange(count, dtype=jnp.int32)[:, None])

        def compact(x):
            return jnp.sum(jnp.where(chosen, x.reshape(-1)[None, :], 0), axis=1).astype(jnp.int32)

        blocks = jnp.broadcast_to(jnp.arange(block_count, dtype=jnp.int32)[:, None], listed.shape)
        valid = jnp.any(chosen, axis=1).astype(jnp.int32)
        return valid, compact(blocks), compact(row - first * piece), compact(listed * BLOCK)

    middle_items, late_items = 2 * capacity + 1, capacity + 1
    middle_list = item_list(early_count, late_count, middle_items)
    late_list = item_list(late_count, piece_count, late_items)
    summaries = summary_pos.shape[1]
    per_device = summaries // ctx_count
    mine_pos = lax.dynamic_slice_in_dim(summary_pos[0], ctx_index * per_device, per_device, 0)
    mine_lists = lax.dynamic_slice_in_dim(summary_blocks[0], ctx_index * per_device, per_device, 0)
    mine = (mine_pos - ctx_index * tok_rows).astype(jnp.int32)
    piece_first = ((arrival // 2) ^ ctx_index) * block_count + (arrival % 2) * piece_blocks
    key_blocks = (piece_first[:, None] + jnp.arange(piece_blocks, dtype=jnp.int32)).reshape(-1)
    in_list = jnp.any(mine_lists[:, :, None] == key_blocks[None, None, :], axis=1)
    key_pos = (key_blocks[:, None] * BLOCK + jnp.arange(BLOCK, dtype=jnp.int32)).reshape(-1)
    seen = jnp.repeat(in_list, BLOCK, axis=1) & (
        segment_ids(key_pos, bounds)[None, :] == segment_ids(mine_pos, bounds)[:, None]
    )
    sbias = jnp.pad(jnp.where(seen, 0.0, MASKED), ((0, 8 - per_device), (0, 0)))
    tables = (early_off, early_pos, middle_list, late_list, bounds, mine, base, sbias, side)

    swap = [(0, 1), (1, 0)]

    def other_half(x):
        return lax.ppermute(x, "heads", swap)

    def from_slot(x, slot):
        return lax.ppermute(x, "ctx", [(i, i ^ slot) for i in range(ctx_count)])

    def array(*shape, dtype=F32):
        return jax.ShapeDtypeStruct(shape, dtype)

    def like(arrays):
        return [pltpu.VMEM(x.shape, x.dtype) for x in arrays]

    def whole_call(kernel, scalars, args, far_args, outs, far_outs, scratch, work, name, **sizes):
        far = pl.BlockSpec(memory_space=pltpu.HBM)
        near = pl.BlockSpec(memory_space=pltpu.VMEM)
        return pl.pallas_call(
            functools.partial(kernel, **sizes),
            in_specs=[pl.BlockSpec(memory_space=pltpu.SMEM)] * len(scalars)
            + [near] * len(args)
            + [far] * len(far_args),
            out_specs=[far] * len(far_outs) + [near] * len(outs),
            out_shape=far_outs + outs,
            scratch_shapes=scratch,
            compiler_params=params(),
            cost_estimate=pl.CostEstimate(
                flops=int(work * 1e9), bytes_accessed=int(work * 3.5e6), transcendentals=0
            ),
            name=name,
        )(*scalars, *args, *far_args)

    low, high = own_tokens[:piece], own_tokens[piece:]
    own_there = other_half(own_tokens)
    here2a = from_slot(low, 2)
    here1a = from_slot(low, 1)
    high, tables = lax.optimization_barrier((high, tables))
    early_off, early_pos, middle_list, late_list, bounds, mine, base, sbias, side = tables
    here2b = from_slot(high, 2)
    here1b = from_slot(high, 1)
    w_q, w_kv, mark = whole_call(
        weights_kernel,
        [],
        [],
        [w_qkv],
        [array(2 * half, cols, dtype=BF16), array(2, 2 * half, cols, dtype=BF16), array(8, LANES)],
        [],
        [pltpu.SemaphoreType.DMA((2,))],
        1,
        "near_weights",
    )
    here2a, mark = lax.optimization_barrier((here2a, mark))
    there1a, there2a = other_half(here1a), other_half(here2a)
    queries, own_kv = whole_call(
        first_kernel,
        [side],
        [own_tokens, own_there, w_q, w_kv, mark],
        [],
        [array(tok_rows, cols, dtype=BF16), array(2, tok_rows, cols, dtype=BF16)],
        [],
        [],
        2,
        "own_projections",
    )
    here2b, here1b, own_kv = lax.optimization_barrier((here2b, here1b, own_kv))
    here3b = from_slot(here2b, 1)
    there1b, there2b = other_half(here1b), other_half(here2b)
    piece_kv = array(2, piece, cols, dtype=BF16)
    kv1a, kv2a = whole_call(
        pieces_kernel,
        [side],
        [w_kv, here1a, there1a, here2a, there2a],
        [],
        [piece_kv, piece_kv],
        [],
        [],
        1,
        "piece_projections",
    )
    kv3a = from_slot(kv2a, 1)
    there3b = other_half(here3b)

    sizes = dict(pair_count=pair_count, head_count=head_count)
    state = [array(tok_rows, cols)] * 3
    srows = 8 * head_count
    summary_state = [array(srows, cols), array(srows, LANES)]
    *state, kv, sacc, sml, squery = whole_call(
        early_kernel,
        [early_off, early_pos, bounds, base, mine],
        [queries, sbias, own_kv, kv1a, kv2a],
        [],
        state
        + [array(2, early_rows, cols, dtype=BF16)]
        + summary_state
        + [array(srows, cols, dtype=BF16)],
        [],
        [
            pltpu.VMEM((BLOCK, items * BLOCK), F32),
            pltpu.VMEM((head_count // PAIR, PAIR * BLOCK, items * BLOCK), F32),
            pltpu.SemaphoreType.DMA((3,)),
        ],
        7,
        "early_attention",
        items=items,
        **sizes,
    )
    *state, sacc, sml, w_out_near = whole_call(
        middle_kernel,
        [*middle_list, bounds, base, side],
        [queries, w_kv, sbias, *state, sacc, sml, squery, here1b, there1b, here2b, there2b],
        [w_out],
        [array(tok_rows, cols)] * 3 + summary_state + [array(*w_out.shape, dtype=BF16)],
        [],
        [pltpu.VMEM((2, 2 * piece, cols), BF16), pltpu.SemaphoreType.DMA],
        5,
        "middle_attention",
        items=middle_items,
        group=4,
        first_key=early_rows,
        **sizes,
    )
    own_term, other_term = whole_call(
        late_kernel,
        [*late_list, bounds, base, mine, side],
        [queries, w_kv, w_out_near, sbias, *state, sacc, sml, squery, kv3a, here3b, there3b],
        [],
        [array(tok_rows, half, dtype=BF16)] * 2,
        [],
        [pltpu.VMEM((2, late_rows, cols), BF16)] + [pltpu.VMEM((tok_rows, cols), F32)] * 3,
        4,
        "late_attention",
        items=late_items,
        group=4,
        **sizes,
    )

    received = other_half(other_term)
    hidden = own_tokens.astype(F32) + (own_term.astype(F32) + received.astype(F32))
    sums = jnp.stack([jnp.sum(hidden, axis=1), jnp.sum(hidden * hidden, axis=1)])
    sums = sums + other_half(sums)
    row_mean = sums[0] / full_width
    row_var = sums[1] / full_width - row_mean * row_mean
    normed = (hidden - row_mean[:, None]) * lax.rsqrt(row_var + 1e-05)[:, None] * ln_gain + ln_bias
    return normed.astype(BF16)[None]


def shards(*arrays):
    tokens, w_qkv, random_blocks = arrays[0], arrays[1], arrays[5]
    ctx_count = lax.axis_size("ctx")
    picked = random_blocks.shape[1] * random_blocks.shape[2]
    if (
        lax.axis_size("heads") == 2
        and ctx_count == 4
        and picked >= ctx_count
        and tokens.shape[1] % (2 * BLOCK) == 0
        and w_qkv.shape[2] % LANES == 0
        and arrays[6].shape[1] // ctx_count <= 8
    ):
        return gathered(*arrays)
    return requested(*arrays)


def solution(mesh):
    in_specs = (
        P(("groups", "dp"), "ctx", "heads"),
        P(None, None, "heads"),
        P("heads", None),
        P("heads"),
        P("heads"),
        P(("groups", "dp"), "ctx", None),
        P(("groups", "dp"), None),
        P(("groups", "dp"), None, None),
        P(("groups", "dp"), None),
    )
    out_specs = P(("groups", "dp"), "ctx", "heads")
    return jax.shard_map(shards, mesh=mesh, in_specs=in_specs, out_specs=out_specs, check_vma=False)
```

```python
import functools
import jax
import jax.numpy as jnp
from jax import lax
from jax.experimental import pallas as pl
from jax.experimental.pallas import tpu as pltpu
from jax.sharding import PartitionSpec as P

HEAD = 64
BLOCK = 128


MASKED = -1e30


def extended(x, sides, width):
    for axis, dim in sides:
        size, length = (lax.axis_size(axis), x.shape[dim])
        up = [(i, (i + 1) % size) for i in range(size - 1)]
        down = [(j, i) for i, j in up]
        last = lax.slice_in_dim(x, length - width, length, axis=dim)
        first = lax.slice_in_dim(x, 0, width, axis=dim)
        before = lax.ppermute(last, axis, up)
        after = lax.ppermute(first, axis, down)
        x = jnp.concatenate([before, x, after], axis=dim)
    return x


def segment_ids(positions, bounds):
    return jnp.sum((positions[..., None] >= bounds).astype(jnp.int32), axis=-1)


def attend(queries, keys, values, allowed, head_count):
    group_count, query_len, all_width = queries.shape
    key_len = keys.shape[1]
    query_heads = queries.reshape(group_count, query_len, head_count, HEAD)
    key_heads = keys.reshape(group_count, key_len, head_count, HEAD)
    value_heads = values.reshape(group_count, key_len, head_count, HEAD)
    scores = jnp.einsum(
        "gqhe,gkhe->ghqk", query_heads, key_heads, preferred_element_type=jnp.float32
    ) * HEAD ** (-0.5)
    scores = jnp.where(allowed[:, None], scores, MASKED)
    maxima = jnp.max(scores, axis=-1, keepdims=True)
    weights = jnp.where(allowed[:, None], jnp.exp(scores - maxima), 0.0)
    totals = jnp.sum(weights, axis=-1)
    mixture = jnp.einsum(
        "ghqk,gkhe->gqhe",
        weights.astype(jnp.bfloat16),
        value_heads,
        preferred_element_type=jnp.float32,
    )
    mixture = mixture / jnp.transpose(totals, (0, 2, 1))[..., None]
    return mixture.reshape(group_count, query_len, all_width).astype(jnp.bfloat16)


def three_views(window_span, group_size, axis_pos):
    views = []
    for shift_index in range(3):
        piece = lax.slice_in_dim(
            window_span,
            shift_index * BLOCK,
            shift_index * BLOCK + group_size * BLOCK,
            axis=axis_pos,
        )
        new_shape = (
            window_span.shape[:axis_pos] + (group_size, BLOCK) + window_span.shape[axis_pos + 1 :]
        )
        views.append(piece.reshape(new_shape))
    return jnp.concatenate(views, axis=axis_pos + 1)


def requested(
    tokens, w_qkv, w_out, ln_gain, ln_bias, random_blocks, summary_pos, summary_blocks, pair_lengths
):
    tok_rows = tokens.shape[1]
    head_cols = tokens.shape[2]
    heads_here = head_cols // HEAD
    full_width = w_out.shape[1]
    ctx_count = lax.axis_size("ctx")
    ctx_index = lax.axis_index("ctx")
    block_count = tok_rows // BLOCK
    seq_total = tok_rows * ctx_count
    bounds = jnp.cumsum(pair_lengths[0])
    own_tokens = tokens[0]
    projected = jnp.einsum(
        "nc,kcd->knd",
        lax.all_gather(own_tokens, "heads", axis=1, tiled=True),
        w_qkv,
        preferred_element_type=jnp.float32,
    ).astype(jnp.bfloat16)
    queries = projected[0]
    own_kv = projected[1:3]
    rim_kv = extended(own_kv, (("ctx", 1),), BLOCK)
    query_pos = ctx_index * tok_rows + jnp.arange(tok_rows, dtype=jnp.int32)
    own_seg = segment_ids(query_pos, bounds)
    rim_pos = ctx_index * tok_rows - BLOCK + jnp.arange(tok_rows + 2 * BLOCK, dtype=jnp.int32)
    rim_ok = (rim_pos >= 0) & (rim_pos < seq_total)
    rim_seg = segment_ids(rim_pos, bounds)
    rand_count = random_blocks.shape[2]
    picked = random_blocks[0].reshape(-1)
    pick_count = picked.shape[0]
    capacity = max(2, -(-pick_count // ctx_count))
    owners = picked // block_count
    within = picked % block_count
    slot_order = jnp.arange(pick_count, dtype=jnp.int32)
    earlier = (owners[:, None] == owners[None, :]) & (slot_order[None, :] < slot_order[:, None])
    pick_rank = jnp.sum(earlier.astype(jnp.int32), axis=1)
    pick_slot = owners * capacity + pick_rank
    slot_table = (
        pick_slot[:, None] == jnp.arange(ctx_count * capacity, dtype=jnp.int32)[None, :]
    ).astype(jnp.int32)
    requests = jnp.sum(slot_table * within[:, None], axis=0).reshape(ctx_count, capacity)
    own_blocks = own_kv.reshape(2, block_count, BLOCK, head_cols).transpose(1, 0, 2, 3)
    reply = jnp.take(
        own_blocks, lax.all_to_all(requests, "ctx", split_axis=0, concat_axis=0, tiled=True), axis=0
    )
    fetched = lax.all_to_all(reply, "ctx", split_axis=0, concat_axis=0, tiled=True)
    flat_blocks = fetched.reshape(ctx_count * capacity, 2, BLOCK, head_cols)
    far_kv = jnp.take(flat_blocks, pick_slot, axis=0).reshape(
        block_count, rand_count, 2, BLOCK, head_cols
    )
    far_kv = far_kv.transpose(2, 0, 1, 3, 4).reshape(2, block_count, rand_count * BLOCK, head_cols)
    far_pos = (
        picked.reshape(block_count, rand_count)[:, :, None] * BLOCK
        + jnp.arange(BLOCK, dtype=jnp.int32)
    ).reshape(block_count, rand_count * BLOCK)
    far_seg = segment_ids(far_pos, bounds)
    group_size = min(4, block_count)
    group_steps = block_count // group_size

    def window_step(unused, step_index):
        near_kv = three_views(rim_kv, group_size, 1)
        near_ok = three_views(rim_ok, group_size, 0)
        near_seg = three_views(rim_seg, group_size, 0)
        key_set = jnp.concatenate([near_kv, far_kv], axis=2)
        key_seg = jnp.concatenate([near_seg, far_seg], axis=1)
        key_ok = jnp.concatenate([near_ok, jnp.ones(far_seg.shape, jnp.bool_)], axis=1)
        query_seg = own_seg.reshape(group_size, BLOCK)
        allowed = key_ok[:, None, :] & (key_seg[:, None, :] == query_seg[:, :, None])
        query_group = queries.reshape(group_size, BLOCK, head_cols)
        return (unused, attend(query_group, key_set[0], key_set[1], allowed, heads_here))

    _, window_out = lax.scan(window_step, 0, jnp.arange(group_steps, dtype=jnp.int32))
    attention = window_out.reshape(tok_rows, head_cols)
    summary_rows = summary_pos[0]
    summary_lists = summary_blocks[0]
    summaries = summary_rows.shape[0]
    per_device = summaries // ctx_count
    mine = (
        lax.dynamic_slice_in_dim(summary_rows, ctx_index * per_device, per_device, 0)
        - ctx_index * tok_rows
    )
    summary_query = jnp.take(queries, mine, axis=0)
    all_queries = lax.all_gather(summary_query, "ctx", axis=0, tiled=True)
    summary_seg = segment_ids(summary_rows, bounds)
    key_block = ctx_index * block_count + jnp.arange(block_count, dtype=jnp.int32)
    listed = jnp.any(summary_lists[:, :, None] == key_block[None, None, :], axis=1)
    key_heads = own_kv[0].reshape(tok_rows, heads_here, HEAD)
    value_heads = own_kv[1].reshape(tok_rows, heads_here, HEAD)
    summary_group = min(128, summaries)
    group_total = summaries // summary_group

    def group_scores():
        query_part = all_queries.reshape(summary_group, heads_here, HEAD)
        allowed = jnp.broadcast_to(listed[:, :, None], (summary_group, block_count, BLOCK)).reshape(
            summary_group, tok_rows
        )
        allowed = allowed & (own_seg[None, :] == summary_seg[:, None])
        scores = jnp.einsum(
            "qhe,khe->hqk", query_part, key_heads, preferred_element_type=jnp.float32
        ) * HEAD ** (-0.5)
        return (jnp.where(allowed[None], scores, MASKED), allowed)

    def weigh(scores, allowed, maxima):
        weights = jnp.where(allowed[None], jnp.exp(scores - maxima[:, :, None]), 0.0)
        totals = jnp.sum(weights, axis=-1)
        mixture = jnp.einsum(
            "hqk,khe->qhe",
            weights.astype(jnp.bfloat16),
            value_heads,
            preferred_element_type=jnp.float32,
        )
        return (totals.T, mixture.reshape(summary_group, head_cols))

    def max_step(unused, group_index):
        scores, allowed = group_scores()
        return (unused, jnp.max(scores, axis=-1).T)

    _, maxima_all = lax.scan(max_step, 0, jnp.arange(group_total, dtype=jnp.int32))
    maxima_all = lax.pmax(maxima_all.reshape(summaries, heads_here), "ctx")

    def sum_step(unused, group_index):
        scores, allowed = group_scores()
        maxima = maxima_all.T
        return (unused, weigh(scores, allowed, maxima))

    _, (totals_all, mixture_all) = lax.scan(sum_step, 0, jnp.arange(group_total, dtype=jnp.int32))
    totals_all = totals_all.reshape(summaries, heads_here)
    mixture_all = mixture_all.reshape(summaries, head_cols)
    totals_all, mixture_all = (
        lax.psum(totals_all.astype(jnp.bfloat16), "ctx").astype(jnp.float32),
        lax.psum(mixture_all.astype(jnp.bfloat16), "ctx").astype(jnp.float32),
    )
    own_totals = lax.dynamic_slice_in_dim(totals_all, ctx_index * per_device, per_device, 0)
    own_mixture = lax.dynamic_slice_in_dim(mixture_all, ctx_index * per_device, per_device, 0)
    summary_out = (own_mixture / jnp.repeat(own_totals, HEAD, axis=1)).astype(jnp.bfloat16)
    attention = attention.at[mine].set(summary_out)
    partial_value = jnp.dot(attention, w_out, preferred_element_type=jnp.float32)
    summed = lax.psum_scatter(
        partial_value.astype(jnp.bfloat16), "heads", scatter_dimension=1, tiled=True
    ).astype(jnp.float32)
    hidden = own_tokens.astype(jnp.float32) + summed
    row_sums = lax.psum((jnp.sum(hidden, axis=1), jnp.sum(hidden * hidden, axis=1)), "heads")
    row_mean = row_sums[0] / full_width
    row_var = row_sums[1] / full_width - row_mean * row_mean
    normed = (hidden - row_mean[:, None]) * lax.rsqrt(row_var + 1e-05)[:, None] * ln_gain + ln_bias
    return normed.astype(jnp.bfloat16)[None]


LANES = 128
PAIR = LANES // HEAD
VMEM_LIMIT = 14 * 1024 * 1024
F32 = jnp.float32
BF16 = jnp.bfloat16
NT = (((1,), (1,)), ((), ()))


def whole_block(shape):
    return pl.BlockSpec(shape, lambda *_: (0,) * len(shape))


def params(*semantics):
    return pltpu.CompilerParams(
        dimension_semantics=semantics or None, vmem_limit_bytes=VMEM_LIMIT
    )


def project_rows(side_ref, here_ref, there_ref, w_ref):
    half = here_ref.shape[1]
    low = pl.multiple_of(side_ref[0] * half, half)
    high = pl.multiple_of((1 - side_ref[0]) * half, half)
    product = jnp.dot(here_ref[...], w_ref[pl.ds(low, half), :], preferred_element_type=F32)
    product += jnp.dot(there_ref[...], w_ref[pl.ds(high, half), :], preferred_element_type=F32)
    return product.astype(BF16)


def pair_up(refs):
    return list(zip(refs[0::2], refs[1::2]))


def weights_kernel(w_hbm, w_q_ref, w_kv_ref, mark_ref, sem):
    mark_ref[...] = jnp.zeros(mark_ref.shape, F32)
    copies = [
        pltpu.make_async_copy(w_hbm.at[0], w_q_ref, sem.at[0]),
        pltpu.make_async_copy(w_hbm.at[pl.ds(1, 2)], w_kv_ref, sem.at[1]),
    ]
    for copy in copies:
        copy.start()
    for copy in copies:
        copy.wait()


def first_kernel(side_ref, here_ref, there_ref, w_q_ref, w_kv_ref, mark_ref, q_ref, kv_ref):
    q_ref[...] = project_rows(side_ref, here_ref, there_ref, w_q_ref)
    for j in range(2):
        kv_ref[j] = project_rows(side_ref, here_ref, there_ref, w_kv_ref.at[j])


def pieces_kernel(side_ref, w_kv_ref, *refs):
    count = len(refs) // 3
    for piece, kv_ref in zip(pair_up(refs[: 2 * count]), refs[2 * count :]):
        project_pieces(side_ref, [piece], w_kv_ref, kv_ref, 0)


def segments_of(position, bounds_ref, pair_count):
    segment = jnp.zeros(position.shape, jnp.int32)
    for pair in range(pair_count):
        segment += (position >= bounds_ref[pair]).astype(jnp.int32)
    return segment


def item_bias(query_seg, key_pos, bounds_ref, pair_count):
    lane = lax.broadcasted_iota(jnp.int32, (1, BLOCK), 1)
    key_seg = segments_of(key_pos + lane, bounds_ref, pair_count)
    key_seg = jnp.where(key_pos >= 0, key_seg, -1)
    return jnp.where(query_seg == key_seg, 0.0, MASKED)


def split_heads(pair_queries):
    lane = lax.broadcasted_iota(jnp.int32, pair_queries.shape, 1)
    scaled = pair_queries.astype(F32) * HEAD ** (-0.5)
    low = jnp.where(lane < HEAD, scaled, 0.0)
    high = jnp.where(lane >= HEAD, scaled, 0.0)
    return jnp.concatenate([low, high], axis=0).astype(BF16)


def join_heads(stacked):
    rows = stacked.shape[0] // PAIR
    lane = lax.broadcasted_iota(jnp.int32, (rows, LANES), 1)
    return jnp.where(lane < HEAD, stacked[:rows], stacked[rows:])


def spread_pair(low, high):
    lane = lax.broadcasted_iota(jnp.int32, (low.shape[0], LANES), 1)
    return jnp.where(lane < HEAD, low, high)


def summary_queries(rows_ref, q_ref, head_count):
    tok_rows, cols = q_ref.shape
    row = lax.broadcasted_iota(jnp.int32, (8, tok_rows), 0)
    col = lax.broadcasted_iota(jnp.int32, (8, tok_rows), 1)
    chosen = jnp.zeros((8, tok_rows), F32)
    for u in range(rows_ref.shape[0]):
        chosen = jnp.where((row == u) & (col == rows_ref[u]), 1.0, chosen)
    picked = jnp.dot(chosen.astype(BF16), q_ref[...], preferred_element_type=F32)
    picked = picked * HEAD ** (-0.5)
    lane = lax.broadcasted_iota(jnp.int32, (8, cols), 1)
    parts = [
        jnp.where((lane >= h * HEAD) & (lane < (h + 1) * HEAD), picked, 0.0)
        for h in range(head_count)
    ]
    return jnp.concatenate(parts, axis=0).astype(BF16)


def attend_blocks(
    first_block, block_total, off_ref, pos_ref, bounds_ref, base_ref, q_ref, kv_ref,
    acc_ref, top_ref, sum_ref, bias_ref, score_ref, items, pair_count, head_count,
):
    row = lax.broadcasted_iota(jnp.int32, (BLOCK, 1), 0)

    def block_step(step, carry):
        place = pl.ds(pl.multiple_of(step * BLOCK, BLOCK), BLOCK)
        first = pl.multiple_of((first_block + step) * BLOCK, BLOCK)
        query_seg = segments_of(base_ref[0] + first + row, bounds_ref, pair_count)
        offsets = []
        for item in range(items):
            at = (first_block + step) * items + item
            offsets.append(pl.multiple_of(off_ref[at], BLOCK))
            bias_ref[:, item * BLOCK : (item + 1) * BLOCK] = item_bias(
                query_seg, pos_ref[at], bounds_ref, pair_count
            )
        tops = []
        for pair in range(head_count // PAIR):
            cols = slice(pair * LANES, (pair + 1) * LANES)
            keys = jnp.concatenate([kv_ref[0, pl.ds(o, BLOCK), cols] for o in offsets], axis=0)
            scores = lax.dot_general(
                split_heads(q_ref[pl.ds(first, BLOCK), cols]), keys, NT, preferred_element_type=F32
            )
            for j in range(PAIR):
                rows = slice(j * BLOCK, (j + 1) * BLOCK)
                part = scores[rows] + bias_ref[...]
                score_ref[pair, rows] = part
                tops.append(jnp.max(part, axis=1, keepdims=True))
        for pair in range(head_count // PAIR):
            cols = slice(pair * LANES, (pair + 1) * LANES)
            values = jnp.concatenate([kv_ref[1, pl.ds(o, BLOCK), cols] for o in offsets], axis=0)
            values = jnp.concatenate([values, jnp.ones_like(values)], axis=1)
            peaks = tops[pair * PAIR : (pair + 1) * PAIR]
            weights = jnp.exp(score_ref[pair] - jnp.concatenate(peaks, axis=0)).astype(BF16)
            product = jnp.dot(weights, values, preferred_element_type=F32)
            acc_ref[place, cols] = join_heads(product[:, :LANES])
            sum_ref[place, cols] = join_heads(product[:, LANES:])
            top_ref[place, cols] = spread_pair(*peaks)
        return carry

    lax.fori_loop(0, block_total, block_step, 0)


def project_pieces(side_ref, pieces, w_ref, kv_ref, row):
    for here_ref, there_ref in pieces:
        rows = here_ref.shape[0]
        for j in range(2):
            kv_ref[j, row : row + rows] = project_rows(side_ref, here_ref, there_ref, w_ref.at[j])
        row += rows


def add_summary(queries, keys, values, bias, before, head_count):
    scores = lax.dot_general(queries, keys, NT, preferred_element_type=F32)
    scores = scores + jnp.concatenate([bias] * head_count, axis=0)
    top = jnp.max(scores, axis=1, keepdims=True)
    if before is not None:
        top = jnp.maximum(top, before[1])
    weights = jnp.exp(scores - top)
    total = jnp.sum(weights, axis=1, keepdims=True)
    mixture = jnp.dot(weights.astype(BF16), values, preferred_element_type=F32)
    if before is not None:
        fade = jnp.exp(before[1] - top)
        mixture = mixture + before[0] * fade
        total = total + before[2] * fade
    return mixture, top, total


def store_summary(state, sacc_ref, sml_ref):
    mixture, top, total = state
    sacc_ref[...] = mixture
    lane = lax.broadcasted_iota(jnp.int32, sml_ref.shape, 1)
    sml_ref[...] = jnp.where(lane == 0, top, total)


def load_summary(sacc_ref, sml_ref):
    return sacc_ref[...], sml_ref[:, 0:1], sml_ref[:, 1:2]


def early_kernel(
    off_ref, pos_ref, bounds_ref, base_ref, mine_ref, q_ref, sbias_ref, own_ref, *refs,
    items, pair_count, head_count,
):
    *held, acc_ref, top_ref, sum_ref, kv_ref, sacc_ref, sml_ref, squery_ref = refs[:-3]
    bias_ref, score_ref, sem = refs[-3:]
    copies = []
    row = 0
    for i, part in enumerate([own_ref] + held):
        rows = part.shape[1]
        copies.append(pltpu.make_async_copy(part, kv_ref.at[:, pl.ds(row, rows)], sem.at[i]))
        copies[-1].start()
        row += rows
    for copy in copies:
        copy.wait()
    attend_blocks(
        0, acc_ref.shape[0] // BLOCK, off_ref, pos_ref, bounds_ref, base_ref, q_ref, kv_ref,
        acc_ref, top_ref, sum_ref, bias_ref, score_ref, items, pair_count, head_count,
    )
    squery_ref[...] = summary_queries(mine_ref, q_ref, head_count)
    bias = sbias_ref[:, : kv_ref.shape[1]]
    state = add_summary(squery_ref[...], kv_ref[0], kv_ref[1], bias, None, head_count)
    store_summary(state, sacc_ref, sml_ref)


def item_part(q_ref, kv_ref, first, offset, bias, head_count):
    pairs = head_count // PAIR
    scores, tops = [], []
    for pair in range(pairs):
        cols = slice(pair * LANES, (pair + 1) * LANES)
        product = lax.dot_general(
            split_heads(q_ref[pl.ds(first, BLOCK), cols]),
            kv_ref[0, pl.ds(offset, BLOCK), cols],
            NT,
            preferred_element_type=F32,
        )
        product = product + jnp.concatenate([bias] * PAIR, axis=0)
        scores.append(product)
        tops.append(jnp.max(product, axis=1, keepdims=True))
    peaks, totals, mixtures = [], [], []
    for pair in range(pairs):
        cols = slice(pair * LANES, (pair + 1) * LANES)
        weights = jnp.exp(scores[pair] - tops[pair]).astype(BF16)
        values = kv_ref[1, pl.ds(offset, BLOCK), cols]
        values = jnp.concatenate([values, jnp.ones_like(values)], axis=1)
        product = jnp.dot(weights, values, preferred_element_type=F32)
        peaks.append(spread_pair(tops[pair][:BLOCK], tops[pair][BLOCK:]))
        mixtures.append(join_heads(product[:, :LANES]))
        totals.append(join_heads(product[:, LANES:]))
    return peaks, totals, mixtures


def add_items(
    tables, bounds_ref, base_ref, q_ref, kv_ref, state, items, group, pair_count, head_count
):
    valid_ref, block_ref, off_ref, pos_ref = tables
    peak_ref, total_ref, mix_ref = state
    row = lax.broadcasted_iota(jnp.int32, (BLOCK, 1), 0)

    def add_group(start):
        parts = []
        for item in range(start, min(start + group, items)):
            offset = pl.multiple_of(off_ref[item], BLOCK)
            first = pl.multiple_of(block_ref[item] * BLOCK, BLOCK)
            query_seg = segments_of(base_ref[0] + first + row, bounds_ref, pair_count)
            key_pos = jnp.where(valid_ref[item] == 1, pos_ref[item], -(2**30))
            bias = item_bias(query_seg, key_pos, bounds_ref, pair_count)
            parts.append((first, item_part(q_ref, kv_ref, first, offset, bias, head_count)))
        for first, (peaks, totals, mixtures) in parts:
            rows = pl.ds(first, BLOCK)
            for pair in range(head_count // PAIR):
                cols = slice(pair * LANES, (pair + 1) * LANES)
                before = peak_ref[rows, cols]
                top = jnp.maximum(before, peaks[pair])
                fade = jnp.exp(before - top)
                share = jnp.exp(peaks[pair] - top)
                peak_ref[rows, cols] = top
                total_ref[rows, cols] = total_ref[rows, cols] * fade + totals[pair] * share
                mix_ref[rows, cols] = mix_ref[rows, cols] * fade + mixtures[pair] * share

    for start in range(0, items, group):
        pl.when(valid_ref[start] == 1)(functools.partial(add_group, start))


def middle_kernel(
    valid_ref, block_ref, off_ref, pos_ref, bounds_ref, base_ref, side_ref,
    q_ref, w_kv_ref, sbias_ref, acc_in, top_in, sum_in, sacc_in, sml_in, squery_ref,
    here0_ref, there0_ref, here1_ref, there1_ref, w_out_hbm,
    acc_ref, top_ref, sum_ref, sacc_ref, sml_ref, w_out_ref,
    kv_ref, sem, *, items, group, pair_count, head_count, first_key,
):
    copy = pltpu.make_async_copy(w_out_hbm, w_out_ref, sem)
    copy.start()
    pieces = [(here0_ref, there0_ref), (here1_ref, there1_ref)]
    project_pieces(side_ref, pieces, w_kv_ref, kv_ref, 0)
    add_items(
        (valid_ref, block_ref, off_ref, pos_ref), bounds_ref, base_ref, q_ref, kv_ref,
        (top_ref, sum_ref, acc_ref), items, group, pair_count, head_count,
    )
    bias = sbias_ref[:, first_key : first_key + kv_ref.shape[1]]
    state = load_summary(sacc_in, sml_in)
    state = add_summary(squery_ref[...], kv_ref[0], kv_ref[1], bias, state, head_count)
    store_summary(state, sacc_ref, sml_ref)
    copy.wait()


def late_kernel(
    valid_ref, block_ref, off_ref, pos_ref, bounds_ref, base_ref, mine_ref, side_ref,
    q_ref, w_kv_ref, w_ref, sbias_ref, acc_ref, top_ref, sum_ref,
    sacc_ref, sml_ref, squery_ref, fresh_ref, here_ref, there_ref,
    own_ref, other_ref, mix_ref, peak_ref, total_ref, kv_ref,
    *, items, group, pair_count, head_count,
):
    tok_rows, cols_all = mix_ref.shape
    fresh_rows = fresh_ref.shape[1]
    kv_ref[:, :fresh_rows] = fresh_ref[...]
    project_pieces(side_ref, [(here_ref, there_ref)], w_kv_ref, kv_ref, fresh_rows)
    add_items(
        (valid_ref, block_ref, off_ref, pos_ref), bounds_ref, base_ref, q_ref, kv_ref,
        (peak_ref, total_ref, mix_ref), items, group, pair_count, head_count,
    )

    bias = sbias_ref[:, -kv_ref.shape[1] :]
    state = load_summary(sacc_ref, sml_ref)
    state = add_summary(squery_ref[...], kv_ref[0], kv_ref[1], bias, state, head_count)
    mixture = state[0] / state[2]
    slane = lax.broadcasted_iota(jnp.int32, (8, cols_all), 1)
    summary = jnp.zeros((8, cols_all), F32)
    for h in range(head_count):
        summary = jnp.where(
            (slane >= h * HEAD) & (slane < (h + 1) * HEAD), mixture[h * 8 : (h + 1) * 8], summary
        )

    all_rows = lax.broadcasted_iota(jnp.int32, (tok_rows, 1), 0)
    columns = []
    for pair in range(head_count // PAIR):
        cols = slice(pair * LANES, (pair + 1) * LANES)
        part = mix_ref[:, cols] / total_ref[:, cols]
        for u in range(mine_ref.shape[0]):
            part = jnp.where(all_rows == mine_ref[u], summary[u : u + 1, cols], part)
        columns.append(part.astype(BF16))
    attention = jnp.concatenate(columns, axis=1)
    half = w_ref.shape[1] // 2
    low = pl.multiple_of(side_ref[0] * half, half)
    high = pl.multiple_of((1 - side_ref[0]) * half, half)
    other_ref[...] = jnp.dot(
        attention, w_ref[:, pl.ds(high, half)], preferred_element_type=F32
    ).astype(BF16)
    own_ref[...] = jnp.dot(
        attention, w_ref[:, pl.ds(low, half)], preferred_element_type=F32
    ).astype(BF16)


def running_sum(values):
    order = jnp.arange(values.shape[0], dtype=jnp.int32)
    return jnp.sum(jnp.where(order[None, :] <= order[:, None], values[None, :], 0), axis=1)


def gathered(
    tokens, w_qkv, w_out, ln_gain, ln_bias, random_blocks, summary_pos, summary_blocks, pair_lengths
):
    tok_rows, half = tokens.shape[1:]
    cols = w_qkv.shape[2]
    head_count = cols // HEAD
    full_width = w_out.shape[1]
    ctx_count = lax.axis_size("ctx")
    ctx_index = lax.axis_index("ctx")
    side = lax.axis_index("heads").astype(jnp.int32).reshape(1)
    block_count = tok_rows // BLOCK
    total_blocks = block_count * ctx_count
    pair_count = pair_lengths.shape[1]
    own_tokens = tokens[0]
    piece = tok_rows // 2
    piece_blocks = block_count // 2
    arrival = jnp.array([0, 1, 2, 4, 3, 5, 6, 7], jnp.int32)
    place_of = jnp.array([0, 1, 2, 4, 3, 5, 6, 7], jnp.int32)
    early_count, late_count, piece_count = 4, 6, 2 * ctx_count
    early_rows, late_rows = early_count * piece, (piece_count - late_count) * piece

    bounds = running_sum(pair_lengths[0])
    base = (ctx_index * tok_rows).astype(jnp.int32).reshape(1)
    picks = random_blocks[0]
    rand_count = picks.shape[1]
    block_ids = ctx_index * block_count + jnp.arange(block_count, dtype=jnp.int32)
    window = block_ids[:, None] + jnp.arange(-1, 2, dtype=jnp.int32)[None, :]
    listed = jnp.concatenate([window, picks], axis=1)
    items = listed.shape[1]
    inside = (listed >= 0) & (listed < total_blocks)
    slot_of = (listed // block_count) ^ ctx_index
    within = listed % block_count
    number = slot_of * 2 + within // piece_blocks
    place = jnp.sum(
        jnp.where(number[..., None] == jnp.arange(piece_count), place_of, 0), axis=-1
    )
    row = place * piece + (within % piece_blocks) * BLOCK
    early = inside & (place < early_count)
    early_off = jnp.where(early, row, 0).reshape(-1)
    early_pos = jnp.where(early, listed * BLOCK, -(2**30)).reshape(-1)
    capacity = max(2, -(-block_count * rand_count // ctx_count))

    def item_list(first, last, count):
        held = (inside & (place >= first) & (place < last)).reshape(-1)
        rank = running_sum(held.astype(jnp.int32)) - 1
        chosen = held[None, :] & (rank[None, :] == jnp.arange(count, dtype=jnp.int32)[:, None])

        def compact(x):
            return jnp.sum(jnp.where(chosen, x.reshape(-1)[None, :], 0), axis=1).astype(jnp.int32)

        blocks = jnp.broadcast_to(jnp.arange(block_count, dtype=jnp.int32)[:, None], listed.shape)
        valid = jnp.any(chosen, axis=1).astype(jnp.int32)
        return valid, compact(blocks), compact(row - first * piece), compact(listed * BLOCK)

    middle_items, late_items = 2 * capacity + 1, capacity + 1
    middle_list = item_list(early_count, late_count, middle_items)
    late_list = item_list(late_count, piece_count, late_items)
    summaries = summary_pos.shape[1]
    per_device = summaries // ctx_count
    mine_pos = lax.dynamic_slice_in_dim(summary_pos[0], ctx_index * per_device, per_device, 0)
    mine_lists = lax.dynamic_slice_in_dim(summary_blocks[0], ctx_index * per_device, per_device, 0)
    mine = (mine_pos - ctx_index * tok_rows).astype(jnp.int32)
    piece_first = ((arrival // 2) ^ ctx_index) * block_count + (arrival % 2) * piece_blocks
    key_blocks = (piece_first[:, None] + jnp.arange(piece_blocks, dtype=jnp.int32)).reshape(-1)
    in_list = jnp.any(mine_lists[:, :, None] == key_blocks[None, None, :], axis=1)
    key_pos = (key_blocks[:, None] * BLOCK + jnp.arange(BLOCK, dtype=jnp.int32)).reshape(-1)
    seen = jnp.repeat(in_list, BLOCK, axis=1) & (
        segment_ids(key_pos, bounds)[None, :] == segment_ids(mine_pos, bounds)[:, None]
    )
    sbias = jnp.pad(jnp.where(seen, 0.0, MASKED), ((0, 8 - per_device), (0, 0)))
    tables = (early_off, early_pos, middle_list, late_list, bounds, mine, base, sbias, side)

    swap = [(0, 1), (1, 0)]

    def other_half(x):
        return lax.ppermute(x, "heads", swap)

    def from_slot(x, slot):
        return lax.ppermute(x, "ctx", [(i, i ^ slot) for i in range(ctx_count)])

    def array(*shape, dtype=F32):
        return jax.ShapeDtypeStruct(shape, dtype)

    def like(arrays):
        return [pltpu.VMEM(x.shape, x.dtype) for x in arrays]

    def whole_call(kernel, scalars, args, far_args, outs, far_outs, scratch, work, name, aliases=None, **sizes):
        far = pl.BlockSpec(memory_space=pltpu.HBM)
        near = pl.BlockSpec(memory_space=pltpu.VMEM)
        return pl.pallas_call(
            functools.partial(kernel, **sizes),
            in_specs=[pl.BlockSpec(memory_space=pltpu.SMEM)] * len(scalars)
            + [near] * len(args)
            + [far] * len(far_args),
            out_specs=[far] * len(far_outs) + [near] * len(outs),
            out_shape=far_outs + outs,
            scratch_shapes=scratch,
            input_output_aliases=aliases or {},
            compiler_params=params(),
            cost_estimate=pl.CostEstimate(
                flops=int(work * 1e9), bytes_accessed=int(work * 3.5e6), transcendentals=0
            ),
            name=name,
        )(*scalars, *args, *far_args)

    low, high = own_tokens[:piece], own_tokens[piece:]
    own_there = other_half(own_tokens)
    here2a = from_slot(low, 2)
    here1a = from_slot(low, 1)
    high, tables = lax.optimization_barrier((high, tables))
    early_off, early_pos, middle_list, late_list, bounds, mine, base, sbias, side = tables
    here2b = from_slot(high, 2)
    here1b = from_slot(high, 1)
    w_q, w_kv, mark = whole_call(
        weights_kernel,
        [],
        [],
        [w_qkv],
        [array(2 * half, cols, dtype=BF16), array(2, 2 * half, cols, dtype=BF16), array(8, LANES)],
        [],
        [pltpu.SemaphoreType.DMA((2,))],
        1,
        "near_weights",
    )
    here2a, mark = lax.optimization_barrier((here2a, mark))
    there1a, there2a = other_half(here1a), other_half(here2a)
    queries, own_kv = whole_call(
        first_kernel,
        [side],
        [own_tokens, own_there, w_q, w_kv, mark],
        [],
        [array(tok_rows, cols, dtype=BF16), array(2, tok_rows, cols, dtype=BF16)],
        [],
        [],
        2,
        "own_projections",
    )
    here2b, here1b, own_kv = lax.optimization_barrier((here2b, here1b, own_kv))
    here3b = from_slot(here2b, 1)
    there1b, there2b = other_half(here1b), other_half(here2b)
    piece_kv = array(2, piece, cols, dtype=BF16)

    def piece_projections(here, there):
        return whole_call(
            pieces_kernel,
            [side],
            [w_kv, here, there],
            [],
            [piece_kv],
            [],
            [],
            1,
            "piece_projections",
        )[0]

    kv2a = piece_projections(here2a, there2a)
    kv3a = from_slot(kv2a, 1)
    kv1a = piece_projections(here1a, there1a)
    there3b = other_half(here3b)

    sizes = dict(pair_count=pair_count, head_count=head_count)
    state = [array(tok_rows, cols)] * 3
    srows = 8 * head_count
    summary_state = [array(srows, cols), array(srows, LANES)]
    *state, kv, sacc, sml, squery = whole_call(
        early_kernel,
        [early_off, early_pos, bounds, base, mine],
        [queries, sbias, own_kv, kv1a, kv2a],
        [],
        state
        + [array(2, early_rows, cols, dtype=BF16)]
        + summary_state
        + [array(srows, cols, dtype=BF16)],
        [],
        [
            pltpu.VMEM((BLOCK, items * BLOCK), F32),
            pltpu.VMEM((head_count // PAIR, PAIR * BLOCK, items * BLOCK), F32),
            pltpu.SemaphoreType.DMA((3,)),
        ],
        7,
        "early_attention",
        items=items,
        **sizes,
    )
    *state, sacc, sml, w_out_near = whole_call(
        middle_kernel,
        [*middle_list, bounds, base, side],
        [queries, w_kv, sbias, *state, sacc, sml, squery, here1b, there1b, here2b, there2b],
        [w_out],
        [array(tok_rows, cols)] * 3 + summary_state + [array(*w_out.shape, dtype=BF16)],
        [],
        [pltpu.VMEM((2, 2 * piece, cols), BF16), pltpu.SemaphoreType.DMA],
        5,
        "middle_attention",
        aliases={len(middle_list) + 3 + 3 + i: i for i in range(3)},
        items=middle_items,
        group=4,
        first_key=early_rows,
        **sizes,
    )
    own_term, other_term, *state = whole_call(
        late_kernel,
        [*late_list, bounds, base, mine, side],
        [queries, w_kv, w_out_near, sbias, *state, sacc, sml, squery, kv3a, here3b, there3b],
        [],
        [array(tok_rows, half, dtype=BF16)] * 2 + [array(tok_rows, cols)] * 3,
        [],
        [pltpu.VMEM((2, late_rows, cols), BF16)],
        4,
        "late_attention",
        aliases={len(late_list) + 4 + 4 + i: 2 + i for i in range(3)},
        items=late_items,
        group=4,
        **sizes,
    )

    received = other_half(other_term)
    hidden = own_tokens.astype(F32) + (own_term.astype(F32) + received.astype(F32))
    sums = jnp.stack([jnp.sum(hidden, axis=1), jnp.sum(hidden * hidden, axis=1)])
    sums = sums + other_half(sums)
    row_mean = sums[0] / full_width
    row_var = sums[1] / full_width - row_mean * row_mean
    normed = (hidden - row_mean[:, None]) * lax.rsqrt(row_var + 1e-05)[:, None] * ln_gain + ln_bias
    return normed.astype(BF16)[None]


def shards(*arrays):
    tokens, w_qkv, random_blocks = arrays[0], arrays[1], arrays[5]
    ctx_count = lax.axis_size("ctx")
    picked = random_blocks.shape[1] * random_blocks.shape[2]
    if (
        lax.axis_size("heads") == 2
        and ctx_count == 4
        and picked >= ctx_count
        and tokens.shape[1] % (2 * BLOCK) == 0
        and w_qkv.shape[2] % LANES == 0
        and arrays[6].shape[1] // ctx_count <= 8
    ):
        return gathered(*arrays)
    return requested(*arrays)


def solution(mesh):
    in_specs = (
        P(("groups", "dp"), "ctx", "heads"),
        P(None, None, "heads"),
        P("heads", None),
        P("heads"),
        P("heads"),
        P(("groups", "dp"), "ctx", None),
        P(("groups", "dp"), None),
        P(("groups", "dp"), None, None),
        P(("groups", "dp"), None),
    )
    out_specs = P(("groups", "dp"), "ctx", "heads")
    return jax.shard_map(shards, mesh=mesh, in_specs=in_specs, out_specs=out_specs, check_vma=False)
```

```python
import functools
import jax
import jax.numpy as jnp
from jax import lax
from jax.experimental import pallas as pl
from jax.experimental.pallas import tpu as pltpu
from jax.sharding import PartitionSpec as P

HEAD = 64
BLOCK = 128


MASKED = -1e30


def extended(x, sides, width):
    for axis, dim in sides:
        size, length = (lax.axis_size(axis), x.shape[dim])
        up = [(i, (i + 1) % size) for i in range(size - 1)]
        down = [(j, i) for i, j in up]
        last = lax.slice_in_dim(x, length - width, length, axis=dim)
        first = lax.slice_in_dim(x, 0, width, axis=dim)
        before = lax.ppermute(last, axis, up)
        after = lax.ppermute(first, axis, down)
        x = jnp.concatenate([before, x, after], axis=dim)
    return x


def segment_ids(positions, bounds):
    return jnp.sum((positions[..., None] >= bounds).astype(jnp.int32), axis=-1)


def attend(queries, keys, values, allowed, head_count):
    group_count, query_len, all_width = queries.shape
    key_len = keys.shape[1]
    query_heads = queries.reshape(group_count, query_len, head_count, HEAD)
    key_heads = keys.reshape(group_count, key_len, head_count, HEAD)
    value_heads = values.reshape(group_count, key_len, head_count, HEAD)
    scores = jnp.einsum(
        "gqhe,gkhe->ghqk", query_heads, key_heads, preferred_element_type=jnp.float32
    ) * HEAD ** (-0.5)
    scores = jnp.where(allowed[:, None], scores, MASKED)
    maxima = jnp.max(scores, axis=-1, keepdims=True)
    weights = jnp.where(allowed[:, None], jnp.exp(scores - maxima), 0.0)
    totals = jnp.sum(weights, axis=-1)
    mixture = jnp.einsum(
        "ghqk,gkhe->gqhe",
        weights.astype(jnp.bfloat16),
        value_heads,
        preferred_element_type=jnp.float32,
    )
    mixture = mixture / jnp.transpose(totals, (0, 2, 1))[..., None]
    return mixture.reshape(group_count, query_len, all_width).astype(jnp.bfloat16)


def three_views(window_span, group_size, axis_pos):
    views = []
    for shift_index in range(3):
        piece = lax.slice_in_dim(
            window_span,
            shift_index * BLOCK,
            shift_index * BLOCK + group_size * BLOCK,
            axis=axis_pos,
        )
        new_shape = (
            window_span.shape[:axis_pos] + (group_size, BLOCK) + window_span.shape[axis_pos + 1 :]
        )
        views.append(piece.reshape(new_shape))
    return jnp.concatenate(views, axis=axis_pos + 1)


def requested(
    tokens, w_qkv, w_out, ln_gain, ln_bias, random_blocks, summary_pos, summary_blocks, pair_lengths
):
    tok_rows = tokens.shape[1]
    head_cols = tokens.shape[2]
    heads_here = head_cols // HEAD
    full_width = w_out.shape[1]
    ctx_count = lax.axis_size("ctx")
    ctx_index = lax.axis_index("ctx")
    block_count = tok_rows // BLOCK
    seq_total = tok_rows * ctx_count
    bounds = jnp.cumsum(pair_lengths[0])
    own_tokens = tokens[0]
    projected = jnp.einsum(
        "nc,kcd->knd",
        lax.all_gather(own_tokens, "heads", axis=1, tiled=True),
        w_qkv,
        preferred_element_type=jnp.float32,
    ).astype(jnp.bfloat16)
    queries = projected[0]
    own_kv = projected[1:3]
    rim_kv = extended(own_kv, (("ctx", 1),), BLOCK)
    query_pos = ctx_index * tok_rows + jnp.arange(tok_rows, dtype=jnp.int32)
    own_seg = segment_ids(query_pos, bounds)
    rim_pos = ctx_index * tok_rows - BLOCK + jnp.arange(tok_rows + 2 * BLOCK, dtype=jnp.int32)
    rim_ok = (rim_pos >= 0) & (rim_pos < seq_total)
    rim_seg = segment_ids(rim_pos, bounds)
    rand_count = random_blocks.shape[2]
    picked = random_blocks[0].reshape(-1)
    pick_count = picked.shape[0]
    capacity = max(2, -(-pick_count // ctx_count))
    owners = picked // block_count
    within = picked % block_count
    slot_order = jnp.arange(pick_count, dtype=jnp.int32)
    earlier = (owners[:, None] == owners[None, :]) & (slot_order[None, :] < slot_order[:, None])
    pick_rank = jnp.sum(earlier.astype(jnp.int32), axis=1)
    pick_slot = owners * capacity + pick_rank
    slot_table = (
        pick_slot[:, None] == jnp.arange(ctx_count * capacity, dtype=jnp.int32)[None, :]
    ).astype(jnp.int32)
    requests = jnp.sum(slot_table * within[:, None], axis=0).reshape(ctx_count, capacity)
    own_blocks = own_kv.reshape(2, block_count, BLOCK, head_cols).transpose(1, 0, 2, 3)
    reply = jnp.take(
        own_blocks, lax.all_to_all(requests, "ctx", split_axis=0, concat_axis=0, tiled=True), axis=0
    )
    fetched = lax.all_to_all(reply, "ctx", split_axis=0, concat_axis=0, tiled=True)
    flat_blocks = fetched.reshape(ctx_count * capacity, 2, BLOCK, head_cols)
    far_kv = jnp.take(flat_blocks, pick_slot, axis=0).reshape(
        block_count, rand_count, 2, BLOCK, head_cols
    )
    far_kv = far_kv.transpose(2, 0, 1, 3, 4).reshape(2, block_count, rand_count * BLOCK, head_cols)
    far_pos = (
        picked.reshape(block_count, rand_count)[:, :, None] * BLOCK
        + jnp.arange(BLOCK, dtype=jnp.int32)
    ).reshape(block_count, rand_count * BLOCK)
    far_seg = segment_ids(far_pos, bounds)
    group_size = min(4, block_count)
    group_steps = block_count // group_size

    def window_step(unused, step_index):
        near_kv = three_views(rim_kv, group_size, 1)
        near_ok = three_views(rim_ok, group_size, 0)
        near_seg = three_views(rim_seg, group_size, 0)
        key_set = jnp.concatenate([near_kv, far_kv], axis=2)
        key_seg = jnp.concatenate([near_seg, far_seg], axis=1)
        key_ok = jnp.concatenate([near_ok, jnp.ones(far_seg.shape, jnp.bool_)], axis=1)
        query_seg = own_seg.reshape(group_size, BLOCK)
        allowed = key_ok[:, None, :] & (key_seg[:, None, :] == query_seg[:, :, None])
        query_group = queries.reshape(group_size, BLOCK, head_cols)
        return (unused, attend(query_group, key_set[0], key_set[1], allowed, heads_here))

    _, window_out = lax.scan(window_step, 0, jnp.arange(group_steps, dtype=jnp.int32))
    attention = window_out.reshape(tok_rows, head_cols)
    summary_rows = summary_pos[0]
    summary_lists = summary_blocks[0]
    summaries = summary_rows.shape[0]
    per_device = summaries // ctx_count
    mine = (
        lax.dynamic_slice_in_dim(summary_rows, ctx_index * per_device, per_device, 0)
        - ctx_index * tok_rows
    )
    summary_query = jnp.take(queries, mine, axis=0)
    all_queries = lax.all_gather(summary_query, "ctx", axis=0, tiled=True)
    summary_seg = segment_ids(summary_rows, bounds)
    key_block = ctx_index * block_count + jnp.arange(block_count, dtype=jnp.int32)
    listed = jnp.any(summary_lists[:, :, None] == key_block[None, None, :], axis=1)
    key_heads = own_kv[0].reshape(tok_rows, heads_here, HEAD)
    value_heads = own_kv[1].reshape(tok_rows, heads_here, HEAD)
    summary_group = min(128, summaries)
    group_total = summaries // summary_group

    def group_scores():
        query_part = all_queries.reshape(summary_group, heads_here, HEAD)
        allowed = jnp.broadcast_to(listed[:, :, None], (summary_group, block_count, BLOCK)).reshape(
            summary_group, tok_rows
        )
        allowed = allowed & (own_seg[None, :] == summary_seg[:, None])
        scores = jnp.einsum(
            "qhe,khe->hqk", query_part, key_heads, preferred_element_type=jnp.float32
        ) * HEAD ** (-0.5)
        return (jnp.where(allowed[None], scores, MASKED), allowed)

    def weigh(scores, allowed, maxima):
        weights = jnp.where(allowed[None], jnp.exp(scores - maxima[:, :, None]), 0.0)
        totals = jnp.sum(weights, axis=-1)
        mixture = jnp.einsum(
            "hqk,khe->qhe",
            weights.astype(jnp.bfloat16),
            value_heads,
            preferred_element_type=jnp.float32,
        )
        return (totals.T, mixture.reshape(summary_group, head_cols))

    def max_step(unused, group_index):
        scores, allowed = group_scores()
        return (unused, jnp.max(scores, axis=-1).T)

    _, maxima_all = lax.scan(max_step, 0, jnp.arange(group_total, dtype=jnp.int32))
    maxima_all = lax.pmax(maxima_all.reshape(summaries, heads_here), "ctx")

    def sum_step(unused, group_index):
        scores, allowed = group_scores()
        maxima = maxima_all.T
        return (unused, weigh(scores, allowed, maxima))

    _, (totals_all, mixture_all) = lax.scan(sum_step, 0, jnp.arange(group_total, dtype=jnp.int32))
    totals_all = totals_all.reshape(summaries, heads_here)
    mixture_all = mixture_all.reshape(summaries, head_cols)
    totals_all, mixture_all = (
        lax.psum(totals_all.astype(jnp.bfloat16), "ctx").astype(jnp.float32),
        lax.psum(mixture_all.astype(jnp.bfloat16), "ctx").astype(jnp.float32),
    )
    own_totals = lax.dynamic_slice_in_dim(totals_all, ctx_index * per_device, per_device, 0)
    own_mixture = lax.dynamic_slice_in_dim(mixture_all, ctx_index * per_device, per_device, 0)
    summary_out = (own_mixture / jnp.repeat(own_totals, HEAD, axis=1)).astype(jnp.bfloat16)
    attention = attention.at[mine].set(summary_out)
    partial_value = jnp.dot(attention, w_out, preferred_element_type=jnp.float32)
    summed = lax.psum_scatter(
        partial_value.astype(jnp.bfloat16), "heads", scatter_dimension=1, tiled=True
    ).astype(jnp.float32)
    hidden = own_tokens.astype(jnp.float32) + summed
    row_sums = lax.psum((jnp.sum(hidden, axis=1), jnp.sum(hidden * hidden, axis=1)), "heads")
    row_mean = row_sums[0] / full_width
    row_var = row_sums[1] / full_width - row_mean * row_mean
    normed = (hidden - row_mean[:, None]) * lax.rsqrt(row_var + 1e-05)[:, None] * ln_gain + ln_bias
    return normed.astype(jnp.bfloat16)[None]


LANES = 128
PAIR = LANES // HEAD
VMEM_LIMIT = 14 * 1024 * 1024
F32 = jnp.float32
BF16 = jnp.bfloat16
NT = (((1,), (1,)), ((), ()))


def whole_block(shape):
    return pl.BlockSpec(shape, lambda *_: (0,) * len(shape))


def params(*semantics):
    return pltpu.CompilerParams(
        dimension_semantics=semantics or None, vmem_limit_bytes=VMEM_LIMIT
    )


def project_rows(side_ref, here_ref, there_ref, w_ref):
    half = here_ref.shape[1]
    low = pl.multiple_of(side_ref[0] * half, half)
    high = pl.multiple_of((1 - side_ref[0]) * half, half)
    product = jnp.dot(here_ref[...], w_ref[pl.ds(low, half), :], preferred_element_type=F32)
    product += jnp.dot(there_ref[...], w_ref[pl.ds(high, half), :], preferred_element_type=F32)
    return product.astype(BF16)


def pair_up(refs):
    return list(zip(refs[0::2], refs[1::2]))


def weights_kernel(w_hbm, unused_hbm, other_hbm, w_q_ref, w_kv_ref, mark_ref, sem):
    mark_ref[...] = jnp.zeros(mark_ref.shape, F32)
    copies = [
        pltpu.make_async_copy(w_hbm.at[0], w_q_ref, sem.at[0]),
        pltpu.make_async_copy(w_hbm.at[pl.ds(1, 2)], w_kv_ref, sem.at[1]),
    ]
    for copy in copies:
        copy.start()
    for copy in copies:
        copy.wait()


def first_kernel(side_ref, here_ref, there_ref, w_q_ref, w_kv_ref, mark_ref, q_ref, kv_ref):
    q_ref[...] = project_rows(side_ref, here_ref, there_ref, w_q_ref)
    for j in range(2):
        kv_ref[j] = project_rows(side_ref, here_ref, there_ref, w_kv_ref.at[j])


def pieces_kernel(side_ref, w_kv_ref, *refs):
    count = len(refs) // 3
    for piece, kv_ref in zip(pair_up(refs[: 2 * count]), refs[2 * count :]):
        project_pieces(side_ref, [piece], w_kv_ref, kv_ref, 0)


def segments_of(position, bounds_ref, pair_count):
    segment = jnp.zeros(position.shape, jnp.int32)
    for pair in range(pair_count):
        segment += (position >= bounds_ref[pair]).astype(jnp.int32)
    return segment


def item_bias(query_seg, key_pos, bounds_ref, pair_count):
    lane = lax.broadcasted_iota(jnp.int32, (1, BLOCK), 1)
    key_seg = segments_of(key_pos + lane, bounds_ref, pair_count)
    key_seg = jnp.where(key_pos >= 0, key_seg, -1)
    return jnp.where(query_seg == key_seg, 0.0, MASKED)


def split_heads(pair_queries):
    lane = lax.broadcasted_iota(jnp.int32, pair_queries.shape, 1)
    scaled = pair_queries.astype(F32) * HEAD ** (-0.5)
    low = jnp.where(lane < HEAD, scaled, 0.0)
    high = jnp.where(lane >= HEAD, scaled, 0.0)
    return jnp.concatenate([low, high], axis=0).astype(BF16)


def join_heads(stacked):
    rows = stacked.shape[0] // PAIR
    lane = lax.broadcasted_iota(jnp.int32, (rows, LANES), 1)
    return jnp.where(lane < HEAD, stacked[:rows], stacked[rows:])


def spread_pair(low, high):
    lane = lax.broadcasted_iota(jnp.int32, (low.shape[0], LANES), 1)
    return jnp.where(lane < HEAD, low, high)


def summary_queries(rows_ref, q_ref, head_count):
    tok_rows, cols = q_ref.shape
    row = lax.broadcasted_iota(jnp.int32, (8, tok_rows), 0)
    col = lax.broadcasted_iota(jnp.int32, (8, tok_rows), 1)
    chosen = jnp.zeros((8, tok_rows), F32)
    for u in range(rows_ref.shape[0]):
        chosen = jnp.where((row == u) & (col == rows_ref[u]), 1.0, chosen)
    picked = jnp.dot(chosen.astype(BF16), q_ref[...], preferred_element_type=F32)
    picked = picked * HEAD ** (-0.5)
    lane = lax.broadcasted_iota(jnp.int32, (8, cols), 1)
    parts = [
        jnp.where((lane >= h * HEAD) & (lane < (h + 1) * HEAD), picked, 0.0)
        for h in range(head_count)
    ]
    return jnp.concatenate(parts, axis=0).astype(BF16)


def attend_blocks(
    first_block, block_total, off_ref, pos_ref, bounds_ref, base_ref, q_ref, kv_ref,
    acc_ref, top_ref, sum_ref, bias_ref, score_ref, items, pair_count, head_count,
):
    row = lax.broadcasted_iota(jnp.int32, (BLOCK, 1), 0)

    def block_step(step, carry):
        place = pl.ds(pl.multiple_of(step * BLOCK, BLOCK), BLOCK)
        first = pl.multiple_of((first_block + step) * BLOCK, BLOCK)
        query_seg = segments_of(base_ref[0] + first + row, bounds_ref, pair_count)
        offsets = []
        for item in range(items):
            at = (first_block + step) * items + item
            offsets.append(pl.multiple_of(off_ref[at], BLOCK))
            bias_ref[:, item * BLOCK : (item + 1) * BLOCK] = item_bias(
                query_seg, pos_ref[at], bounds_ref, pair_count
            )
        tops = []
        for pair in range(head_count // PAIR):
            cols = slice(pair * LANES, (pair + 1) * LANES)
            keys = jnp.concatenate([kv_ref[0, pl.ds(o, BLOCK), cols] for o in offsets], axis=0)
            scores = lax.dot_general(
                split_heads(q_ref[pl.ds(first, BLOCK), cols]), keys, NT, preferred_element_type=F32
            )
            for j in range(PAIR):
                rows = slice(j * BLOCK, (j + 1) * BLOCK)
                part = scores[rows] + bias_ref[...]
                score_ref[pair, rows] = part
                tops.append(jnp.max(part, axis=1, keepdims=True))
        for pair in range(head_count // PAIR):
            cols = slice(pair * LANES, (pair + 1) * LANES)
            values = jnp.concatenate([kv_ref[1, pl.ds(o, BLOCK), cols] for o in offsets], axis=0)
            values = jnp.concatenate([values, jnp.ones_like(values)], axis=1)
            peaks = tops[pair * PAIR : (pair + 1) * PAIR]
            weights = jnp.exp(score_ref[pair] - jnp.concatenate(peaks, axis=0)).astype(BF16)
            product = jnp.dot(weights, values, preferred_element_type=F32)
            acc_ref[place, cols] = join_heads(product[:, :LANES])
            sum_ref[place, cols] = join_heads(product[:, LANES:])
            top_ref[place, cols] = spread_pair(*peaks)
        return carry

    lax.fori_loop(0, block_total, block_step, 0)


def project_pieces(side_ref, pieces, w_ref, kv_ref, row):
    for here_ref, there_ref in pieces:
        rows = here_ref.shape[0]
        for j in range(2):
            kv_ref[j, row : row + rows] = project_rows(side_ref, here_ref, there_ref, w_ref.at[j])
        row += rows


def add_summary(queries, keys, values, bias, before, head_count):
    scores = lax.dot_general(queries, keys, NT, preferred_element_type=F32)
    scores = scores + jnp.concatenate([bias] * head_count, axis=0)
    top = jnp.max(scores, axis=1, keepdims=True)
    if before is not None:
        top = jnp.maximum(top, before[1])
    weights = jnp.exp(scores - top)
    total = jnp.sum(weights, axis=1, keepdims=True)
    mixture = jnp.dot(weights.astype(BF16), values, preferred_element_type=F32)
    if before is not None:
        fade = jnp.exp(before[1] - top)
        mixture = mixture + before[0] * fade
        total = total + before[2] * fade
    return mixture, top, total


def store_summary(state, sacc_ref, sml_ref):
    mixture, top, total = state
    sacc_ref[...] = mixture
    lane = lax.broadcasted_iota(jnp.int32, sml_ref.shape, 1)
    sml_ref[...] = jnp.where(lane == 0, top, total)


def load_summary(sacc_ref, sml_ref):
    return sacc_ref[...], sml_ref[:, 0:1], sml_ref[:, 1:2]


def early_kernel(
    off_ref, pos_ref, bounds_ref, base_ref, mine_ref, q_ref, sbias_ref, own_ref, *refs,
    items, pair_count, head_count,
):
    *held, acc_ref, top_ref, sum_ref, kv_ref, sacc_ref, sml_ref, squery_ref = refs[:-3]
    bias_ref, score_ref, sem = refs[-3:]
    copies = []
    row = 0
    for i, part in enumerate([own_ref] + held):
        rows = part.shape[1]
        copies.append(pltpu.make_async_copy(part, kv_ref.at[:, pl.ds(row, rows)], sem.at[i]))
        copies[-1].start()
        row += rows
    for copy in copies:
        copy.wait()
    attend_blocks(
        0, acc_ref.shape[0] // BLOCK, off_ref, pos_ref, bounds_ref, base_ref, q_ref, kv_ref,
        acc_ref, top_ref, sum_ref, bias_ref, score_ref, items, pair_count, head_count,
    )
    squery_ref[...] = summary_queries(mine_ref, q_ref, head_count)
    bias = sbias_ref[:, : kv_ref.shape[1]]
    state = add_summary(squery_ref[...], kv_ref[0], kv_ref[1], bias, None, head_count)
    store_summary(state, sacc_ref, sml_ref)


def item_part(q_ref, kv_ref, first, offset, bias, head_count):
    pairs = head_count // PAIR
    scores, tops = [], []
    for pair in range(pairs):
        cols = slice(pair * LANES, (pair + 1) * LANES)
        product = lax.dot_general(
            split_heads(q_ref[pl.ds(first, BLOCK), cols]),
            kv_ref[0, pl.ds(offset, BLOCK), cols],
            NT,
            preferred_element_type=F32,
        )
        product = product + jnp.concatenate([bias] * PAIR, axis=0)
        scores.append(product)
        tops.append(jnp.max(product, axis=1, keepdims=True))
    peaks, totals, mixtures = [], [], []
    for pair in range(pairs):
        cols = slice(pair * LANES, (pair + 1) * LANES)
        weights = jnp.exp(scores[pair] - tops[pair]).astype(BF16)
        values = kv_ref[1, pl.ds(offset, BLOCK), cols]
        values = jnp.concatenate([values, jnp.ones_like(values)], axis=1)
        product = jnp.dot(weights, values, preferred_element_type=F32)
        peaks.append(spread_pair(tops[pair][:BLOCK], tops[pair][BLOCK:]))
        mixtures.append(join_heads(product[:, :LANES]))
        totals.append(join_heads(product[:, LANES:]))
    return peaks, totals, mixtures


def add_items(
    tables, bounds_ref, base_ref, q_ref, kv_ref, state, items, group, pair_count, head_count
):
    valid_ref, block_ref, off_ref, pos_ref = tables
    peak_ref, total_ref, mix_ref = state
    row = lax.broadcasted_iota(jnp.int32, (BLOCK, 1), 0)

    def add_group(start):
        parts = []
        for item in range(start, min(start + group, items)):
            offset = pl.multiple_of(off_ref[item], BLOCK)
            first = pl.multiple_of(block_ref[item] * BLOCK, BLOCK)
            query_seg = segments_of(base_ref[0] + first + row, bounds_ref, pair_count)
            key_pos = jnp.where(valid_ref[item] == 1, pos_ref[item], -(2**30))
            bias = item_bias(query_seg, key_pos, bounds_ref, pair_count)
            parts.append((first, item_part(q_ref, kv_ref, first, offset, bias, head_count)))
        for first, (peaks, totals, mixtures) in parts:
            rows = pl.ds(first, BLOCK)
            for pair in range(head_count // PAIR):
                cols = slice(pair * LANES, (pair + 1) * LANES)
                before = peak_ref[rows, cols]
                top = jnp.maximum(before, peaks[pair])
                fade = jnp.exp(before - top)
                share = jnp.exp(peaks[pair] - top)
                peak_ref[rows, cols] = top
                total_ref[rows, cols] = total_ref[rows, cols] * fade + totals[pair] * share
                mix_ref[rows, cols] = mix_ref[rows, cols] * fade + mixtures[pair] * share

    for start in range(0, items, group):
        pl.when(valid_ref[start] == 1)(functools.partial(add_group, start))


def middle_kernel(
    valid_ref, block_ref, off_ref, pos_ref, bounds_ref, base_ref, side_ref,
    q_ref, w_kv_ref, sbias_ref, acc_in, top_in, sum_in, sacc_in, sml_in, squery_ref,
    here0_ref, there0_ref, here1_ref, there1_ref, w_out_hbm,
    acc_ref, top_ref, sum_ref, sacc_ref, sml_ref, w_out_ref,
    kv_ref, sem, *, items, group, pair_count, head_count, first_key,
):
    copy = pltpu.make_async_copy(w_out_hbm, w_out_ref, sem)
    copy.start()
    pieces = [(here0_ref, there0_ref), (here1_ref, there1_ref)]
    project_pieces(side_ref, pieces, w_kv_ref, kv_ref, 0)
    add_items(
        (valid_ref, block_ref, off_ref, pos_ref), bounds_ref, base_ref, q_ref, kv_ref,
        (top_ref, sum_ref, acc_ref), items, group, pair_count, head_count,
    )
    bias = sbias_ref[:, first_key : first_key + kv_ref.shape[1]]
    state = load_summary(sacc_in, sml_in)
    state = add_summary(squery_ref[...], kv_ref[0], kv_ref[1], bias, state, head_count)
    store_summary(state, sacc_ref, sml_ref)
    copy.wait()


def late_kernel(
    valid_ref, block_ref, off_ref, pos_ref, bounds_ref, base_ref, mine_ref, side_ref,
    q_ref, w_kv_ref, w_ref, sbias_ref, acc_ref, top_ref, sum_ref,
    sacc_ref, sml_ref, squery_ref, fresh_ref, here_ref, there_ref,
    own_ref, other_ref, mix_ref, peak_ref, total_ref, kv_ref,
    *, items, group, pair_count, head_count,
):
    tok_rows, cols_all = mix_ref.shape
    fresh_rows = fresh_ref.shape[1]
    kv_ref[:, :fresh_rows] = fresh_ref[...]
    project_pieces(side_ref, [(here_ref, there_ref)], w_kv_ref, kv_ref, fresh_rows)
    add_items(
        (valid_ref, block_ref, off_ref, pos_ref), bounds_ref, base_ref, q_ref, kv_ref,
        (peak_ref, total_ref, mix_ref), items, group, pair_count, head_count,
    )

    bias = sbias_ref[:, -kv_ref.shape[1] :]
    state = load_summary(sacc_ref, sml_ref)
    state = add_summary(squery_ref[...], kv_ref[0], kv_ref[1], bias, state, head_count)
    mixture = state[0] / state[2]
    slane = lax.broadcasted_iota(jnp.int32, (8, cols_all), 1)
    summary = jnp.zeros((8, cols_all), F32)
    for h in range(head_count):
        summary = jnp.where(
            (slane >= h * HEAD) & (slane < (h + 1) * HEAD), mixture[h * 8 : (h + 1) * 8], summary
        )

    all_rows = lax.broadcasted_iota(jnp.int32, (tok_rows, 1), 0)
    columns = []
    for pair in range(head_count // PAIR):
        cols = slice(pair * LANES, (pair + 1) * LANES)
        part = mix_ref[:, cols] / total_ref[:, cols]
        for u in range(mine_ref.shape[0]):
            part = jnp.where(all_rows == mine_ref[u], summary[u : u + 1, cols], part)
        columns.append(part.astype(BF16))
    attention = jnp.concatenate(columns, axis=1)
    half = w_ref.shape[1] // 2
    low = pl.multiple_of(side_ref[0] * half, half)
    high = pl.multiple_of((1 - side_ref[0]) * half, half)
    other_ref[...] = jnp.dot(
        attention, w_ref[:, pl.ds(high, half)], preferred_element_type=F32
    ).astype(BF16)
    own_ref[...] = jnp.dot(
        attention, w_ref[:, pl.ds(low, half)], preferred_element_type=F32
    ).astype(BF16)


def running_sum(values):
    order = jnp.arange(values.shape[0], dtype=jnp.int32)
    return jnp.sum(jnp.where(order[None, :] <= order[:, None], values[None, :], 0), axis=1)


def gathered(
    tokens, w_qkv, w_out, ln_gain, ln_bias, random_blocks, summary_pos, summary_blocks, pair_lengths
):
    tok_rows, half = tokens.shape[1:]
    cols = w_qkv.shape[2]
    head_count = cols // HEAD
    full_width = w_out.shape[1]
    ctx_count = lax.axis_size("ctx")
    ctx_index = lax.axis_index("ctx")
    side = lax.axis_index("heads").astype(jnp.int32).reshape(1)
    block_count = tok_rows // BLOCK
    total_blocks = block_count * ctx_count
    pair_count = pair_lengths.shape[1]
    own_tokens = tokens[0]
    piece = tok_rows // 2
    piece_blocks = block_count // 2
    arrival = jnp.array([0, 1, 2, 4, 3, 5, 6, 7], jnp.int32)
    place_of = jnp.array([0, 1, 2, 4, 3, 5, 6, 7], jnp.int32)
    early_count, late_count, piece_count = 4, 6, 2 * ctx_count
    early_rows, late_rows = early_count * piece, (piece_count - late_count) * piece

    bounds = running_sum(pair_lengths[0])
    base = (ctx_index * tok_rows).astype(jnp.int32).reshape(1)
    picks = random_blocks[0]
    rand_count = picks.shape[1]
    block_ids = ctx_index * block_count + jnp.arange(block_count, dtype=jnp.int32)
    window = block_ids[:, None] + jnp.arange(-1, 2, dtype=jnp.int32)[None, :]
    listed = jnp.concatenate([window, picks], axis=1)
    items = listed.shape[1]
    inside = (listed >= 0) & (listed < total_blocks)
    slot_of = (listed // block_count) ^ ctx_index
    within = listed % block_count
    number = slot_of * 2 + within // piece_blocks
    place = jnp.sum(
        jnp.where(number[..., None] == jnp.arange(piece_count), place_of, 0), axis=-1
    )
    row = place * piece + (within % piece_blocks) * BLOCK
    early = inside & (place < early_count)
    early_off = jnp.where(early, row, 0).reshape(-1)
    early_pos = jnp.where(early, listed * BLOCK, -(2**30)).reshape(-1)
    capacity = max(2, -(-block_count * rand_count // ctx_count))

    def item_list(first, last, count):
        held = (inside & (place >= first) & (place < last)).reshape(-1)
        rank = running_sum(held.astype(jnp.int32)) - 1
        chosen = held[None, :] & (rank[None, :] == jnp.arange(count, dtype=jnp.int32)[:, None])

        def compact(x):
            return jnp.sum(jnp.where(chosen, x.reshape(-1)[None, :], 0), axis=1).astype(jnp.int32)

        blocks = jnp.broadcast_to(jnp.arange(block_count, dtype=jnp.int32)[:, None], listed.shape)
        valid = jnp.any(chosen, axis=1).astype(jnp.int32)
        return valid, compact(blocks), compact(row - first * piece), compact(listed * BLOCK)

    middle_items, late_items = 2 * capacity + 1, capacity + 1
    middle_list = item_list(early_count, late_count, middle_items)
    late_list = item_list(late_count, piece_count, late_items)
    summaries = summary_pos.shape[1]
    per_device = summaries // ctx_count
    mine_pos = lax.dynamic_slice_in_dim(summary_pos[0], ctx_index * per_device, per_device, 0)
    mine_lists = lax.dynamic_slice_in_dim(summary_blocks[0], ctx_index * per_device, per_device, 0)
    mine = (mine_pos - ctx_index * tok_rows).astype(jnp.int32)
    piece_first = ((arrival // 2) ^ ctx_index) * block_count + (arrival % 2) * piece_blocks
    key_blocks = (piece_first[:, None] + jnp.arange(piece_blocks, dtype=jnp.int32)).reshape(-1)
    in_list = jnp.any(mine_lists[:, :, None] == key_blocks[None, None, :], axis=1)
    key_pos = (key_blocks[:, None] * BLOCK + jnp.arange(BLOCK, dtype=jnp.int32)).reshape(-1)
    seen = jnp.repeat(in_list, BLOCK, axis=1) & (
        segment_ids(key_pos, bounds)[None, :] == segment_ids(mine_pos, bounds)[:, None]
    )
    sbias = jnp.pad(jnp.where(seen, 0.0, MASKED), ((0, 8 - per_device), (0, 0)))
    tables = (early_off, early_pos, middle_list, late_list, bounds, mine, base, sbias, side)

    swap = [(0, 1), (1, 0)]

    def other_half(x):
        return lax.ppermute(x, "heads", swap)

    def from_slot(x, slot):
        return lax.ppermute(x, "ctx", [(i, i ^ slot) for i in range(ctx_count)])

    def array(*shape, dtype=F32):
        return jax.ShapeDtypeStruct(shape, dtype)

    def like(arrays):
        return [pltpu.VMEM(x.shape, x.dtype) for x in arrays]

    def whole_call(kernel, scalars, args, far_args, outs, far_outs, scratch, work, name, aliases=None, **sizes):
        far = pl.BlockSpec(memory_space=pltpu.HBM)
        near = pl.BlockSpec(memory_space=pltpu.VMEM)
        return pl.pallas_call(
            functools.partial(kernel, **sizes),
            in_specs=[pl.BlockSpec(memory_space=pltpu.SMEM)] * len(scalars)
            + [near] * len(args)
            + [far] * len(far_args),
            out_specs=[far] * len(far_outs) + [near] * len(outs),
            out_shape=far_outs + outs,
            scratch_shapes=scratch,
            input_output_aliases=aliases or {},
            compiler_params=params(),
            cost_estimate=pl.CostEstimate(
                flops=int(work * 1e9), bytes_accessed=int(work * 3.5e6), transcendentals=0
            ),
            name=name,
        )(*scalars, *args, *far_args)

    low, high = own_tokens[:piece], own_tokens[piece:]
    own_there = other_half(own_tokens)
    here2a = from_slot(low, 2)
    here1a = from_slot(low, 1)
    high, tables = lax.optimization_barrier((high, tables))
    early_off, early_pos, middle_list, late_list, bounds, mine, base, sbias, side = tables
    here2b = from_slot(high, 2)
    here1b = from_slot(high, 1)
    w_q, w_kv, mark = whole_call(
        weights_kernel,
        [],
        [],
        [w_qkv, here1a, sbias],
        [array(2 * half, cols, dtype=BF16), array(2, 2 * half, cols, dtype=BF16), array(8, LANES)],
        [],
        [pltpu.SemaphoreType.DMA((2,))],
        1,
        "near_weights",
    )
    there2a = other_half(here2a)
    here1a, own_there = lax.optimization_barrier((here1a, own_there))
    there1a = other_half(here1a)
    queries, own_kv = whole_call(
        first_kernel,
        [side],
        [own_tokens, own_there, w_q, w_kv, mark],
        [],
        [array(tok_rows, cols, dtype=BF16), array(2, tok_rows, cols, dtype=BF16)],
        [],
        [],
        2,
        "own_projections",
    )
    piece_kv = array(2, piece, cols, dtype=BF16)

    def piece_projections(here, there):
        return whole_call(
            pieces_kernel,
            [side],
            [w_kv, here, there],
            [],
            [piece_kv],
            [],
            [],
            1,
            "piece_projections",
        )[0]

    kv2a = piece_projections(here2a, there2a)
    here2b, here1b, own_kv, kv2a = lax.optimization_barrier((here2b, here1b, own_kv, kv2a))
    here3b = from_slot(here2b, 1)
    there1b, there2b = other_half(here1b), other_half(here2b)
    kv3a = from_slot(kv2a, 1)
    kv1a = piece_projections(here1a, there1a)
    there3b = other_half(here3b)

    sizes = dict(pair_count=pair_count, head_count=head_count)
    state = [array(tok_rows, cols)] * 3
    srows = 8 * head_count
    summary_state = [array(srows, cols), array(srows, LANES)]
    *state, kv, sacc, sml, squery = whole_call(
        early_kernel,
        [early_off, early_pos, bounds, base, mine],
        [queries, sbias, own_kv, kv1a, kv2a],
        [],
        state
        + [array(2, early_rows, cols, dtype=BF16)]
        + summary_state
        + [array(srows, cols, dtype=BF16)],
        [],
        [
            pltpu.VMEM((BLOCK, items * BLOCK), F32),
            pltpu.VMEM((head_count // PAIR, PAIR * BLOCK, items * BLOCK), F32),
            pltpu.SemaphoreType.DMA((3,)),
        ],
        7,
        "early_attention",
        items=items,
        **sizes,
    )
    *state, sacc, sml, w_out_near = whole_call(
        middle_kernel,
        [*middle_list, bounds, base, side],
        [queries, w_kv, sbias, *state, sacc, sml, squery, here1b, there1b, here2b, there2b],
        [w_out],
        [array(tok_rows, cols)] * 3 + summary_state + [array(*w_out.shape, dtype=BF16)],
        [],
        [pltpu.VMEM((2, 2 * piece, cols), BF16), pltpu.SemaphoreType.DMA],
        5,
        "middle_attention",
        aliases={len(middle_list) + 3 + 3 + i: i for i in range(3)},
        items=middle_items,
        group=4,
        first_key=early_rows,
        **sizes,
    )
    own_term, other_term, *state = whole_call(
        late_kernel,
        [*late_list, bounds, base, mine, side],
        [queries, w_kv, w_out_near, sbias, *state, sacc, sml, squery, kv3a, here3b, there3b],
        [],
        [array(tok_rows, half, dtype=BF16)] * 2 + [array(tok_rows, cols)] * 3,
        [],
        [pltpu.VMEM((2, late_rows, cols), BF16)],
        4,
        "late_attention",
        aliases={len(late_list) + 4 + 4 + i: 2 + i for i in range(3)},
        items=late_items,
        group=4,
        **sizes,
    )

    received = other_half(other_term)
    hidden = own_tokens.astype(F32) + (own_term.astype(F32) + received.astype(F32))
    sums = jnp.stack([jnp.sum(hidden, axis=1), jnp.sum(hidden * hidden, axis=1)])
    sums = sums + other_half(sums)
    row_mean = sums[0] / full_width
    row_var = sums[1] / full_width - row_mean * row_mean
    normed = (hidden - row_mean[:, None]) * lax.rsqrt(row_var + 1e-05)[:, None] * ln_gain + ln_bias
    return normed.astype(BF16)[None]


def shards(*arrays):
    tokens, w_qkv, random_blocks = arrays[0], arrays[1], arrays[5]
    ctx_count = lax.axis_size("ctx")
    picked = random_blocks.shape[1] * random_blocks.shape[2]
    if (
        lax.axis_size("heads") == 2
        and ctx_count == 4
        and picked >= ctx_count
        and tokens.shape[1] % (2 * BLOCK) == 0
        and w_qkv.shape[2] % LANES == 0
        and arrays[6].shape[1] // ctx_count <= 8
    ):
        return gathered(*arrays)
    return requested(*arrays)


def solution(mesh):
    in_specs = (
        P(("groups", "dp"), "ctx", "heads"),
        P(None, None, "heads"),
        P("heads", None),
        P("heads"),
        P("heads"),
        P(("groups", "dp"), "ctx", None),
        P(("groups", "dp"), None),
        P(("groups", "dp"), None, None),
        P(("groups", "dp"), None),
    )
    out_specs = P(("groups", "dp"), "ctx", "heads")
    return jax.shard_map(shards, mesh=mesh, in_specs=in_specs, out_specs=out_specs, check_vma=False)
```

```python
import functools
import jax
import jax.numpy as jnp
from jax import lax
from jax.experimental import pallas as pl
from jax.experimental.pallas import tpu as pltpu
from jax.sharding import PartitionSpec as P

HEAD = 64
BLOCK = 128


MASKED = -1e30


def extended(x, sides, width):
    for axis, dim in sides:
        size, length = (lax.axis_size(axis), x.shape[dim])
        up = [(i, (i + 1) % size) for i in range(size - 1)]
        down = [(j, i) for i, j in up]
        last = lax.slice_in_dim(x, length - width, length, axis=dim)
        first = lax.slice_in_dim(x, 0, width, axis=dim)
        before = lax.ppermute(last, axis, up)
        after = lax.ppermute(first, axis, down)
        x = jnp.concatenate([before, x, after], axis=dim)
    return x


def segment_ids(positions, bounds):
    return jnp.sum((positions[..., None] >= bounds).astype(jnp.int32), axis=-1)


def attend(queries, keys, values, allowed, head_count):
    group_count, query_len, all_width = queries.shape
    key_len = keys.shape[1]
    query_heads = queries.reshape(group_count, query_len, head_count, HEAD)
    key_heads = keys.reshape(group_count, key_len, head_count, HEAD)
    value_heads = values.reshape(group_count, key_len, head_count, HEAD)
    scores = jnp.einsum(
        "gqhe,gkhe->ghqk", query_heads, key_heads, preferred_element_type=jnp.float32
    ) * HEAD ** (-0.5)
    scores = jnp.where(allowed[:, None], scores, MASKED)
    maxima = jnp.max(scores, axis=-1, keepdims=True)
    weights = jnp.where(allowed[:, None], jnp.exp(scores - maxima), 0.0)
    totals = jnp.sum(weights, axis=-1)
    mixture = jnp.einsum(
        "ghqk,gkhe->gqhe",
        weights.astype(jnp.bfloat16),
        value_heads,
        preferred_element_type=jnp.float32,
    )
    mixture = mixture / jnp.transpose(totals, (0, 2, 1))[..., None]
    return mixture.reshape(group_count, query_len, all_width).astype(jnp.bfloat16)


def three_views(window_span, group_size, axis_pos):
    views = []
    for shift_index in range(3):
        piece = lax.slice_in_dim(
            window_span,
            shift_index * BLOCK,
            shift_index * BLOCK + group_size * BLOCK,
            axis=axis_pos,
        )
        new_shape = (
            window_span.shape[:axis_pos] + (group_size, BLOCK) + window_span.shape[axis_pos + 1 :]
        )
        views.append(piece.reshape(new_shape))
    return jnp.concatenate(views, axis=axis_pos + 1)


def requested(
    tokens, w_qkv, w_out, ln_gain, ln_bias, random_blocks, summary_pos, summary_blocks, pair_lengths
):
    tok_rows = tokens.shape[1]
    head_cols = tokens.shape[2]
    heads_here = head_cols // HEAD
    full_width = w_out.shape[1]
    ctx_count = lax.axis_size("ctx")
    ctx_index = lax.axis_index("ctx")
    block_count = tok_rows // BLOCK
    seq_total = tok_rows * ctx_count
    bounds = jnp.cumsum(pair_lengths[0])
    own_tokens = tokens[0]
    projected = jnp.einsum(
        "nc,kcd->knd",
        lax.all_gather(own_tokens, "heads", axis=1, tiled=True),
        w_qkv,
        preferred_element_type=jnp.float32,
    ).astype(jnp.bfloat16)
    queries = projected[0]
    own_kv = projected[1:3]
    rim_kv = extended(own_kv, (("ctx", 1),), BLOCK)
    query_pos = ctx_index * tok_rows + jnp.arange(tok_rows, dtype=jnp.int32)
    own_seg = segment_ids(query_pos, bounds)
    rim_pos = ctx_index * tok_rows - BLOCK + jnp.arange(tok_rows + 2 * BLOCK, dtype=jnp.int32)
    rim_ok = (rim_pos >= 0) & (rim_pos < seq_total)
    rim_seg = segment_ids(rim_pos, bounds)
    rand_count = random_blocks.shape[2]
    picked = random_blocks[0].reshape(-1)
    pick_count = picked.shape[0]
    capacity = max(2, -(-pick_count // ctx_count))
    owners = picked // block_count
    within = picked % block_count
    slot_order = jnp.arange(pick_count, dtype=jnp.int32)
    earlier = (owners[:, None] == owners[None, :]) & (slot_order[None, :] < slot_order[:, None])
    pick_rank = jnp.sum(earlier.astype(jnp.int32), axis=1)
    pick_slot = owners * capacity + pick_rank
    slot_table = (
        pick_slot[:, None] == jnp.arange(ctx_count * capacity, dtype=jnp.int32)[None, :]
    ).astype(jnp.int32)
    requests = jnp.sum(slot_table * within[:, None], axis=0).reshape(ctx_count, capacity)
    own_blocks = own_kv.reshape(2, block_count, BLOCK, head_cols).transpose(1, 0, 2, 3)
    reply = jnp.take(
        own_blocks, lax.all_to_all(requests, "ctx", split_axis=0, concat_axis=0, tiled=True), axis=0
    )
    fetched = lax.all_to_all(reply, "ctx", split_axis=0, concat_axis=0, tiled=True)
    flat_blocks = fetched.reshape(ctx_count * capacity, 2, BLOCK, head_cols)
    far_kv = jnp.take(flat_blocks, pick_slot, axis=0).reshape(
        block_count, rand_count, 2, BLOCK, head_cols
    )
    far_kv = far_kv.transpose(2, 0, 1, 3, 4).reshape(2, block_count, rand_count * BLOCK, head_cols)
    far_pos = (
        picked.reshape(block_count, rand_count)[:, :, None] * BLOCK
        + jnp.arange(BLOCK, dtype=jnp.int32)
    ).reshape(block_count, rand_count * BLOCK)
    far_seg = segment_ids(far_pos, bounds)
    group_size = min(4, block_count)
    group_steps = block_count // group_size

    def window_step(unused, step_index):
        near_kv = three_views(rim_kv, group_size, 1)
        near_ok = three_views(rim_ok, group_size, 0)
        near_seg = three_views(rim_seg, group_size, 0)
        key_set = jnp.concatenate([near_kv, far_kv], axis=2)
        key_seg = jnp.concatenate([near_seg, far_seg], axis=1)
        key_ok = jnp.concatenate([near_ok, jnp.ones(far_seg.shape, jnp.bool_)], axis=1)
        query_seg = own_seg.reshape(group_size, BLOCK)
        allowed = key_ok[:, None, :] & (key_seg[:, None, :] == query_seg[:, :, None])
        query_group = queries.reshape(group_size, BLOCK, head_cols)
        return (unused, attend(query_group, key_set[0], key_set[1], allowed, heads_here))

    _, window_out = lax.scan(window_step, 0, jnp.arange(group_steps, dtype=jnp.int32))
    attention = window_out.reshape(tok_rows, head_cols)
    summary_rows = summary_pos[0]
    summary_lists = summary_blocks[0]
    summaries = summary_rows.shape[0]
    per_device = summaries // ctx_count
    mine = (
        lax.dynamic_slice_in_dim(summary_rows, ctx_index * per_device, per_device, 0)
        - ctx_index * tok_rows
    )
    summary_query = jnp.take(queries, mine, axis=0)
    all_queries = lax.all_gather(summary_query, "ctx", axis=0, tiled=True)
    summary_seg = segment_ids(summary_rows, bounds)
    key_block = ctx_index * block_count + jnp.arange(block_count, dtype=jnp.int32)
    listed = jnp.any(summary_lists[:, :, None] == key_block[None, None, :], axis=1)
    key_heads = own_kv[0].reshape(tok_rows, heads_here, HEAD)
    value_heads = own_kv[1].reshape(tok_rows, heads_here, HEAD)
    summary_group = min(128, summaries)
    group_total = summaries // summary_group

    def group_scores():
        query_part = all_queries.reshape(summary_group, heads_here, HEAD)
        allowed = jnp.broadcast_to(listed[:, :, None], (summary_group, block_count, BLOCK)).reshape(
            summary_group, tok_rows
        )
        allowed = allowed & (own_seg[None, :] == summary_seg[:, None])
        scores = jnp.einsum(
            "qhe,khe->hqk", query_part, key_heads, preferred_element_type=jnp.float32
        ) * HEAD ** (-0.5)
        return (jnp.where(allowed[None], scores, MASKED), allowed)

    def weigh(scores, allowed, maxima):
        weights = jnp.where(allowed[None], jnp.exp(scores - maxima[:, :, None]), 0.0)
        totals = jnp.sum(weights, axis=-1)
        mixture = jnp.einsum(
            "hqk,khe->qhe",
            weights.astype(jnp.bfloat16),
            value_heads,
            preferred_element_type=jnp.float32,
        )
        return (totals.T, mixture.reshape(summary_group, head_cols))

    def max_step(unused, group_index):
        scores, allowed = group_scores()
        return (unused, jnp.max(scores, axis=-1).T)

    _, maxima_all = lax.scan(max_step, 0, jnp.arange(group_total, dtype=jnp.int32))
    maxima_all = lax.pmax(maxima_all.reshape(summaries, heads_here), "ctx")

    def sum_step(unused, group_index):
        scores, allowed = group_scores()
        maxima = maxima_all.T
        return (unused, weigh(scores, allowed, maxima))

    _, (totals_all, mixture_all) = lax.scan(sum_step, 0, jnp.arange(group_total, dtype=jnp.int32))
    totals_all = totals_all.reshape(summaries, heads_here)
    mixture_all = mixture_all.reshape(summaries, head_cols)
    totals_all, mixture_all = (
        lax.psum(totals_all.astype(jnp.bfloat16), "ctx").astype(jnp.float32),
        lax.psum(mixture_all.astype(jnp.bfloat16), "ctx").astype(jnp.float32),
    )
    own_totals = lax.dynamic_slice_in_dim(totals_all, ctx_index * per_device, per_device, 0)
    own_mixture = lax.dynamic_slice_in_dim(mixture_all, ctx_index * per_device, per_device, 0)
    summary_out = (own_mixture / jnp.repeat(own_totals, HEAD, axis=1)).astype(jnp.bfloat16)
    attention = attention.at[mine].set(summary_out)
    partial_value = jnp.dot(attention, w_out, preferred_element_type=jnp.float32)
    summed = lax.psum_scatter(
        partial_value.astype(jnp.bfloat16), "heads", scatter_dimension=1, tiled=True
    ).astype(jnp.float32)
    hidden = own_tokens.astype(jnp.float32) + summed
    row_sums = lax.psum((jnp.sum(hidden, axis=1), jnp.sum(hidden * hidden, axis=1)), "heads")
    row_mean = row_sums[0] / full_width
    row_var = row_sums[1] / full_width - row_mean * row_mean
    normed = (hidden - row_mean[:, None]) * lax.rsqrt(row_var + 1e-05)[:, None] * ln_gain + ln_bias
    return normed.astype(jnp.bfloat16)[None]


LANES = 128
PAIR = LANES // HEAD
VMEM_LIMIT = 14 * 1024 * 1024
F32 = jnp.float32
BF16 = jnp.bfloat16
NT = (((1,), (1,)), ((), ()))


def whole_block(shape):
    return pl.BlockSpec(shape, lambda *_: (0,) * len(shape))


def params(*semantics):
    return pltpu.CompilerParams(
        dimension_semantics=semantics or None, vmem_limit_bytes=VMEM_LIMIT
    )


def project_rows(side_ref, here_ref, there_ref, w_ref):
    half = here_ref.shape[1]
    low = pl.multiple_of(side_ref[0] * half, half)
    high = pl.multiple_of((1 - side_ref[0]) * half, half)
    product = jnp.dot(here_ref[...], w_ref[pl.ds(low, half), :], preferred_element_type=F32)
    product += jnp.dot(there_ref[...], w_ref[pl.ds(high, half), :], preferred_element_type=F32)
    return product.astype(BF16)


def pair_up(refs):
    return list(zip(refs[0::2], refs[1::2]))


def weights_kernel(w_hbm, unused_hbm, other_hbm, w_q_ref, w_kv_ref, mark_ref, sem):
    mark_ref[...] = jnp.zeros(mark_ref.shape, F32)
    copies = [
        pltpu.make_async_copy(w_hbm.at[0], w_q_ref, sem.at[0]),
        pltpu.make_async_copy(w_hbm.at[pl.ds(1, 2)], w_kv_ref, sem.at[1]),
    ]
    for copy in copies:
        copy.start()
    for copy in copies:
        copy.wait()


def first_kernel(side_ref, here_ref, there_ref, w_q_ref, w_kv_ref, mark_ref, q_ref, kv_ref):
    q_ref[...] = project_rows(side_ref, here_ref, there_ref, w_q_ref)
    for j in range(2):
        kv_ref[j] = project_rows(side_ref, here_ref, there_ref, w_kv_ref.at[j])


def pieces_kernel(side_ref, w_kv_ref, *refs):
    count = len(refs) // 3
    for piece, kv_ref in zip(pair_up(refs[: 2 * count]), refs[2 * count :]):
        project_pieces(side_ref, [piece], w_kv_ref, kv_ref, 0)


def segments_of(position, bounds_ref, pair_count):
    segment = jnp.zeros(position.shape, jnp.int32)
    for pair in range(pair_count):
        segment += (position >= bounds_ref[pair]).astype(jnp.int32)
    return segment


def item_bias(query_seg, key_pos, bounds_ref, pair_count):
    lane = lax.broadcasted_iota(jnp.int32, (1, BLOCK), 1)
    key_seg = segments_of(key_pos + lane, bounds_ref, pair_count)
    key_seg = jnp.where(key_pos >= 0, key_seg, -1)
    return jnp.where(query_seg == key_seg, 0.0, MASKED)


def split_heads(pair_queries):
    lane = lax.broadcasted_iota(jnp.int32, pair_queries.shape, 1)
    scaled = pair_queries.astype(F32) * HEAD ** (-0.5)
    low = jnp.where(lane < HEAD, scaled, 0.0)
    high = jnp.where(lane >= HEAD, scaled, 0.0)
    return jnp.concatenate([low, high], axis=0).astype(BF16)


def join_heads(stacked):
    rows = stacked.shape[0] // PAIR
    lane = lax.broadcasted_iota(jnp.int32, (rows, LANES), 1)
    return jnp.where(lane < HEAD, stacked[:rows], stacked[rows:])


def spread_pair(low, high):
    lane = lax.broadcasted_iota(jnp.int32, (low.shape[0], LANES), 1)
    return jnp.where(lane < HEAD, low, high)


def summary_queries(rows_ref, q_ref, head_count):
    tok_rows, cols = q_ref.shape
    row = lax.broadcasted_iota(jnp.int32, (8, tok_rows), 0)
    col = lax.broadcasted_iota(jnp.int32, (8, tok_rows), 1)
    chosen = jnp.zeros((8, tok_rows), F32)
    for u in range(rows_ref.shape[0]):
        chosen = jnp.where((row == u) & (col == rows_ref[u]), 1.0, chosen)
    picked = jnp.dot(chosen.astype(BF16), q_ref[...], preferred_element_type=F32)
    picked = picked * HEAD ** (-0.5)
    lane = lax.broadcasted_iota(jnp.int32, (8, cols), 1)
    parts = [
        jnp.where((lane >= h * HEAD) & (lane < (h + 1) * HEAD), picked, 0.0)
        for h in range(head_count)
    ]
    return jnp.concatenate(parts, axis=0).astype(BF16)


def attend_blocks(
    first_block, block_total, off_ref, pos_ref, bounds_ref, base_ref, q_ref, kv_ref,
    acc_ref, top_ref, sum_ref, bias_ref, score_ref, items, pair_count, head_count,
):
    row = lax.broadcasted_iota(jnp.int32, (BLOCK, 1), 0)

    def block_step(step, carry):
        place = pl.ds(pl.multiple_of(step * BLOCK, BLOCK), BLOCK)
        first = pl.multiple_of((first_block + step) * BLOCK, BLOCK)
        query_seg = segments_of(base_ref[0] + first + row, bounds_ref, pair_count)
        offsets = []
        for item in range(items):
            at = (first_block + step) * items + item
            offsets.append(pl.multiple_of(off_ref[at], BLOCK))
            bias_ref[:, item * BLOCK : (item + 1) * BLOCK] = item_bias(
                query_seg, pos_ref[at], bounds_ref, pair_count
            )
        tops = []
        for pair in range(head_count // PAIR):
            cols = slice(pair * LANES, (pair + 1) * LANES)
            keys = jnp.concatenate([kv_ref[0, pl.ds(o, BLOCK), cols] for o in offsets], axis=0)
            scores = lax.dot_general(
                split_heads(q_ref[pl.ds(first, BLOCK), cols]), keys, NT, preferred_element_type=F32
            )
            for j in range(PAIR):
                rows = slice(j * BLOCK, (j + 1) * BLOCK)
                part = scores[rows] + bias_ref[...]
                score_ref[pair, rows] = part
                tops.append(jnp.max(part, axis=1, keepdims=True))
        for pair in range(head_count // PAIR):
            cols = slice(pair * LANES, (pair + 1) * LANES)
            values = jnp.concatenate([kv_ref[1, pl.ds(o, BLOCK), cols] for o in offsets], axis=0)
            values = jnp.concatenate([values, jnp.ones_like(values)], axis=1)
            peaks = tops[pair * PAIR : (pair + 1) * PAIR]
            weights = jnp.exp(score_ref[pair] - jnp.concatenate(peaks, axis=0)).astype(BF16)
            product = jnp.dot(weights, values, preferred_element_type=F32)
            acc_ref[place, cols] = join_heads(product[:, :LANES])
            sum_ref[place, cols] = join_heads(product[:, LANES:])
            top_ref[place, cols] = spread_pair(*peaks)
        return carry

    lax.fori_loop(0, block_total, block_step, 0)


def project_pieces(side_ref, pieces, w_ref, kv_ref, row):
    for here_ref, there_ref in pieces:
        rows = here_ref.shape[0]
        for j in range(2):
            kv_ref[j, row : row + rows] = project_rows(side_ref, here_ref, there_ref, w_ref.at[j])
        row += rows


def add_summary(queries, keys, values, bias, before, head_count):
    scores = lax.dot_general(queries, keys, NT, preferred_element_type=F32)
    scores = scores + jnp.concatenate([bias] * head_count, axis=0)
    top = jnp.max(scores, axis=1, keepdims=True)
    if before is not None:
        top = jnp.maximum(top, before[1])
    weights = jnp.exp(scores - top)
    total = jnp.sum(weights, axis=1, keepdims=True)
    mixture = jnp.dot(weights.astype(BF16), values, preferred_element_type=F32)
    if before is not None:
        fade = jnp.exp(before[1] - top)
        mixture = mixture + before[0] * fade
        total = total + before[2] * fade
    return mixture, top, total


def store_summary(state, sacc_ref, sml_ref):
    mixture, top, total = state
    sacc_ref[...] = mixture
    lane = lax.broadcasted_iota(jnp.int32, sml_ref.shape, 1)
    sml_ref[...] = jnp.where(lane == 0, top, total)


def load_summary(sacc_ref, sml_ref):
    return sacc_ref[...], sml_ref[:, 0:1], sml_ref[:, 1:2]


def early_kernel(
    off_ref, pos_ref, bounds_ref, base_ref, q_ref, own_ref, *refs,
    items, pair_count, head_count,
):
    *held, acc_ref, top_ref, sum_ref, kv_ref = refs[:-3]
    bias_ref, score_ref, sem = refs[-3:]
    copies = []
    row = 0
    for i, part in enumerate([own_ref] + held):
        rows = part.shape[1]
        copies.append(pltpu.make_async_copy(part, kv_ref.at[:, pl.ds(row, rows)], sem.at[i]))
        copies[-1].start()
        row += rows
    for copy in copies:
        copy.wait()
    attend_blocks(
        0, acc_ref.shape[0] // BLOCK // 2, off_ref, pos_ref, bounds_ref, base_ref, q_ref, kv_ref,
        acc_ref, top_ref, sum_ref, bias_ref, score_ref, items, pair_count, head_count,
    )


def second_kernel(
    off_ref, pos_ref, bounds_ref, base_ref, mine_ref,
    q_ref, sbias_ref, kv_ref, acc_in, top_in, sum_in,
    acc_ref, top_ref, sum_ref, sacc_ref, sml_ref, squery_ref, bias_ref, score_ref,
    *, items, pair_count, head_count,
):
    rows = acc_ref.shape[0] // 2
    rest = pl.ds(rows, rows)
    attend_blocks(
        rows // BLOCK, rows // BLOCK, off_ref, pos_ref, bounds_ref, base_ref, q_ref, kv_ref,
        acc_ref.at[rest], top_ref.at[rest], sum_ref.at[rest], bias_ref, score_ref,
        items, pair_count, head_count,
    )
    squery_ref[...] = summary_queries(mine_ref, q_ref, head_count)
    bias = sbias_ref[:, : kv_ref.shape[1]]
    state = add_summary(squery_ref[...], kv_ref[0], kv_ref[1], bias, None, head_count)
    store_summary(state, sacc_ref, sml_ref)


def item_part(q_ref, kv_ref, first, offset, bias, head_count):
    pairs = head_count // PAIR
    scores, tops = [], []
    for pair in range(pairs):
        cols = slice(pair * LANES, (pair + 1) * LANES)
        product = lax.dot_general(
            split_heads(q_ref[pl.ds(first, BLOCK), cols]),
            kv_ref[0, pl.ds(offset, BLOCK), cols],
            NT,
            preferred_element_type=F32,
        )
        product = product + jnp.concatenate([bias] * PAIR, axis=0)
        scores.append(product)
        tops.append(jnp.max(product, axis=1, keepdims=True))
    peaks, totals, mixtures = [], [], []
    for pair in range(pairs):
        cols = slice(pair * LANES, (pair + 1) * LANES)
        weights = jnp.exp(scores[pair] - tops[pair]).astype(BF16)
        values = kv_ref[1, pl.ds(offset, BLOCK), cols]
        values = jnp.concatenate([values, jnp.ones_like(values)], axis=1)
        product = jnp.dot(weights, values, preferred_element_type=F32)
        peaks.append(spread_pair(tops[pair][:BLOCK], tops[pair][BLOCK:]))
        mixtures.append(join_heads(product[:, :LANES]))
        totals.append(join_heads(product[:, LANES:]))
    return peaks, totals, mixtures


def add_items(
    tables, bounds_ref, base_ref, q_ref, kv_ref, state, items, group, pair_count, head_count
):
    valid_ref, block_ref, off_ref, pos_ref = tables
    peak_ref, total_ref, mix_ref = state
    row = lax.broadcasted_iota(jnp.int32, (BLOCK, 1), 0)

    def add_group(start):
        parts = []
        for item in range(start, min(start + group, items)):
            offset = pl.multiple_of(off_ref[item], BLOCK)
            first = pl.multiple_of(block_ref[item] * BLOCK, BLOCK)
            query_seg = segments_of(base_ref[0] + first + row, bounds_ref, pair_count)
            key_pos = jnp.where(valid_ref[item] == 1, pos_ref[item], -(2**30))
            bias = item_bias(query_seg, key_pos, bounds_ref, pair_count)
            parts.append((first, item_part(q_ref, kv_ref, first, offset, bias, head_count)))
        for first, (peaks, totals, mixtures) in parts:
            rows = pl.ds(first, BLOCK)
            for pair in range(head_count // PAIR):
                cols = slice(pair * LANES, (pair + 1) * LANES)
                before = peak_ref[rows, cols]
                top = jnp.maximum(before, peaks[pair])
                fade = jnp.exp(before - top)
                share = jnp.exp(peaks[pair] - top)
                peak_ref[rows, cols] = top
                total_ref[rows, cols] = total_ref[rows, cols] * fade + totals[pair] * share
                mix_ref[rows, cols] = mix_ref[rows, cols] * fade + mixtures[pair] * share

    for start in range(0, items, group):
        pl.when(valid_ref[start] == 1)(functools.partial(add_group, start))


def middle_kernel(
    valid_ref, block_ref, off_ref, pos_ref, bounds_ref, base_ref, side_ref,
    q_ref, w_kv_ref, sbias_ref, acc_in, top_in, sum_in, sacc_in, sml_in, squery_ref,
    here0_ref, there0_ref, here1_ref, there1_ref, w_out_hbm,
    acc_ref, top_ref, sum_ref, sacc_ref, sml_ref, w_out_ref,
    kv_ref, sem, *, items, group, pair_count, head_count, first_key,
):
    copy = pltpu.make_async_copy(w_out_hbm, w_out_ref, sem)
    copy.start()
    pieces = [(here0_ref, there0_ref), (here1_ref, there1_ref)]
    project_pieces(side_ref, pieces, w_kv_ref, kv_ref, 0)
    add_items(
        (valid_ref, block_ref, off_ref, pos_ref), bounds_ref, base_ref, q_ref, kv_ref,
        (top_ref, sum_ref, acc_ref), items, group, pair_count, head_count,
    )
    bias = sbias_ref[:, first_key : first_key + kv_ref.shape[1]]
    state = load_summary(sacc_in, sml_in)
    state = add_summary(squery_ref[...], kv_ref[0], kv_ref[1], bias, state, head_count)
    store_summary(state, sacc_ref, sml_ref)
    copy.wait()


def late_kernel(
    valid_ref, block_ref, off_ref, pos_ref, bounds_ref, base_ref, mine_ref, side_ref,
    q_ref, w_kv_ref, w_ref, sbias_ref, acc_ref, top_ref, sum_ref,
    sacc_ref, sml_ref, squery_ref, fresh_ref, here_ref, there_ref,
    own_ref, other_ref, mix_ref, peak_ref, total_ref, kv_ref,
    *, items, group, pair_count, head_count,
):
    tok_rows, cols_all = mix_ref.shape
    fresh_rows = fresh_ref.shape[1]
    kv_ref[:, :fresh_rows] = fresh_ref[...]
    project_pieces(side_ref, [(here_ref, there_ref)], w_kv_ref, kv_ref, fresh_rows)
    add_items(
        (valid_ref, block_ref, off_ref, pos_ref), bounds_ref, base_ref, q_ref, kv_ref,
        (peak_ref, total_ref, mix_ref), items, group, pair_count, head_count,
    )

    bias = sbias_ref[:, -kv_ref.shape[1] :]
    state = load_summary(sacc_ref, sml_ref)
    state = add_summary(squery_ref[...], kv_ref[0], kv_ref[1], bias, state, head_count)
    mixture = state[0] / state[2]
    slane = lax.broadcasted_iota(jnp.int32, (8, cols_all), 1)
    summary = jnp.zeros((8, cols_all), F32)
    for h in range(head_count):
        summary = jnp.where(
            (slane >= h * HEAD) & (slane < (h + 1) * HEAD), mixture[h * 8 : (h + 1) * 8], summary
        )

    all_rows = lax.broadcasted_iota(jnp.int32, (tok_rows, 1), 0)
    columns = []
    for pair in range(head_count // PAIR):
        cols = slice(pair * LANES, (pair + 1) * LANES)
        part = mix_ref[:, cols] / total_ref[:, cols]
        for u in range(mine_ref.shape[0]):
            part = jnp.where(all_rows == mine_ref[u], summary[u : u + 1, cols], part)
        columns.append(part.astype(BF16))
    attention = jnp.concatenate(columns, axis=1)
    half = w_ref.shape[1] // 2
    low = pl.multiple_of(side_ref[0] * half, half)
    high = pl.multiple_of((1 - side_ref[0]) * half, half)
    other_ref[...] = jnp.dot(
        attention, w_ref[:, pl.ds(high, half)], preferred_element_type=F32
    ).astype(BF16)
    own_ref[...] = jnp.dot(
        attention, w_ref[:, pl.ds(low, half)], preferred_element_type=F32
    ).astype(BF16)


def running_sum(values):
    order = jnp.arange(values.shape[0], dtype=jnp.int32)
    return jnp.sum(jnp.where(order[None, :] <= order[:, None], values[None, :], 0), axis=1)


def gathered(
    tokens, w_qkv, w_out, ln_gain, ln_bias, random_blocks, summary_pos, summary_blocks, pair_lengths
):
    tok_rows, half = tokens.shape[1:]
    cols = w_qkv.shape[2]
    head_count = cols // HEAD
    full_width = w_out.shape[1]
    ctx_count = lax.axis_size("ctx")
    ctx_index = lax.axis_index("ctx")
    side = lax.axis_index("heads").astype(jnp.int32).reshape(1)
    block_count = tok_rows // BLOCK
    total_blocks = block_count * ctx_count
    pair_count = pair_lengths.shape[1]
    own_tokens = tokens[0]
    piece = tok_rows // 2
    piece_blocks = block_count // 2
    arrival = jnp.array([0, 1, 2, 4, 3, 5, 6, 7], jnp.int32)
    place_of = jnp.array([0, 1, 2, 4, 3, 5, 6, 7], jnp.int32)
    early_count, late_count, piece_count = 4, 6, 2 * ctx_count
    early_rows, late_rows = early_count * piece, (piece_count - late_count) * piece

    bounds = running_sum(pair_lengths[0])
    base = (ctx_index * tok_rows).astype(jnp.int32).reshape(1)
    picks = random_blocks[0]
    rand_count = picks.shape[1]
    block_ids = ctx_index * block_count + jnp.arange(block_count, dtype=jnp.int32)
    window = block_ids[:, None] + jnp.arange(-1, 2, dtype=jnp.int32)[None, :]
    listed = jnp.concatenate([window, picks], axis=1)
    items = listed.shape[1]
    inside = (listed >= 0) & (listed < total_blocks)
    slot_of = (listed // block_count) ^ ctx_index
    within = listed % block_count
    number = slot_of * 2 + within // piece_blocks
    place = jnp.sum(
        jnp.where(number[..., None] == jnp.arange(piece_count), place_of, 0), axis=-1
    )
    row = place * piece + (within % piece_blocks) * BLOCK
    early = inside & (place < early_count)
    early_off = jnp.where(early, row, 0).reshape(-1)
    early_pos = jnp.where(early, listed * BLOCK, -(2**30)).reshape(-1)
    capacity = max(2, -(-block_count * rand_count // ctx_count))

    def item_list(first, last, count):
        held = (inside & (place >= first) & (place < last)).reshape(-1)
        rank = running_sum(held.astype(jnp.int32)) - 1
        chosen = held[None, :] & (rank[None, :] == jnp.arange(count, dtype=jnp.int32)[:, None])

        def compact(x):
            return jnp.sum(jnp.where(chosen, x.reshape(-1)[None, :], 0), axis=1).astype(jnp.int32)

        blocks = jnp.broadcast_to(jnp.arange(block_count, dtype=jnp.int32)[:, None], listed.shape)
        valid = jnp.any(chosen, axis=1).astype(jnp.int32)
        return valid, compact(blocks), compact(row - first * piece), compact(listed * BLOCK)

    middle_items, late_items = 2 * capacity + 1, capacity + 1
    middle_list = item_list(early_count, late_count, middle_items)
    late_list = item_list(late_count, piece_count, late_items)
    summaries = summary_pos.shape[1]
    per_device = summaries // ctx_count
    mine_pos = lax.dynamic_slice_in_dim(summary_pos[0], ctx_index * per_device, per_device, 0)
    mine_lists = lax.dynamic_slice_in_dim(summary_blocks[0], ctx_index * per_device, per_device, 0)
    mine = (mine_pos - ctx_index * tok_rows).astype(jnp.int32)
    piece_first = ((arrival // 2) ^ ctx_index) * block_count + (arrival % 2) * piece_blocks
    key_blocks = (piece_first[:, None] + jnp.arange(piece_blocks, dtype=jnp.int32)).reshape(-1)
    in_list = jnp.any(mine_lists[:, :, None] == key_blocks[None, None, :], axis=1)
    key_pos = (key_blocks[:, None] * BLOCK + jnp.arange(BLOCK, dtype=jnp.int32)).reshape(-1)
    seen = jnp.repeat(in_list, BLOCK, axis=1) & (
        segment_ids(key_pos, bounds)[None, :] == segment_ids(mine_pos, bounds)[:, None]
    )
    sbias = jnp.pad(jnp.where(seen, 0.0, MASKED), ((0, 8 - per_device), (0, 0)))
    tables = (early_off, early_pos, middle_list, late_list, bounds, mine, base, sbias, side)

    swap = [(0, 1), (1, 0)]

    def other_half(x):
        return lax.ppermute(x, "heads", swap)

    def from_slot(x, slot):
        return lax.ppermute(x, "ctx", [(i, i ^ slot) for i in range(ctx_count)])

    def array(*shape, dtype=F32):
        return jax.ShapeDtypeStruct(shape, dtype)

    def like(arrays):
        return [pltpu.VMEM(x.shape, x.dtype) for x in arrays]

    def whole_call(kernel, scalars, args, far_args, outs, far_outs, scratch, work, name, aliases=None, **sizes):
        far = pl.BlockSpec(memory_space=pltpu.HBM)
        near = pl.BlockSpec(memory_space=pltpu.VMEM)
        return pl.pallas_call(
            functools.partial(kernel, **sizes),
            in_specs=[pl.BlockSpec(memory_space=pltpu.SMEM)] * len(scalars)
            + [near] * len(args)
            + [far] * len(far_args),
            out_specs=[far] * len(far_outs) + [near] * len(outs),
            out_shape=far_outs + outs,
            scratch_shapes=scratch,
            input_output_aliases=aliases or {},
            compiler_params=params(),
            cost_estimate=pl.CostEstimate(
                flops=int(work * 1e9), bytes_accessed=int(work * 3.5e6), transcendentals=0
            ),
            name=name,
        )(*scalars, *args, *far_args)

    low, high = own_tokens[:piece], own_tokens[piece:]
    own_there = other_half(own_tokens)
    here2a = from_slot(low, 2)
    here1a = from_slot(low, 1)
    high, tables = lax.optimization_barrier((high, tables))
    early_off, early_pos, middle_list, late_list, bounds, mine, base, sbias, side = tables
    here2b = from_slot(high, 2)
    here1b = from_slot(high, 1)
    w_q, w_kv, mark = whole_call(
        weights_kernel,
        [],
        [],
        [w_qkv, here1a, sbias],
        [array(2 * half, cols, dtype=BF16), array(2, 2 * half, cols, dtype=BF16), array(8, LANES)],
        [],
        [pltpu.SemaphoreType.DMA((2,))],
        1,
        "near_weights",
    )
    there2a = other_half(here2a)
    here1a, own_there = lax.optimization_barrier((here1a, own_there))
    there1a = other_half(here1a)
    queries, own_kv = whole_call(
        first_kernel,
        [side],
        [own_tokens, own_there, w_q, w_kv, mark],
        [],
        [array(tok_rows, cols, dtype=BF16), array(2, tok_rows, cols, dtype=BF16)],
        [],
        [],
        2,
        "own_projections",
    )
    piece_kv = array(2, piece, cols, dtype=BF16)

    def piece_projections(here, there):
        return whole_call(
            pieces_kernel,
            [side],
            [w_kv, here, there],
            [],
            [piece_kv],
            [],
            [],
            1,
            "piece_projections",
        )[0]

    kv2a = piece_projections(here2a, there2a)
    here2b, here1b, own_kv, kv2a = lax.optimization_barrier((here2b, here1b, own_kv, kv2a))
    here3b = from_slot(here2b, 1)
    there1b, there2b = other_half(here1b), other_half(here2b)
    kv3a = from_slot(kv2a, 1)
    kv1a = piece_projections(here1a, there1a)
    there3b = other_half(here3b)

    sizes = dict(pair_count=pair_count, head_count=head_count)
    state = [array(tok_rows, cols)] * 3
    srows = 8 * head_count
    summary_state = [array(srows, cols), array(srows, LANES)]
    score_scratch = [
        pltpu.VMEM((BLOCK, items * BLOCK), F32),
        pltpu.VMEM((head_count // PAIR, PAIR * BLOCK, items * BLOCK), F32),
    ]
    *state, kv = whole_call(
        early_kernel,
        [early_off, early_pos, bounds, base],
        [queries, own_kv, kv1a, kv2a],
        [],
        state + [array(2, early_rows, cols, dtype=BF16)],
        [],
        score_scratch + [pltpu.SemaphoreType.DMA((3,))],
        4,
        "early_attention",
        items=items,
        **sizes,
    )
    *state, sacc, sml, squery = whole_call(
        second_kernel,
        [early_off, early_pos, bounds, base, mine],
        [queries, sbias, kv, *state],
        [],
        [array(tok_rows, cols)] * 3 + summary_state + [array(srows, cols, dtype=BF16)],
        [],
        score_scratch,
        4,
        "second_attention",
        aliases={8 + i: i for i in range(3)},
        items=items,
        **sizes,
    )
    *state, sacc, sml, w_out_near = whole_call(
        middle_kernel,
        [*middle_list, bounds, base, side],
        [queries, w_kv, sbias, *state, sacc, sml, squery, here1b, there1b, here2b, there2b],
        [w_out],
        [array(tok_rows, cols)] * 3 + summary_state + [array(*w_out.shape, dtype=BF16)],
        [],
        [pltpu.VMEM((2, 2 * piece, cols), BF16), pltpu.SemaphoreType.DMA],
        5,
        "middle_attention",
        aliases={len(middle_list) + 3 + 3 + i: i for i in range(3)},
        items=middle_items,
        group=4,
        first_key=early_rows,
        **sizes,
    )
    own_term, other_term, *state = whole_call(
        late_kernel,
        [*late_list, bounds, base, mine, side],
        [queries, w_kv, w_out_near, sbias, *state, sacc, sml, squery, kv3a, here3b, there3b],
        [],
        [array(tok_rows, half, dtype=BF16)] * 2 + [array(tok_rows, cols)] * 3,
        [],
        [pltpu.VMEM((2, late_rows, cols), BF16)],
        4,
        "late_attention",
        aliases={len(late_list) + 4 + 4 + i: 2 + i for i in range(3)},
        items=late_items,
        group=4,
        **sizes,
    )

    received = other_half(other_term)
    hidden = own_tokens.astype(F32) + (own_term.astype(F32) + received.astype(F32))
    sums = jnp.stack([jnp.sum(hidden, axis=1), jnp.sum(hidden * hidden, axis=1)])
    sums = sums + other_half(sums)
    row_mean = sums[0] / full_width
    row_var = sums[1] / full_width - row_mean * row_mean
    normed = (hidden - row_mean[:, None]) * lax.rsqrt(row_var + 1e-05)[:, None] * ln_gain + ln_bias
    return normed.astype(BF16)[None]


def shards(*arrays):
    tokens, w_qkv, random_blocks = arrays[0], arrays[1], arrays[5]
    ctx_count = lax.axis_size("ctx")
    picked = random_blocks.shape[1] * random_blocks.shape[2]
    if (
        lax.axis_size("heads") == 2
        and ctx_count == 4
        and picked >= ctx_count
        and tokens.shape[1] % (2 * BLOCK) == 0
        and w_qkv.shape[2] % LANES == 0
        and arrays[6].shape[1] // ctx_count <= 8
    ):
        return gathered(*arrays)
    return requested(*arrays)


def solution(mesh):
    in_specs = (
        P(("groups", "dp"), "ctx", "heads"),
        P(None, None, "heads"),
        P("heads", None),
        P("heads"),
        P("heads"),
        P(("groups", "dp"), "ctx", None),
        P(("groups", "dp"), None),
        P(("groups", "dp"), None, None),
        P(("groups", "dp"), None),
    )
    out_specs = P(("groups", "dp"), "ctx", "heads")
    return jax.shard_map(shards, mesh=mesh, in_specs=in_specs, out_specs=out_specs, check_vma=False)
```
